32 devices in a mesh: dp: 2 (over x), row: 4 (over y, core), col: 4 (over z).
Axes of the slice: x: 2, y: 2, z: 4, core: 2. Of those that a mesh axis runs over, the one named last changes fastest.
Arguments:
- block_input: bfloat16 [2048, 768], P(('dp', 'row'), 'col'), may hold values from -6 to 6
- ln1_gain: float32 [768], P('col'), may hold values from 0.1 to 1.9
- ln1_bias: float32 [768], P('col'), may hold values from -1.75 to 1.75
- qkv_weight: bfloat16 [4, 4, 110592], P('col', 'row'), may hold values from -0.21875 to 0.21875
- qv_bias: float32 [2, 768], P(None, 'row'), may hold values from -1.75 to 1.75
- out_weight: bfloat16 [4, 4, 36864], P('row', 'col'), may hold values from -1.25 to 1.25
- out_bias: float32 [768], P('col'), may hold values from -1.75 to 1.75
- ln2_gain: float32 [768], P('col'), may hold values from 0.1 to 1.9
- ln2_bias: float32 [768], P('col'), may hold values from -1.75 to 1.75
- up_weight: bfloat16 [768, 3072], P('col', 'row'), may hold values from -0.21875 to 0.21875
- up_bias: float32 [3072], P('row'), may hold values from -3 to 3
- down_weight: bfloat16 [768, 3072], P('col', 'row'), may hold values from -0.109375 to 0.109375
- down_bias: float32 [768], P('col'), may hold values from -1.75 to 1.75
- out_grad: bfloat16 [2048, 768], P(('dp', 'row'), 'col'), may hold values from -6 to 6
Outputs:
- block_output: bfloat16 [2048, 768], P(('dp', 'row'), 'col')
- input_grad: bfloat16 [2048, 768], P(('dp', 'row'), 'col')
- ln1_gain_grad: float32 [768], P('col')
- ln1_bias_grad: float32 [768], P('col')
- qkv_weight_grad: float32 [4, 4, 110592], P('col', 'row')
- qv_bias_grad: float32 [2, 768], P(None, 'row')
- out_weight_grad: float32 [4, 4, 36864], P('row', 'col')
- out_bias_grad: float32 [768], P('col')
- ln2_gain_grad: float32 [768], P('col')
- ln2_bias_grad: float32 [768], P('col')
- up_weight_grad: float32 [768, 3072], P('col', 'row')
- up_bias_grad: float32 [3072], P('row')
- down_weight_grad: float32 [768, 3072], P('col', 'row')
- down_bias_grad: float32 [768], P('col')
The draws below stay inside these ranges and needn't reach their ends.
All inputs are finite; a program needn't handle non-finite values.
Results may differ from the reference program's by a relative error of at most 0.015.
Values may be sent and summed in bfloat16 or wider, within the bound.
No kernel may reach another device: no remote copies, remote signals or barrier semaphores. Data moves between devices by JAX's collectives and lax.ppermute only.
A program may use at most 64 MiB of HBM per device.

```python
import math
import jax
import jax.numpy as jnp
from jax import lax

D = 768
HEADS = 12
HEAD = 64
FF = 3072
SEQ = 1024
TOKENS = 2048
N_DP = 2
N_ROW = 4
N_COL = 4


def level_of(stream_key, shape, shards, low, largest):
    level = 1.0
    for position, shards_of in shards:
        draws = jax.random.uniform(jax.random.fold_in(jax.random.fold_in(stream_key, 6), position), (shards_of,), jnp.float32, low / len(shards), largest / len(shards))
        level = level * jnp.repeat(jnp.exp(draws), shape[position] // shards_of).reshape((-1,) + (1,) * (len(shape) - 1 - position))
    return level


def scatter_about(key, extent, width, reach, cuts=(), held_as=jnp.bfloat16):
    array = jax.random.normal(key, extent, jnp.float32) * width
    if len(cuts) > 0:
        array = level_of(key, extent, cuts, -0.22, 0.18) * array
    return jnp.clip(array, min=-reach, max=reach).astype(held_as)


def setup_inputs(seed: int = 0) -> dict:
    seeds = jax.random.split(jax.random.key(seed), 15)
    return {
        "block_input": scatter_about(seeds[0], (TOKENS, D), 1.0, 6.0, ((0, 8), (1, 4))),
        "ln1_gain": jnp.clip(1.0 + 0.18 * jax.random.normal(seeds[1], (D,), jnp.float32), 0.1, 1.9),
        "ln1_bias": scatter_about(seeds[2], (D,), 0.3, 1.75, ((0, 4),), jnp.float32),
        "qkv_weight": scatter_about(seeds[3], (N_COL, N_ROW, D // N_COL * 3 * (D // N_ROW)), D ** -0.5, 0.21875, ((0, 4), (1, 4))),
        "qv_bias": scatter_about(seeds[4], (2, D), 0.3, 1.75, ((1, 4),), jnp.float32),
        "out_weight": scatter_about(seeds[5], (N_ROW, N_COL, D // N_ROW * (D // N_COL)), (D // 32) ** -0.5, 1.25, ((0, 4), (1, 4))),
        "out_bias": scatter_about(seeds[6], (D,), 0.3, 1.75, ((0, 4),), jnp.float32),
        "ln2_gain": jnp.clip(1.0 + 0.18 * jax.random.normal(seeds[7], (D,), jnp.float32), 0.1, 1.9),
        "ln2_bias": scatter_about(seeds[8], (D,), 0.3, 1.75, ((0, 4),), jnp.float32),
        "up_weight": scatter_about(seeds[9], (D, FF), D ** -0.5, 0.21875, ((0, 4), (1, 4))),
        "up_bias": scatter_about(seeds[10], (FF,), 0.5, 3.0, ((0, 4),), jnp.float32),
        "down_weight": scatter_about(seeds[11], (D, FF), FF ** -0.5, 0.109375, ((0, 4), (1, 4))),
        "down_bias": scatter_about(seeds[12], (D,), 0.3, 1.75, ((0, 4),), jnp.float32),
        "out_grad": scatter_about(seeds[13], (TOKENS, D), 1.0, 6.0, ((0, 8), (1, 4))),
    }


highest = lax.Precision.HIGHEST

@jax.custom_vjp
def low(v):
    return lax.optimization_barrier(v.astype(jnp.bfloat16)).astype(jnp.float32)

@jax.custom_vjp
def low_back(v):
    return v

def low_keep(v):
    return (low(v), None)

def low_pass(kept, grad):
    return (grad,)

def back_keep(v):
    return (v, None)

def back_low(kept, grad):
    return (low(grad),)
low.defvjp(low_keep, low_pass)
low_back.defvjp(back_keep, back_low)

def layer_norm(values, gain, shift):
    mean_value = lax.optimization_barrier(jnp.mean(values, axis=-1, keepdims=True))
    variance = lax.optimization_barrier(jnp.mean(values * values, axis=-1, keepdims=True)) - mean_value * mean_value
    return (values - mean_value) * lax.rsqrt(variance + 1e-05) * gain + shift

def attend_head(triple):
    queries, keys_head, values_head = triple
    scores = jnp.dot(queries, keys_head.T, precision=highest) * (1.0 / math.sqrt(HEAD))
    scores = low_back(scores)
    places = jnp.arange(SEQ)
    scores = jnp.where(places[None, :] <= places[:, None], scores, -1e+30)
    weights = jax.nn.softmax(scores, axis=-1)
    return jnp.dot(low(weights), values_head, precision=highest)

def unblock_qkv(blocked):
    shaped = blocked.reshape(N_COL, N_ROW, D // N_COL, 3, D // N_ROW)
    return shaped.transpose(0, 2, 3, 1, 4).reshape(D, 3, D)

def unblock_out(blocked):
    shaped = blocked.reshape(N_ROW, N_COL, D // N_ROW, D // N_COL)
    return shaped.transpose(0, 2, 1, 3).reshape(D, D)

def block_fn(resid_in, gain_one, shift_one, qkv_blocks, qv_shift, out_blocks, out_shift, gain_two, shift_two, up_mat, up_shift, down_mat, down_shift):
    qkv_mat = unblock_qkv(qkv_blocks)
    out_mat = unblock_out(out_blocks)
    normed_one = low(layer_norm(resid_in, gain_one, shift_one))
    projected = jnp.einsum('td,dke->tke', normed_one, qkv_mat, precision=highest)
    shifts = jnp.stack([qv_shift[0], jnp.zeros_like(qv_shift[0]), qv_shift[1]])
    projected = low_back(low(projected + shifts))
    split_heads = projected.reshape(SEQ, 3, HEADS, HEAD).transpose(1, 2, 0, 3)
    mixed = lax.map(jax.checkpoint(attend_head), (split_heads[0], split_heads[1], split_heads[2]))
    attended = low_back(low(mixed.transpose(1, 0, 2).reshape(SEQ, D)))
    branch_one = low_back(jnp.dot(attended, out_mat, precision=highest) + out_shift)
    resid_one = resid_in + branch_one
    normed_two = low(layer_norm(resid_one, gain_two, shift_two))
    hidden_pre = low_back(jnp.dot(normed_two, up_mat, precision=highest) + up_shift)
    hidden_act = low(jax.nn.gelu(hidden_pre, approximate=True))
    branch_two = low_back(jnp.dot(hidden_act, down_mat.T, precision=highest) + down_shift)
    return resid_one + branch_two

def reference(block_input, ln1_gain, ln1_bias, qkv_weight, qv_bias, out_weight, out_bias, ln2_gain, ln2_bias, up_weight, up_bias, down_weight, down_bias, out_grad):
    params = tuple((weight.astype(jnp.float32) for weight in (ln1_gain, ln1_bias, qkv_weight, qv_bias, out_weight, out_bias, ln2_gain, ln2_bias, up_weight, up_bias, down_weight, down_bias)))
    inputs = block_input.astype(jnp.float32).reshape(N_DP, SEQ, D)
    cotangents = out_grad.astype(jnp.float32).reshape(N_DP, SEQ, D)

    def one_sequence(totals, pair):
        resid_in, cotangent = pair
        result, pull = jax.vjp(block_fn, resid_in, *params)
        grads = pull(cotangent)
        summed = tuple((total + grad for total, grad in zip(totals, grads[1:])))
        return (summed, (result.astype(jnp.bfloat16), grads[0].astype(jnp.bfloat16)))
    zeros = tuple((jnp.zeros_like(weight) for weight in params))
    totals, (results, in_grads) = lax.scan(one_sequence, zeros, (inputs, cotangents))
    return (results.reshape(TOKENS, D), in_grads.reshape(TOKENS, D), totals[0], totals[1], totals[2], totals[3], totals[4], totals[5], totals[6], totals[7], totals[8], totals[9], totals[10], totals[11])
```

```python
import math

import jax
import jax.numpy as jnp
from jax import lax
from jax.experimental import pallas as pl
from jax.experimental.pallas import tpu as pltpu
from jax.sharding import PartitionSpec as P

D = 768
HEAD = 64
SCALE = 1.0 / math.sqrt(HEAD)
bf16 = jnp.bfloat16
f32 = jnp.float32


def dot_nn(a, b):
    return lax.dot_general(a, b, (((1,), (0,)), ((), ())), preferred_element_type=f32)


def dot_nt(a, b):
    return lax.dot_general(a, b, (((1,), (1,)), ((), ())), preferred_element_type=f32)


def dot_tn(a, b):
    return lax.dot_general(a, b, (((0,), (0,)), ((), ())), preferred_element_type=f32)


def swap(value, axis, bit):
    n = lax.axis_size(axis)
    return lax.ppermute(value, axis, [(i, i ^ bit) for i in range(n)])


def row_bits():
    n = lax.axis_size("row")
    bits = []
    b = n // 2
    while b:
        bits.append(b)
        b //= 2
    return bits


def row_order():
    order = [0]
    for b in row_bits():
        order = order + [o ^ b for o in order]
    return order


def gather_row(value):
    for b in row_bits():
        value = jnp.concatenate([value, swap(value, "row", b)], axis=0)
    return value


def scatter_row(partial):
    for b in reversed(row_bits()):
        half = partial.shape[0] // 2
        partial = partial[:half] + swap(partial[half:].astype(bf16), "row", b).astype(f32)
    return partial


def turn_cols(value, split, concat):
    return lax.all_to_all(value, "col", split, concat, tiled=True)


def sum_cols(parts):
    n = lax.axis_size("col")
    c = lax.axis_index("col")
    total = lax.dynamic_index_in_dim(parts, c, 0, keepdims=False).astype(f32)
    for k in range(1, n):
        piece = lax.dynamic_index_in_dim(parts, (c + k) % n, 0, keepdims=False)
        total = total + lax.ppermute(piece, "col", [(i, (i + k) % n) for i in range(n)]).astype(f32)
    return total


def sum_grad(grad):
    n_dp = lax.axis_size("dp")
    n_col, rows, width = grad.shape
    if n_dp == 2:
        d = lax.axis_index("dp")
        halves = grad.astype(bf16).reshape(n_col, 2, rows // 2, width)
        mine = lax.dynamic_index_in_dim(halves, d, 1, keepdims=False)
        other = lax.dynamic_index_in_dim(halves, 1 - d, 1, keepdims=False)
        both = (mine.astype(f32) + swap(other, "dp", 1).astype(f32)).astype(bf16)
        part = sum_cols(both).astype(bf16)
        away = swap(part, "dp", 1)
        low = jnp.where(d == 0, part, away)
        high = jnp.where(d == 0, away, part)
        return jnp.concatenate([low, high], axis=0).astype(f32)
    total = sum_cols(grad.astype(bf16)).astype(bf16)
    return lax.psum(total, "dp").astype(f32)


def natural(order, row_ref, n_col, body):
    n_row = len(order)
    r = row_ref[0]
    for place in range(n_row):
        want = place ^ r
        k = jnp.int32(0)
        for idx, o in enumerate(order):
            k = jnp.where(want == o, idx, k)
        for c in range(n_col):
            body(place, c, k)


def load_natural(order, row_ref, src, dst, chunk):
    n_col = src.shape[0]
    block = n_col * chunk

    def one(place, c, k):
        rows = pl.ds(pl.multiple_of(k * chunk, chunk), chunk)
        dst[place * block + c * chunk : place * block + (c + 1) * chunk, :] = src[c, rows, :]

    natural(order, row_ref, n_col, one)


def store_natural(order, row_ref, src, dst, chunk):
    n_col = dst.shape[0]
    block = n_col * chunk

    def one(place, c, k):
        rows = pl.ds(pl.multiple_of(k * chunk, chunk), chunk)
        dst[c, rows, :] = src[place * block + c * chunk : place * block + (c + 1) * chunk, :]

    natural(order, row_ref, n_col, one)


def block_probs(q, k, block, i):
    scores = dot_nt(q, k) * SCALE
    rows = lax.broadcasted_iota(jnp.int32, scores.shape, 0) + i * block
    cols = lax.broadcasted_iota(jnp.int32, scores.shape, 1)
    scores = jnp.where(cols <= rows, scores, -1e30)
    top = jnp.max(scores, axis=-1, keepdims=True)
    e = jnp.exp(scores - top)
    return e / jnp.sum(e, axis=-1, keepdims=True)


def forward_kernel(order, chunk, row_ref, qkv_ref, out_ref, nat, res):
    load_natural(order, row_ref, qkv_ref, nat, chunk)
    seq = nat.shape[0]
    block = seq // len(order)
    k = nat[:, HEAD : 2 * HEAD]
    v = nat[:, 2 * HEAD :]
    for i in range(len(order)):
        upto = (i + 1) * block
        p = block_probs(nat[i * block : upto, :HEAD], k[:upto], block, i)
        res[i * block : upto, :] = dot_nn(p.astype(bf16), v[:upto]).astype(bf16)
    store_natural(order, row_ref, res, out_ref, chunk)


def backward_kernel(order, chunk, row_ref, qkv_ref, do_ref, out_ref, nat, dnat, res, dkt, dvt):
    load_natural(order, row_ref, qkv_ref, nat, chunk)
    load_natural(order, row_ref, do_ref, dnat, chunk)
    seq = nat.shape[0]
    block = seq // len(order)
    k = nat[:, HEAD : 2 * HEAD]
    v = nat[:, 2 * HEAD :]
    dkt[...] = jnp.zeros_like(dkt)
    dvt[...] = jnp.zeros_like(dvt)
    for i in range(len(order)):
        upto = (i + 1) * block
        q = nat[i * block : upto, :HEAD]
        do = dnat[i * block : upto, :]
        p = block_probs(q, k[:upto], block, i)
        dvt[:, :upto] += dot_tn(do, p.astype(bf16))
        dp = dot_nt(do, v[:upto])
        ds = (p * (dp - jnp.sum(dp * p, axis=-1, keepdims=True))).astype(bf16)
        res[i * block : upto, :HEAD] = (dot_nn(ds, k[:upto]) * SCALE).astype(bf16)
        dkt[:, :upto] += dot_tn(q, ds)
    res[:, HEAD : 2 * HEAD] = (dkt[...].T * SCALE).astype(bf16)
    res[:, 2 * HEAD :] = dvt[...].T.astype(bf16)
    store_natural(order, row_ref, res, out_ref, chunk)


def attention_forward(row, qkv, order, chunk):
    n_col, tokens, width = qkv.shape
    seq = n_col * tokens
    return pl.pallas_call(
        lambda *refs: forward_kernel(order, chunk, *refs),
        out_shape=jax.ShapeDtypeStruct((n_col, tokens, HEAD), bf16),
        in_specs=[pl.BlockSpec(memory_space=pltpu.SMEM), pl.BlockSpec(memory_space=pltpu.VMEM)],
        out_specs=pl.BlockSpec(memory_space=pltpu.VMEM),
        scratch_shapes=[pltpu.VMEM((seq, width), bf16), pltpu.VMEM((seq, HEAD), bf16)],
        compiler_params=pltpu.CompilerParams(vmem_limit_bytes=32 * 1024 * 1024),
    )(row, qkv)


def attention_backward(row, qkv, d_out, order, chunk):
    n_col, tokens, width = qkv.shape
    seq = n_col * tokens
    return pl.pallas_call(
        lambda *refs: backward_kernel(order, chunk, *refs),
        out_shape=jax.ShapeDtypeStruct((n_col, tokens, width), bf16),
        in_specs=[
            pl.BlockSpec(memory_space=pltpu.SMEM),
            pl.BlockSpec(memory_space=pltpu.VMEM),
            pl.BlockSpec(memory_space=pltpu.VMEM),
        ],
        out_specs=pl.BlockSpec(memory_space=pltpu.VMEM),
        scratch_shapes=[
            pltpu.VMEM((seq, width), bf16),
            pltpu.VMEM((seq, HEAD), bf16),
            pltpu.VMEM((seq, width), bf16),
            pltpu.VMEM((HEAD, seq), f32),
            pltpu.VMEM((HEAD, seq), f32),
        ],
        compiler_params=pltpu.CompilerParams(vmem_limit_bytes=32 * 1024 * 1024),
    )(row, qkv, d_out)


def norm_stats(v):
    mean = jnp.sum(v, axis=-1, keepdims=True) / D
    var = jnp.sum(v * v, axis=-1, keepdims=True) / D - mean * mean
    inverse = lax.rsqrt(var + 1e-05)
    return (v - mean) * inverse, inverse


def norm_back(grad, centred, inverse, gain):
    scaled = grad * gain
    first = jnp.sum(scaled, axis=-1, keepdims=True) / D
    second = jnp.sum(scaled * centred, axis=-1, keepdims=True) / D
    return inverse * (scaled - first - centred * second)


def gelu_tanh(values):
    return jax.nn.gelu(values, approximate=True)


def column_sums(whole):
    return jnp.sum(whole, axis=0, dtype=f32)


def to_heads(value, parts):
    n_col = lax.axis_size("col")
    t = value.shape[0]
    heads = value.shape[1] // (parts * HEAD)
    cut = value.reshape(t, parts, heads, HEAD).transpose(2, 0, 1, 3).reshape(heads, t, parts * HEAD)
    cut = jnp.concatenate([cut, jnp.zeros((n_col - heads, t, parts * HEAD), value.dtype)], axis=0)
    return turn_cols(cut, 0, 0)


def from_heads(value, parts, heads):
    back = turn_cols(value, 0, 0)[:heads]
    t = back.shape[1]
    return back.reshape(heads, t, parts, HEAD).transpose(1, 2, 0, 3).reshape(t, parts * heads * HEAD)


def body(
    block_input,
    ln1_gain,
    ln1_bias,
    qkv_weight,
    qv_bias,
    out_weight,
    out_bias,
    ln2_gain,
    ln2_bias,
    up_weight,
    up_bias,
    down_weight,
    down_bias,
    out_grad,
):
    n_col = lax.axis_size("col")
    width_in = D // n_col
    width_out = D // lax.axis_size("row")
    heads = width_out // HEAD
    order = row_order()
    own = block_input.shape[0] // n_col
    row = lax.axis_index("row").astype(jnp.int32).reshape(1)
    c = lax.axis_index("col")

    x_own = turn_cols(block_input, 0, 1)
    vectors = lax.all_gather(
        jnp.stack([ln1_gain, ln1_bias, ln2_gain, ln2_bias, out_bias, down_bias]), "col", axis=1, tiled=True
    )
    gain1, bias1, gain2, bias2, bias_out, bias_down = [vectors[i] for i in range(6)]
    w_qkv = lax.all_gather(qkv_weight.reshape(width_in, 3 * width_out), "col", axis=0, tiled=True)
    w_out = lax.all_gather(out_weight.reshape(width_out, width_in), "col", axis=1, tiled=True)
    w_up = lax.all_gather(up_weight, "col", axis=0, tiled=True)
    w_down = lax.all_gather(down_weight, "col", axis=0, tiled=True)
    g_own = turn_cols(out_grad, 0, 1)

    x_all = gather_row(x_own)
    centred1, inverse1 = norm_stats(x_all.astype(f32))
    a1 = (centred1 * gain1 + bias1).astype(bf16)
    shifts = jnp.concatenate([qv_bias[0], jnp.zeros_like(qv_bias[0]), qv_bias[1]])
    qkv = (dot_nn(a1, w_qkv) + shifts).astype(bf16)
    qkv_head = to_heads(qkv, 3)
    attended = from_heads(attention_forward(row, qkv_head, order, own), 1, heads)

    resid1 = x_own.astype(f32) + scatter_row(dot_nn(attended, w_out)) + bias_out
    centred2, inverse2 = norm_stats(resid1)
    a2 = gather_row((centred2 * gain2 + bias2).astype(bf16))
    g_all = gather_row(g_own)
    d_act = dot_nn(g_all, w_down)
    pre = dot_nn(a2, w_up) + up_bias
    act = gelu_tanh(pre).astype(bf16)
    d_pre = jax.vjp(gelu_tanh, pre)[1](d_act)[0].astype(bf16)

    d_a2 = scatter_row(dot_nt(d_pre, w_up))
    d_resid1 = g_own.astype(f32) + norm_back(d_a2, centred2, inverse2, gain2)
    gp = d_resid1.astype(bf16)
    gp_all = gather_row(gp)
    d_attended = dot_nt(gp_all, w_out).astype(bf16)
    d_head = to_heads(d_attended, 1)

    block_out = resid1 + scatter_row(dot_nt(act, w_down)) + bias_down
    block_output = turn_cols(block_out.astype(bf16), 1, 0)
    d_down = sum_grad(dot_tn(g_all, act).reshape(n_col, width_in, -1))
    d_up = sum_grad(dot_tn(a2, d_pre).reshape(n_col, width_in, -1))
    d_out = sum_grad(dot_tn(attended, gp_all).reshape(width_out, n_col, width_in).transpose(1, 0, 2))

    d_qkv = from_heads(attention_backward(row, qkv_head, d_head, order, own), 3, heads)
    d_a1_part = dot_nt(d_qkv, w_qkv)
    d_a1 = scatter_row(d_a1_part)
    input_grad = d_resid1 + norm_back(d_a1, centred1[:own], inverse1[:own], gain1)
    input_grad = turn_cols(input_grad.astype(bf16), 1, 0)
    d_qkv_w = sum_grad(dot_tn(a1, d_qkv).reshape(n_col, width_in, -1))

    sums_early = lax.psum(
        jnp.stack([column_sums(d_a2 * centred2), column_sums(d_a2), column_sums(gp), column_sums(g_own)]),
        ("dp", "row", "col"),
    )
    sums_late = lax.psum(jnp.stack([column_sums(d_a1_part * centred1), column_sums(d_a1_part)]), ("dp", "row", "col"))
    mine = lax.dynamic_slice_in_dim(jnp.concatenate([sums_late, sums_early]), c * width_in, width_in, 1)
    d_up_bias = lax.psum(column_sums(d_pre), ("dp", "col"))
    d_qkv_bias = lax.psum(column_sums(d_qkv), ("dp", "col")).reshape(3, width_out)
    d_qv_bias = jnp.stack([d_qkv_bias[0], d_qkv_bias[2]])

    return (
        block_output,
        input_grad,
        mine[0],
        mine[1],
        d_qkv_w.reshape(1, 1, -1),
        d_qv_bias,
        d_out.reshape(1, 1, -1),
        mine[4],
        mine[2],
        mine[3],
        d_up,
        d_up_bias,
        d_down,
        mine[5],
    )


def solution(mesh):
    in_specs = (
        P(("dp", "row"), "col"),
        P("col"),
        P("col"),
        P("col", "row", None),
        P(None, "row"),
        P("row", "col", None),
        P("col"),
        P("col"),
        P("col"),
        P("col", "row"),
        P("row"),
        P("col", "row"),
        P("col"),
        P(("dp", "row"), "col"),
    )
    out_specs = (
        P(("dp", "row"), "col"),
        P(("dp", "row"), "col"),
        P("col"),
        P("col"),
        P("col", "row", None),
        P(None, "row"),
        P("row", "col", None),
        P("col"),
        P("col"),
        P("col"),
        P("col", "row"),
        P("row"),
        P("col", "row"),
        P("col"),
    )
    return jax.shard_map(body, mesh=mesh, in_specs=in_specs, out_specs=out_specs, check_vma=False)
```

```python
import functools
import math

import jax
import jax.numpy as jnp
from jax import lax
from jax.experimental import pallas as pl
from jax.experimental.pallas import tpu as pltpu
from jax.sharding import PartitionSpec as P

D = 768
HEAD = 64
SCALE = 1.0 / math.sqrt(HEAD)
C0 = math.sqrt(2.0 / math.pi)
C1 = 0.044715
bf16 = jnp.bfloat16
f32 = jnp.float32
VMEM = pl.BlockSpec(memory_space=pltpu.VMEM)
SMEM = pl.BlockSpec(memory_space=pltpu.SMEM)


def dot_nn(a, b):
    return lax.dot_general(a, b, (((1,), (0,)), ((), ())), preferred_element_type=f32)


def dot_nt(a, b):
    return lax.dot_general(a, b, (((1,), (1,)), ((), ())), preferred_element_type=f32)


def dot_tn(a, b):
    return lax.dot_general(a, b, (((0,), (0,)), ((), ())), preferred_element_type=f32)


def call(kernel, outs, scalars, args, scratch=()):
    return pl.pallas_call(
        kernel,
        out_shape=[jax.ShapeDtypeStruct(s, t) for s, t in outs],
        in_specs=[SMEM] + [VMEM] * len(args),
        out_specs=[VMEM] * len(outs),
        scratch_shapes=[pltpu.VMEM(s, t) for s, t in scratch],
        compiler_params=pltpu.CompilerParams(vmem_limit_bytes=40 * 1024 * 1024),
    )(scalars, *args)


def swap(value, axis, bit, low=0, high=None):
    n = lax.axis_size(axis)
    return lax.ppermute(value, axis, [(i, i ^ bit) for i in range(n)])


def swap_some(value, axis, bit, sources, targets):
    n = lax.axis_size(axis)
    return lax.ppermute(value, axis, [(i, i ^ bit) for i in range(n) if i < sources and i ^ bit < targets])


def bits_of(axis, first=1):
    n = lax.axis_size(axis)
    bits = []
    b = first
    while b < n:
        bits.append(b)
        b *= 2
    return bits


def row_order():
    order = [0]
    for b in reversed(bits_of("row")):
        order = order + [o ^ b for o in order]
    return order


def gather_row(value):
    pieces = [value]
    for b in reversed(bits_of("row")):
        pieces = pieces + [swap(p, "row", b) for p in pieces]
    return pieces


def finish_row(keep, send):
    bits = bits_of("row")
    total = keep + swap(send, "row", bits[0]).astype(f32)
    for b in bits[1:]:
        half = total.shape[0] // 2
        total = total[:half] + swap(total[half:].astype(bf16), "row", b).astype(f32)
    return total


def by_column(pieces, c):
    pieces = list(pieces)
    bit = 1
    while bit < len(pieces):
        on = (c & bit) != 0
        pieces = [jnp.where(on, pieces[i ^ bit], pieces[i]) for i in range(len(pieces))]
        bit *= 2
    return pieces


def turn_in(value, c):
    n = lax.axis_size("col")
    t = value.shape[0] // n
    cut = [lax.dynamic_slice_in_dim(value, (c ^ k) * t, t, 0) for k in range(n)]
    return jnp.concatenate([cut[0]] + [swap(cut[k], "col", k) for k in range(1, n)], axis=1)


def turn_out(value, c):
    n = lax.axis_size("col")
    w = value.shape[1] // n
    cut = [value[:, k * w : (k + 1) * w] for k in range(n)]
    pieces = [cut[0]] + [swap(cut[k], "col", k) for k in range(1, n)]
    return jnp.concatenate(by_column(pieces, c), axis=0)


def sum_cols(parts):
    total = parts[0].astype(f32)
    for k in range(1, len(parts)):
        total = total + swap(parts[k].astype(bf16), "col", k).astype(f32)
    return total


def sum_dp(value, first):
    for b in bits_of("dp", first):
        value = (value.astype(f32) + swap(value.astype(bf16), "dp", b).astype(f32)).astype(bf16)
    return value


def sum_halves(mine, other):
    n_col = lax.axis_size("col")
    rows = mine.shape[0] // n_col
    got = swap(other, "dp", 1)
    parts = [
        (mine[k * rows : (k + 1) * rows].astype(f32) + got[k * rows : (k + 1) * rows].astype(f32)).astype(bf16)
        for k in range(n_col)
    ]
    total = sum_dp(sum_cols(parts).astype(bf16), 2)
    return total, swap(total, "dp", 1)


def place(scal, order, k, kk, chunk, n_col):
    at = ((scal[0] ^ order[kk]) * n_col + (scal[1] ^ k)) * chunk
    return pl.ds(pl.multiple_of(at, chunk), chunk)


def load_natural(scal, order, pieces, dst):
    chunk = pieces[0].shape[0] // len(order)
    for k, piece in enumerate(pieces):
        for kk in range(len(order)):
            dst[place(scal, order, k, kk, chunk, len(pieces)), :] = piece[kk * chunk : (kk + 1) * chunk, :]


def store_natural(scal, order, src, pieces):
    chunk = pieces[0].shape[0] // len(order)
    for k, piece in enumerate(pieces):
        for kk in range(len(order)):
            piece[kk * chunk : (kk + 1) * chunk, :] = src[place(scal, order, k, kk, chunk, len(pieces)), :]


def block_probs(q, k, block, i):
    scores = dot_nt(q, k) * SCALE
    rows = lax.broadcasted_iota(jnp.int32, scores.shape, 0) + i * block
    cols = lax.broadcasted_iota(jnp.int32, scores.shape, 1)
    scores = jnp.where(cols <= rows, scores, -1e30)
    top = jnp.max(scores, axis=-1, keepdims=True)
    e = jnp.exp(scores - top)
    return e / jnp.sum(e, axis=-1, keepdims=True)


def forward_kernel(order, n_col, scal, *refs):
    pieces, outs, (nat, res) = refs[:n_col], refs[n_col : 2 * n_col], refs[2 * n_col :]
    load_natural(scal, order, pieces, nat)
    block = nat.shape[0] // len(order)
    k = nat[:, HEAD : 2 * HEAD]
    v = nat[:, 2 * HEAD :]
    for i in range(len(order)):
        upto = (i + 1) * block
        p = block_probs(nat[i * block : upto, :HEAD], k[:upto], block, i)
        res[i * block : upto, :] = dot_nn(p.astype(bf16), v[:upto]).astype(bf16)
    store_natural(scal, order, res, outs)


def backward_kernel(order, n_col, scal, *refs):
    pieces, grads, outs = refs[:n_col], refs[n_col : 2 * n_col], refs[2 * n_col : 3 * n_col]
    nat, dnat, res, dkt, dvt = refs[3 * n_col :]
    load_natural(scal, order, pieces, nat)
    load_natural(scal, order, grads, dnat)
    block = nat.shape[0] // len(order)
    k = nat[:, HEAD : 2 * HEAD]
    v = nat[:, 2 * HEAD :]
    dkt[...] = jnp.zeros_like(dkt)
    dvt[...] = jnp.zeros_like(dvt)
    for i in range(len(order)):
        upto = (i + 1) * block
        q = nat[i * block : upto, :HEAD]
        do = dnat[i * block : upto, :]
        p = block_probs(q, k[:upto], block, i)
        dvt[:, :upto] += dot_tn(do, p.astype(bf16))
        dp = dot_nt(do, v[:upto])
        ds = (p * (dp - jnp.sum(dp * p, axis=-1, keepdims=True))).astype(bf16)
        res[i * block : upto, :HEAD] = (dot_nn(ds, k[:upto]) * SCALE).astype(bf16)
        dkt[:, :upto] += dot_tn(q, ds)
    res[:, HEAD : 2 * HEAD] = (dkt[...].T * SCALE).astype(bf16)
    res[:, 2 * HEAD :] = dvt[...].T.astype(bf16)
    store_natural(scal, order, res, outs)


def norm_stats(v):
    mean = jnp.sum(v, axis=-1, keepdims=True) / D
    var = jnp.sum(v * v, axis=-1, keepdims=True) / D - mean * mean
    inverse = lax.rsqrt(var + 1e-05)
    return (v - mean) * inverse, inverse


def norm_back(grad, centred, inverse, gain):
    scaled = grad * gain
    first = jnp.sum(scaled, axis=-1, keepdims=True) / D
    second = jnp.sum(scaled * centred, axis=-1, keepdims=True) / D
    return inverse * (scaled - first - centred * second)


def stacked(refs):
    return jnp.concatenate([r[...] for r in refs], axis=0)


def qkv_kernel(n_row, n_col, heads, scal, *refs):
    xs, refs = refs[:n_row], refs[n_row:]
    gain, bias, shifts, w_own = refs[:4]
    near, far = refs[4 : 3 + n_col], refs[3 + n_col : 2 + 2 * n_col]
    outs, (a1_out, w_all, cut) = refs[2 + 2 * n_col : 2 + 3 * n_col], refs[2 + 3 * n_col :]
    c, d = scal[1], scal[2]
    rows = w_own.shape[0]
    half = rows // 2
    w_all[:rows, :] = w_own[...]
    for k in range(1, n_col):
        w_all[pl.ds(pl.multiple_of(k * rows + d * half, 32), half), :] = near[k - 1][...]
        w_all[pl.ds(pl.multiple_of(k * rows + (1 - d) * half, 32), half), :] = far[k - 1][...]
    centred, _ = norm_stats(stacked(xs).astype(f32))
    a1 = (centred * gain[...] + bias[...]).astype(bf16)
    a1_out[...] = a1
    qkv = (dot_nn(a1, w_all[...]) + shifts[...]).astype(bf16)
    width = heads * HEAD
    for h in range(n_col):
        if h < heads:
            lo = h * HEAD
            piece = jnp.concatenate([qkv[:, j * width + lo : j * width + lo + HEAD] for j in range(3)], axis=1)
        else:
            piece = jnp.zeros((qkv.shape[0], 3 * HEAD), bf16)
        cut[h ^ c] = piece
    for k in range(n_col):
        outs[k][...] = cut[k]


def halves_out(value, keep, send):
    half = value.shape[0] // 2
    keep[...] = value[:half]
    send[...] = value[half:].astype(bf16)


def out_kernel(n_col, heads, scal, *refs):
    os, ws = refs[:n_col], refs[n_col : 2 * n_col]
    att_out, w_out, keep, send, cut = refs[2 * n_col :]
    c = scal[1]
    for k in range(n_col):
        cut[c ^ k] = os[k][...]
    att = jnp.concatenate([cut[h] for h in range(heads)], axis=1)
    w = jnp.concatenate([r[...] for r in ws], axis=1)
    att_out[...] = att
    w_out[...] = w
    halves_out(dot_nn(att, w), keep, send)


def mlp_kernel(n_row, n_col, scal, *refs):
    a2s, gs, refs = refs[:n_row], refs[n_row : 2 * n_row], refs[2 * n_row :]
    up_bias, up_own, down_own = refs[:3]
    near, far = refs[3 : 2 + n_col], refs[2 + n_col : 1 + 2 * n_col]
    act_out, d_pre_out, bias_sum, a_keep, a_send, y_keep, y_send, wu, wd = refs[1 + 2 * n_col :]
    rows, width = up_own.shape
    half = width // 2
    wu[:rows, :] = up_own[...]
    wd[:rows, :] = down_own[...]
    for k in range(1, n_col):
        at = slice(k * rows, (k + 1) * rows)
        wu[at, :half] = near[k - 1][:rows, :]
        wd[at, :half] = near[k - 1][rows:, :]
        wu[at, half:] = far[k - 1][:rows, :]
        wd[at, half:] = far[k - 1][rows:, :]
    pre = dot_nn(stacked(a2s), wu[...]) + up_bias[...]
    square = pre * pre
    t = jnp.tanh(C0 * (pre + C1 * (square * pre)))
    act = (0.5 * pre * (1.0 + t)).astype(bf16)
    slope = 0.5 * (1.0 + t) + (0.5 * C0) * pre * (1.0 - t * t) * (1.0 + (3.0 * C1) * square)
    d_act = dot_nn(stacked(gs), wd[...])
    d_pre = (d_act * slope).astype(bf16)
    act_out[...] = act
    d_pre_out[...] = d_pre
    bias_sum[...] = jnp.sum(d_pre.astype(f32), axis=0, keepdims=True)
    halves_out(dot_nt(d_pre, wu[...]), a_keep, a_send)
    halves_out(dot_nt(act, wd[...]), y_keep, y_send)


def mlp_grad_kernel(n_row, scal, *refs):
    a2s, gs, refs = refs[:n_row], refs[n_row : 2 * n_row], refs[2 * n_row :]
    act, d_pre, up_mine, up_other, down_mine, down_other = refs
    half = act.shape[1] // 2
    a2, g = stacked(a2s), stacked(gs)
    up_mine[...] = dot_tn(a2, d_pre[:, :half]).astype(bf16)
    up_other[...] = dot_tn(a2, d_pre[:, half:]).astype(bf16)
    down_mine[...] = dot_tn(g, act[:, :half]).astype(bf16)
    down_other[...] = dot_tn(g, act[:, half:]).astype(bf16)


def d_att_kernel(n_row, n_col, heads, scal, *refs):
    gps, (att, w), refs = refs[:n_row], refs[n_row : n_row + 2], refs[n_row + 2 :]
    outs, grads, cut = refs[:n_col], refs[n_col : 2 * n_col], refs[2 * n_col]
    c = scal[1]
    gp = stacked(gps)
    d_att = dot_nt(gp, w[...]).astype(bf16)
    for h in range(n_col):
        if h < heads:
            cut[h ^ c] = d_att[:, h * HEAD : (h + 1) * HEAD]
        else:
            cut[h ^ c] = jnp.zeros((gp.shape[0], HEAD), bf16)
    for k in range(n_col):
        outs[k][...] = cut[k]
    grad = dot_tn(att[...], gp).astype(bf16)
    w_k = grad.shape[1] // n_col
    for k in range(n_col):
        grads[k][...] = grad[:, k * w_k : (k + 1) * w_k]


def d_a1_kernel(n_row, n_col, heads, scal, *refs):
    ds, xs, refs = refs[:n_col], refs[n_col : n_col + n_row], refs[n_col + n_row :]
    a1, w, keep, send, sums, bias_sum, mine, other, cut, full = refs
    c, d = scal[1], scal[2]
    for k in range(n_col):
        cut[c ^ k] = ds[k][...]
    pieces = [cut[h] for h in range(heads)]
    d_qkv = jnp.concatenate([p[:, j * HEAD : (j + 1) * HEAD] for j in range(3) for p in pieces], axis=1)
    part = dot_nt(d_qkv, w[...])
    halves_out(part, keep, send)
    full[...] = dot_tn(a1[...], d_qkv).astype(bf16)
    rows = full.shape[0] // n_col
    half = rows // 2
    for k in range(n_col):
        at = slice(k * half, (k + 1) * half)
        mine[at, :] = full[pl.ds(pl.multiple_of(k * rows + d * half, 32), half), :]
        other[at, :] = full[pl.ds(pl.multiple_of(k * rows + (1 - d) * half, 32), half), :]
    centred, _ = norm_stats(stacked(xs).astype(f32))
    sums[0:1, :] = jnp.sum(part * centred, axis=0, keepdims=True)
    sums[1:2, :] = jnp.sum(part, axis=0, keepdims=True)
    bias_sum[...] = jnp.sum(d_qkv.astype(f32), axis=0, keepdims=True)


def body(
    block_input,
    ln1_gain,
    ln1_bias,
    qkv_weight,
    qv_bias,
    out_weight,
    out_bias,
    ln2_gain,
    ln2_bias,
    up_weight,
    up_bias,
    down_weight,
    down_bias,
    out_grad,
):
    n_col = lax.axis_size("col")
    n_row = lax.axis_size("row")
    width_in = D // n_col
    width_out = D // n_row
    heads = width_out // HEAD
    order = row_order()
    own = block_input.shape[0] // n_col
    tokens = own * n_row
    c = lax.axis_index("col").astype(jnp.int32)
    d = lax.axis_index("dp").astype(jnp.int32) & 1
    scal = jnp.stack([lax.axis_index("row").astype(jnp.int32), c, d])
    cols = range(1, n_col)

    x_own = turn_in(block_input, c)
    x_all = gather_row(x_own)

    vectors = jnp.stack([ln1_gain, ln1_bias, ln2_gain, ln2_bias, out_bias, down_bias])
    for b in bits_of("col"):
        vectors = jnp.concatenate([vectors, swap(vectors, "col", b)], axis=1)
    gain1, bias1, gain2, bias2, bias_out, bias_down = [vectors[i : i + 1] for i in range(6)]
    w_qkv = qkv_weight.reshape(width_in, 3 * width_out)
    half_qkv = lax.dynamic_slice_in_dim(w_qkv, d * (width_in // 2), width_in // 2, 0)
    near_qkv = [swap(half_qkv, "col", k) for k in cols]
    far_qkv = [swap(v, "dp", 1) for v in near_qkv]
    w_out_own = out_weight.reshape(width_out, width_in)
    w_out = [w_out_own] + [swap(w_out_own, "col", k) for k in cols]
    g_own = turn_in(out_grad, c)
    g_all = gather_row(g_own)

    half_ff = up_weight.shape[1] // 2

    def turned(v):
        return jnp.where(d == 0, v, jnp.concatenate([v[:, half_ff:], v[:, :half_ff]], axis=1))

    up_own, down_own, up_shift = turned(up_weight), turned(down_weight), turned(up_bias[None])
    half_mlp = jnp.concatenate([up_own[:, :half_ff], down_own[:, :half_ff]], axis=0)
    near_mlp = [swap(half_mlp, "col", k) for k in cols]
    far_mlp = [swap(v, "dp", 1) for v in near_mlp]

    shifts = jnp.concatenate([qv_bias[0], jnp.zeros_like(qv_bias[0]), qv_bias[1]])[None]
    res = call(
        functools.partial(qkv_kernel, n_row, n_col, heads),
        [((tokens, 3 * HEAD), bf16)] * n_col + [((tokens, D), bf16), ((D, 3 * width_out), bf16)],
        scal,
        [*x_all, gain1, bias1, shifts, w_qkv, *near_qkv, *far_qkv],
        [((n_col, tokens, 3 * HEAD), bf16)],
    )
    qkv_cut, (a1, w_qkv_all) = res[:n_col], res[n_col:]
    qkv_head = [qkv_cut[0]] + [swap_some(qkv_cut[k], "col", k, n_col, heads) for k in cols]
    att_head = call(
        functools.partial(forward_kernel, order, n_col),
        [((tokens, HEAD), bf16)] * n_col,
        scal,
        qkv_head,
        [((tokens * n_col, 3 * HEAD), bf16), ((tokens * n_col, HEAD), bf16)],
    )
    att_cut = [att_head[0]] + [swap_some(att_head[k], "col", k, heads, n_col) for k in cols]
    attended, w_out_all, o_keep, o_send = call(
        functools.partial(out_kernel, n_col, heads),
        [
            ((tokens, width_out), bf16),
            ((width_out, D), bf16),
            ((tokens // 2, D), f32),
            ((tokens // 2, D), bf16),
        ],
        scal,
        [*att_cut, *w_out],
        [((n_col, tokens, HEAD), bf16)],
    )
    resid1 = x_own.astype(f32) + finish_row(o_keep, o_send) + bias_out
    centred2, inverse2 = norm_stats(resid1)
    a2 = gather_row((centred2 * gain2 + bias2).astype(bf16))

    ff = 2 * half_ff
    act, d_pre, up_sum, a_keep, a_send, y_keep, y_send = call(
        functools.partial(mlp_kernel, n_row, n_col),
        [
            ((tokens, ff), bf16),
            ((tokens, ff), bf16),
            ((1, ff), f32),
            ((tokens // 2, D), f32),
            ((tokens // 2, D), bf16),
            ((tokens // 2, D), f32),
            ((tokens // 2, D), bf16),
        ],
        scal,
        [*a2, *g_all, up_shift, up_own, down_own, *near_mlp, *far_mlp],
        [((D, ff), bf16), ((D, ff), bf16)],
    )
    d_a2 = finish_row(a_keep, a_send)
    d_resid1 = g_own.astype(f32) + norm_back(d_a2, centred2, inverse2, gain2)
    gp = d_resid1.astype(bf16)
    gp_all = gather_row(gp)
    res = call(
        functools.partial(d_att_kernel, n_row, n_col, heads),
        [((tokens, HEAD), bf16)] * n_col + [((width_out, width_in), bf16)] * n_col,
        scal,
        [*gp_all, attended, w_out_all],
        [((n_col, tokens, HEAD), bf16)],
    )
    d_att_cut, d_out_parts = res[:n_col], res[n_col:]
    d_att_head = [d_att_cut[0]] + [swap_some(d_att_cut[k], "col", k, n_col, heads) for k in cols]
    d_qkv_head = call(
        functools.partial(backward_kernel, order, n_col),
        [((tokens, 3 * HEAD), bf16)] * n_col,
        scal,
        [*qkv_head, *d_att_head],
        [
            ((tokens * n_col, 3 * HEAD), bf16),
            ((tokens * n_col, HEAD), bf16),
            ((tokens * n_col, 3 * HEAD), bf16),
            ((HEAD, tokens * n_col), f32),
            ((HEAD, tokens * n_col), f32),
        ],
    )
    d_qkv_cut = [d_qkv_head[0]] + [swap_some(d_qkv_head[k], "col", k, heads, n_col) for k in cols]
    d_keep, d_send, ln1_sums, qkv_sum, qkv_mine, qkv_other = call(
        functools.partial(d_a1_kernel, n_row, n_col, heads),
        [
            ((tokens // 2, D), f32),
            ((tokens // 2, D), bf16),
            ((2, D), f32),
            ((1, 3 * width_out), f32),
            ((D // 2, 3 * width_out), bf16),
            ((D // 2, 3 * width_out), bf16),
        ],
        scal,
        [*d_qkv_cut, *x_all, a1, w_qkv_all],
        [((n_col, tokens, 3 * HEAD), bf16), ((D, 3 * width_out), bf16)],
    )

    block_out = resid1 + finish_row(y_keep, y_send) + bias_down
    block_output = turn_out(block_out.astype(bf16), c)

    def two(part, away, axis):
        low = jnp.where(d == 0, part, away)
        high = jnp.where(d == 0, away, part)
        return jnp.concatenate([low, high], axis=axis).astype(f32)

    up_mine, up_other, down_mine, down_other = call(
        functools.partial(mlp_grad_kernel, n_row),
        [((D, half_ff), bf16)] * 4,
        scal,
        [*a2, *g_all, act, d_pre],
    )
    d_down = two(*sum_halves(down_mine, down_other), 1)
    d_up = two(*sum_halves(up_mine, up_other), 1)
    d_out = sum_dp(sum_cols(d_out_parts).astype(bf16), 1).astype(f32)

    d_a1 = finish_row(d_keep, d_send)
    centred1, inverse1 = norm_stats(x_own.astype(f32))
    input_grad = d_resid1 + norm_back(d_a1, centred1, inverse1, gain1)
    input_grad = turn_out(input_grad.astype(bf16), c)
    d_qkv_w = two(*sum_halves(qkv_mine, qkv_other), 0)

    def add(value, axis, bit):
        return value + swap(value, axis, bit)

    feats = jnp.concatenate(
        [
            ln1_sums,
            jnp.sum(d_a2 * centred2, axis=0, keepdims=True),
            jnp.sum(d_a2, axis=0, keepdims=True),
            jnp.sum(gp.astype(f32), axis=0, keepdims=True),
            jnp.sum(g_own.astype(f32), axis=0, keepdims=True),
        ]
    )
    feats = feats.reshape(6, n_col, width_in)
    for b in bits_of("col"):
        pairs = feats.reshape(6, -1, 2, width_in)
        feats = pairs[:, :, 0] + swap(pairs[:, :, 1], "col", b)
    feats = feats.reshape(6, width_in)
    for b in bits_of("row"):
        feats = add(feats, "row", b)
    for b in bits_of("dp"):
        feats = add(feats, "dp", b)
    hidden = jnp.concatenate([turned(up_sum), qkv_sum], axis=1)
    for b in bits_of("col"):
        hidden = add(hidden, "col", b)
    for b in bits_of("dp"):
        hidden = add(hidden, "dp", b)
    d_up_bias = hidden[0, :ff]
    d_qv_bias = jnp.stack([hidden[0, ff : ff + width_out], hidden[0, ff + 2 * width_out :]])

    return (
        block_output,
        input_grad,
        feats[0],
        feats[1],
        d_qkv_w.reshape(1, 1, -1),
        d_qv_bias,
        d_out.reshape(1, 1, -1),
        feats[4],
        feats[2],
        feats[3],
        d_up,
        d_up_bias,
        d_down,
        feats[5],
    )


def solution(mesh):
    in_specs = (
        P(("dp", "row"), "col"),
        P("col"),
        P("col"),
        P("col", "row", None),
        P(None, "row"),
        P("row", "col", None),
        P("col"),
        P("col"),
        P("col"),
        P("col", "row"),
        P("row"),
        P("col", "row"),
        P("col"),
        P(("dp", "row"), "col"),
    )
    out_specs = (
        P(("dp", "row"), "col"),
        P(("dp", "row"), "col"),
        P("col"),
        P("col"),
        P("col", "row", None),
        P(None, "row"),
        P("row", "col", None),
        P("col"),
        P("col"),
        P("col"),
        P("col", "row"),
        P("row"),
        P("col", "row"),
        P("col"),
    )
    return jax.shard_map(body, mesh=mesh, in_specs=in_specs, out_specs=out_specs, check_vma=False)
```

```python
import functools
import math

import jax
import jax.numpy as jnp
from jax import lax
from jax.experimental import pallas as pl
from jax.experimental.pallas import tpu as pltpu
from jax.sharding import PartitionSpec as P

D = 768
HEAD = 64
SCALE = 1.0 / math.sqrt(HEAD)
C0 = math.sqrt(2.0 / math.pi)
C1 = 0.044715
bf16 = jnp.bfloat16
f32 = jnp.float32
VMEM = pl.BlockSpec(memory_space=pltpu.VMEM)
SMEM = pl.BlockSpec(memory_space=pltpu.SMEM)


def dot_nn(a, b):
    return lax.dot_general(a, b, (((1,), (0,)), ((), ())), preferred_element_type=f32)


def dot_nt(a, b):
    return lax.dot_general(a, b, (((1,), (1,)), ((), ())), preferred_element_type=f32)


def dot_tn(a, b):
    return lax.dot_general(a, b, (((0,), (0,)), ((), ())), preferred_element_type=f32)


def call(kernel, outs, scalars, args, scratch=()):
    first = [] if scalars is None else [scalars]
    return pl.pallas_call(
        kernel,
        out_shape=[jax.ShapeDtypeStruct(s, t) for s, t in outs],
        in_specs=[SMEM] * len(first) + [VMEM] * len(args),
        out_specs=[VMEM] * len(outs),
        scratch_shapes=[pltpu.VMEM(s, t) for s, t in scratch],
        compiler_params=pltpu.CompilerParams(vmem_limit_bytes=20 * 1024 * 1024),
    )(*first, *args)


def swap(value, axis, bit):
    n = lax.axis_size(axis)
    return lax.ppermute(value, axis, [(i, i ^ bit) for i in range(n)])


def turn(value, split=0, concat=0):
    return lax.all_to_all(value, "col", split, concat, tiled=True)


def bits_of(axis, first=1):
    n = lax.axis_size(axis)
    bits = []
    b = first
    while b < n:
        bits.append(b)
        b *= 2
    return bits


def row_order():
    order = [0]
    for b in reversed(bits_of("row")):
        order = order + [o ^ b for o in order]
    return order


def gather_row(value):
    pieces = [value]
    for b in reversed(bits_of("row")):
        pieces = pieces + [swap(p, "row", b) for p in pieces]
    return pieces


def finish_row(keep, send):
    bits = bits_of("row")
    for b in bits[:-1]:
        keep, send = add_halves(keep, swap(send, "row", b))
    return keep, swap(send, "row", bits[-1])


def add_halves(keep, got):
    rows, width = keep.shape
    return call(halves_kernel, [((rows // 2, width), f32), ((rows // 2, width), bf16)], None, [keep, got])


def three_parts(v):
    high = lax.optimization_barrier(v.astype(bf16))
    rest = v - high.astype(f32)
    middle = lax.optimization_barrier(rest.astype(bf16))
    low = (rest - middle.astype(f32)).astype(bf16)
    return jnp.concatenate([high, middle, low], axis=0)


def place(scal, order, col, kk, chunk, n_col, second):
    half = chunk // 2
    at = ((scal[0] ^ order[kk]) * n_col + col) * chunk + second * half
    return pl.ds(pl.multiple_of(at, half), half)


def load_natural(scal, order, src, dst):
    n_col, rows, width = src.shape
    half = rows // len(order)
    for col in range(n_col):
        for kk in range(len(order)):
            both = src[col, kk * half : (kk + 1) * half, :]
            for second in range(2):
                at = place(scal, order, col, kk, 2 * half, n_col, second)
                dst[at, :] = both[:, second * (width // 2) : (second + 1) * (width // 2)]


def store_natural(scal, order, src, dst):
    n_col, rows, _ = dst.shape
    half = rows // len(order)
    for col in range(n_col):
        for kk in range(len(order)):
            both = [src[place(scal, order, col, kk, 2 * half, n_col, second), :] for second in range(2)]
            dst[col, kk * half : (kk + 1) * half, :] = jnp.concatenate(both, axis=1)


def beside(value, chunk):
    half = chunk // 2
    starts = range(0, value.shape[0], chunk)
    first = jnp.concatenate([value[i : i + half] for i in starts], axis=0)
    second = jnp.concatenate([value[i + half : i + chunk] for i in starts], axis=0)
    return jnp.concatenate([first, second], axis=1)


def under(value, chunk):
    half = chunk // 2
    width = value.shape[1] // 2
    parts = []
    for i in range(0, value.shape[0], half):
        parts += [value[i : i + half, :width], value[i : i + half, width:]]
    return jnp.concatenate(parts, axis=0)


def block_probs(q, k, block, i):
    scores = dot_nt(q, k) * SCALE
    rows = lax.broadcasted_iota(jnp.int32, scores.shape, 0) + i * block
    cols = lax.broadcasted_iota(jnp.int32, scores.shape, 1)
    scores = jnp.where(cols <= rows, scores, -1e30)
    top = jnp.max(scores, axis=-1, keepdims=True)
    e = jnp.exp(scores - top)
    return e / jnp.sum(e, axis=-1, keepdims=True)


def forward_kernel(order, scal, qkv_ref, out_ref, nat, res):
    load_natural(scal, order, qkv_ref, nat)
    block = nat.shape[0] // len(order)
    k = nat[:, HEAD : 2 * HEAD]
    v = nat[:, 2 * HEAD :]
    for i in range(len(order)):
        upto = (i + 1) * block
        p = block_probs(nat[i * block : upto, :HEAD], k[:upto], block, i)
        res[i * block : upto, :] = dot_nn(p.astype(bf16), v[:upto]).astype(bf16)
    store_natural(scal, order, res, out_ref)


def backward_kernel(order, scal, qkv_ref, do_ref, out_ref, nat, dnat, res, dkt, dvt):
    load_natural(scal, order, qkv_ref, nat)
    load_natural(scal, order, do_ref, dnat)
    block = nat.shape[0] // len(order)
    k = nat[:, HEAD : 2 * HEAD]
    v = nat[:, 2 * HEAD :]
    dkt[...] = jnp.zeros_like(dkt)
    dvt[...] = jnp.zeros_like(dvt)
    for i in range(len(order)):
        upto = (i + 1) * block
        q = nat[i * block : upto, :HEAD]
        do = dnat[i * block : upto, :]
        p = block_probs(q, k[:upto], block, i)
        dvt[:, :upto] += dot_tn(do, p.astype(bf16))
        dp = dot_nt(do, v[:upto])
        ds = (p * (dp - jnp.sum(dp * p, axis=-1, keepdims=True))).astype(bf16)
        res[i * block : upto, :HEAD] = (dot_nn(ds, k[:upto]) * SCALE).astype(bf16)
        dkt[:, :upto] += dot_tn(q, ds)
    res[:, HEAD : 2 * HEAD] = (dkt[...].T * SCALE).astype(bf16)
    res[:, 2 * HEAD :] = dvt[...].T.astype(bf16)
    store_natural(scal, order, res, out_ref)


def norm_stats(v):
    mean = jnp.sum(v, axis=-1, keepdims=True) / D
    var = jnp.sum(v * v, axis=-1, keepdims=True) / D - mean * mean
    inverse = lax.rsqrt(var + 1e-05)
    return (v - mean) * inverse, inverse


def norm_back(grad, centred, inverse, gain):
    scaled = grad * gain
    first = jnp.sum(scaled, axis=-1, keepdims=True) / D
    second = jnp.sum(scaled * centred, axis=-1, keepdims=True) / D
    return inverse * (scaled - first - centred * second)


def stacked(refs, rows=slice(None)):
    return jnp.concatenate([r[rows, :] for r in refs], axis=0)


def halves_kernel(keep_ref, got_ref, keep, send):
    half = keep_ref.shape[0] // 2
    keep[...] = keep_ref[:half, :] + got_ref[:half, :].astype(f32)
    send[...] = (keep_ref[half:, :] + got_ref[half:, :].astype(f32)).astype(bf16)


def halves_out(value, keep, send):
    half = value.shape[0] // 2
    keep[...] = value[:half]
    send[...] = value[half:].astype(bf16)


def token_kernel(got, xg, vec):
    n_col, rows, width = got.shape
    two = xg.shape[0]
    for j in range(n_col):
        at = slice(j * width, (j + 1) * width)
        xg[:, at] = got[j, :two, :]
        v = got[j, two:, :].astype(f32)
        vec[:, at] = v[:8] + v[8:16] + v[16:24]


def qkv_kernel(heads, tokens, n_row, n_col, scal, *refs):
    xgs, (vec, shifts, own_qkv, own_out), refs = refs[:n_row], refs[n_row : n_row + 4], refs[n_row + 4 :]
    near, far, (cut, a1_out, w_all, w_out) = refs[: n_col - 1], refs[n_col - 1 : 2 * n_col - 2], refs[2 * n_col - 2 :]
    c, d = scal[1], scal[2]
    rows, width3 = own_qkv.shape
    half = rows // 2
    w_all[pl.ds(pl.multiple_of(c * rows, 64), rows), :] = own_qkv[...]
    w_out[c] = own_out[...]
    for k in range(1, n_col):
        for part, ref in ((d, near[k - 1]), (1 - d, far[k - 1])):
            w_all[pl.ds(pl.multiple_of(((c ^ k) * 2 + part) * half, 32), half), :] = ref[:, :width3]
            w_out[c ^ k, pl.ds(pl.multiple_of(part * half, 32), half), :] = ref[:, width3:]
    x = stacked(xgs, slice(0, tokens // n_row))
    centred, _ = norm_stats(x.astype(f32))
    a1 = (centred * vec[0:1, :] + vec[1:2, :]).astype(bf16)
    a1_out[...] = a1
    qkv = (dot_nn(a1, w_all[...]) + shifts[...]).astype(bf16)
    width = heads * HEAD
    for h in range(n_col):
        if h < heads:
            lo = h * HEAD
            piece = jnp.concatenate([qkv[:, j * width + lo : j * width + lo + HEAD] for j in range(3)], axis=1)
            cut[h] = beside(piece, tokens // n_row)
        else:
            cut[h] = jnp.zeros((tokens // 2, 6 * HEAD), bf16)


def out_kernel(heads, chunk, o, w, att_out, keep, send):
    att = jnp.concatenate([under(o[h], chunk) for h in range(heads)], axis=1)
    att_out[...] = att
    w_all = jnp.concatenate([w[j] for j in range(w.shape[0])], axis=1)
    halves_out(dot_nn(att, w_all), keep, send)


def norm2_kernel(keep, got, xg, vec, resid_out, a2_out):
    own = keep.shape[0]
    resid = xg[:own, :].astype(f32) + (keep[...] + got[...].astype(f32)) + vec[4:5, :]
    resid_out[...] = resid
    centred, _ = norm_stats(resid)
    a2_out[...] = (centred * vec[2:3, :] + vec[3:4, :]).astype(bf16)


def mlp_kernel(n_row, n_col, scal, *refs):
    a2s, gs, refs = refs[:n_row], refs[n_row : 2 * n_row], refs[2 * n_row :]
    up_bias, up_own, down_own = refs[:3]
    near, far = refs[3 : 2 + n_col], refs[2 + n_col : 1 + 2 * n_col]
    act_out, d_pre_out, bias_sum, a_keep, a_send, y_keep, y_send, wu, wd = refs[1 + 2 * n_col :]
    c, d = scal[1], scal[2]
    rows, width = up_own.shape
    half = width // 2
    mine = pl.ds(pl.multiple_of(d * half, 128), half)
    other = pl.ds(pl.multiple_of((1 - d) * half, 128), half)
    here = pl.ds(pl.multiple_of(c * rows, 64), rows)
    for w, own in ((wu, up_own), (wd, down_own)):
        w[here, :half] = own[:, mine]
        w[here, half:] = own[:, other]
    for k in range(1, n_col):
        there = pl.ds(pl.multiple_of((c ^ k) * rows, 64), rows)
        wu[there, :half] = near[k - 1][:rows, :]
        wd[there, :half] = near[k - 1][rows:, :]
        wu[there, half:] = far[k - 1][:rows, :]
        wd[there, half:] = far[k - 1][rows:, :]
    own = a2s[0].shape[0]
    shift = jnp.concatenate([up_bias[:, mine], up_bias[:, other]], axis=1)
    pre = dot_nn(stacked(a2s), wu[...]) + shift
    square = pre * pre
    t = jnp.tanh(C0 * (pre + C1 * (square * pre)))
    act = (0.5 * pre * (1.0 + t)).astype(bf16)
    slope = 0.5 * (1.0 + t) + (0.5 * C0) * pre * (1.0 - t * t) * (1.0 + (3.0 * C1) * square)
    d_act = dot_nn(stacked(gs, slice(own, 2 * own)), wd[...])
    d_pre = (d_act * slope).astype(bf16)
    act_out[...] = act
    d_pre_out[...] = d_pre
    total = jnp.sum(d_pre.astype(f32), axis=0, keepdims=True)
    bias_sum[:, mine] = total[:, :half]
    bias_sum[:, other] = total[:, half:]
    halves_out(dot_nt(d_pre, wu[...]), a_keep, a_send)
    halves_out(dot_nt(act, wd[...]), y_keep, y_send)


def mlp_grad_kernel(n_row, n_col, *refs):
    a2s, gs, refs = refs[:n_row], refs[n_row : 2 * n_row], refs[2 * n_row :]
    act, d_pre, mine, other = refs
    half = act.shape[1] // 2
    own = a2s[0].shape[0]
    a2, g = stacked(a2s), stacked(gs, slice(own, 2 * own))
    rows = a2.shape[1] // n_col
    for value, right, at in ((a2, d_pre, 0), (g, act, rows)):
        grad = dot_tn(value, right[...]).astype(bf16)
        for j in range(n_col):
            to = slice(2 * j * rows + at, 2 * j * rows + at + rows)
            mine[to, :] = grad[j * rows : (j + 1) * rows, :half]
            other[to, :] = grad[j * rows : (j + 1) * rows, half:]


def norm2_back_kernel(keep, got, xg, vec, resid_ref, gp_out, d_resid_out, sums):
    own = keep.shape[0]
    d_a2 = keep[...] + got[...].astype(f32)
    centred, inverse = norm_stats(resid_ref[...])
    g = xg[own:, :].astype(f32)
    d_resid = g + norm_back(d_a2, centred, inverse, vec[2:3, :])
    gp = d_resid.astype(bf16)
    d_resid_out[...] = d_resid
    gp_out[...] = gp
    for i, v in enumerate((d_a2 * centred, d_a2, gp.astype(f32), g)):
        sums[i : i + 1, :] = jnp.sum(v, axis=0, keepdims=True)


def d_att_kernel(n_row, heads, scal, *refs):
    gps, (att, w, cut, mine, other, full) = refs[:n_row], refs[n_row:]
    d = scal[2]
    gp = stacked(gps)
    n_col, rows, width = w.shape
    w_all = jnp.concatenate([w[j] for j in range(n_col)], axis=1)
    d_att = dot_nt(gp, w_all).astype(bf16)
    for h in range(n_col):
        if h < heads:
            cut[h] = beside(d_att[:, h * HEAD : (h + 1) * HEAD], gps[0].shape[0])
        else:
            cut[h] = jnp.zeros((gp.shape[0] // 2, 2 * HEAD), bf16)
    full[...] = dot_tn(att[...], gp).astype(bf16)
    half = rows // 2
    for to, part in ((mine, d), (other, 1 - d)):
        piece = full[pl.ds(pl.multiple_of(part * half, 32), half), :]
        for j in range(n_col):
            to[j * (half // 2) : (j + 1) * (half // 2), :] = beside(piece[:, j * width : (j + 1) * width], half)


def d_a1_kernel(n_row, heads, scal, *refs):
    xgs, (ds, a1, w), refs = refs[:n_row], refs[n_row : n_row + 3], refs[n_row + 3 :]
    keep, send, sums, mine, other, full = refs
    d = scal[2]
    tokens = a1.shape[0]
    pieces = [under(ds[h], tokens // n_row) for h in range(heads)]
    d_qkv = jnp.concatenate([p[:, j * HEAD : (j + 1) * HEAD] for j in range(3) for p in pieces], axis=1)
    part = dot_nt(d_qkv, w[...])
    halves_out(part, keep, send)
    full[...] = dot_tn(a1[...], d_qkv).astype(bf16)
    n_col = ds.shape[0]
    half = full.shape[0] // (2 * n_col)
    for j in range(n_col):
        at = slice(j * half, (j + 1) * half)
        mine[at, :] = full[pl.ds(pl.multiple_of((2 * j + d) * half, 32), half), :]
        other[at, :] = full[pl.ds(pl.multiple_of((2 * j + 1 - d) * half, 32), half), :]
    centred, _ = norm_stats(stacked(xgs, slice(0, tokens // n_row)).astype(f32))
    sums[...] = jnp.zeros_like(sums)
    sums[0:1, :] = jnp.sum(part * centred, axis=0, keepdims=True)
    sums[1:2, :] = jnp.sum(part, axis=0, keepdims=True)
    sums[2:3, : d_qkv.shape[1]] = jnp.sum(d_qkv.astype(f32), axis=0, keepdims=True)


def final_kernel(a_keep, a_got, y_keep, y_got, xg, vec, resid, d_resid, out):
    n_col, rows, width = out.shape
    own = rows // 2
    d_a1 = a_keep[...] + a_got[...].astype(f32)
    centred, inverse = norm_stats(xg[:own, :].astype(f32))
    d_x = (d_resid[...] + norm_back(d_a1, centred, inverse, vec[0:1, :])).astype(bf16)
    y = (resid[...] + (y_keep[...] + y_got[...].astype(f32)) + vec[5:6, :]).astype(bf16)
    for j in range(n_col):
        out[j, :own, :] = d_x[:, j * width : (j + 1) * width]
        out[j, own:, :] = y[:, j * width : (j + 1) * width]


def part_kernel(n_in, scal, *refs):
    mine, got, outs = refs[:n_in], refs[n_in : 2 * n_in], refs[2 * n_in :]
    n_col = len(outs)
    at = 0
    for m, g in zip(mine, got):
        rows = m.shape[0] // n_col
        for k in range(n_col):
            there = pl.ds(pl.multiple_of((scal[1] ^ k) * rows, 16), rows)
            total = m[there, :].astype(f32) + g[there, :].astype(f32)
            outs[k][at : at + rows, :] = total.astype(outs[k].dtype)
        at += rows


def add_kernel(*refs):
    total = refs[0][...].astype(f32)
    for r in refs[1:-1]:
        total = total + r[...].astype(f32)
    refs[-1][...] = total.astype(refs[-1].dtype)


def mlp_out_kernel(scal, part, away, up, down, out):
    d = scal[2]
    rows, width = up.shape
    half = width // 2
    for ref, index in ((part, d), (away, 1 - d)):
        lanes = pl.ds(pl.multiple_of(index * half, 128), half)
        up[:, lanes] = ref[:rows, :].astype(f32)
        down[:, lanes] = ref[rows : 2 * rows, :].astype(f32)
        piece = under(ref[2 * rows :, :].astype(f32), rows // 2)
        out[pl.ds(pl.multiple_of(index * (rows // 2), 32), rows // 2), :] = piece


def qkv_out_kernel(scal, part, away, out):
    half = part.shape[0]
    out[pl.ds(pl.multiple_of(scal[2] * half, 32), half), :] = part[...].astype(f32)
    out[pl.ds(pl.multiple_of((1 - scal[2]) * half, 32), half), :] = away[...].astype(f32)


def sum_parts(pairs, scal):
    n_col = lax.axis_size("col")
    mine = [m for m, _ in pairs]
    got = [swap(o, "dp", 1) for _, o in pairs]
    rows = sum(m.shape[0] for m in mine) // n_col
    width = mine[0].shape[1]
    parts = call(
        functools.partial(part_kernel, len(mine)),
        [((rows, width), f32)] + [((rows, width), bf16)] * (n_col - 1),
        scal,
        [*mine, *got],
    )
    got = [swap(parts[k], "col", k) for k in range(1, n_col)]
    total = call(add_kernel, [((rows, width), bf16)], None, [parts[0], *got])[0]
    for b in bits_of("dp", 2):
        total = call(add_kernel, [((rows, width), bf16)], None, [total, swap(total, "dp", b)])[0]
    return total, swap(total, "dp", 1)


def body(
    block_input,
    ln1_gain,
    ln1_bias,
    qkv_weight,
    qv_bias,
    out_weight,
    out_bias,
    ln2_gain,
    ln2_bias,
    up_weight,
    up_bias,
    down_weight,
    down_bias,
    out_grad,
):
    n_col = lax.axis_size("col")
    n_row = lax.axis_size("row")
    width_in = D // n_col
    width_out = D // n_row
    heads = width_out // HEAD
    order = row_order()
    own = block_input.shape[0] // n_col
    tokens = own * n_row
    half_ff = up_weight.shape[1] // 2
    ff = 2 * half_ff
    cols = range(1, n_col)
    c = lax.axis_index("col").astype(jnp.int32)
    d = lax.axis_index("dp").astype(jnp.int32) & 1
    scal = jnp.stack([lax.axis_index("row").astype(jnp.int32), c, d])
    token_sum = [((tokens // 2, D), f32), ((tokens // 2, D), bf16)]

    zero = jnp.zeros_like(ln1_gain)
    vectors = three_parts(jnp.stack([ln1_gain, ln1_bias, ln2_gain, ln2_bias, out_bias, down_bias, zero, zero]))
    message = jnp.concatenate(
        [
            block_input.reshape(n_col, own, width_in),
            out_grad.reshape(n_col, own, width_in),
            jnp.broadcast_to(jnp.pad(vectors, ((0, 8), (0, 0)))[None], (n_col, 32, width_in)),
        ],
        axis=1,
    )
    got = turn(message.reshape(-1, width_in)).reshape(message.shape)
    xg_own, vec = call(token_kernel, [((2 * own, D), bf16), ((8, D), f32)], None, [got])

    own_qkv = qkv_weight.reshape(width_in, 3 * width_out)
    own_out = out_weight.reshape(width_out, width_in)
    both = jnp.concatenate([own_qkv, own_out], axis=1)
    half_a = lax.dynamic_slice_in_dim(both, d * (width_in // 2), width_in // 2, 0)
    near_a = [swap(half_a, "col", k) for k in cols]
    near_a, up_w, down_w = lax.optimization_barrier((near_a, up_weight, down_weight))
    far_a = [swap(v, "dp", 1) for v in near_a]
    half_m = jnp.concatenate(
        [lax.dynamic_slice_in_dim(w, d * half_ff, half_ff, 1) for w in (up_w, down_w)], axis=0
    )
    near_m = [swap(half_m, "col", k) for k in cols]
    far_m = [swap(v, "dp", 1) for v in near_m]

    xg = gather_row(xg_own)
    shifts = jnp.concatenate([qv_bias[0], jnp.zeros_like(qv_bias[0]), qv_bias[1]])[None]
    qkv_cut, a1, w_qkv, w_out = call(
        functools.partial(qkv_kernel, heads, tokens, n_row, n_col),
        [
            ((n_col, tokens // 2, 6 * HEAD), bf16),
            ((tokens, D), bf16),
            ((D, 3 * width_out), bf16),
            ((n_col, width_out, width_in), bf16),
        ],
        scal,
        [*xg, vec, shifts, own_qkv, own_out, *near_a, *far_a],
    )
    qkv_head = turn(qkv_cut)
    att_head = call(
        functools.partial(forward_kernel, order),
        [((n_col, tokens // 2, 2 * HEAD), bf16)],
        scal,
        [qkv_head],
        [((tokens * n_col, 3 * HEAD), bf16), ((tokens * n_col, HEAD), bf16)],
    )[0]
    attended, o_keep, o_send = call(
        functools.partial(out_kernel, heads, own),
        [((tokens, width_out), bf16)] + token_sum,
        None,
        [turn(att_head), w_out],
    )
    resid1, a2_own = call(
        norm2_kernel, [((own, D), f32), ((own, D), bf16)], None, [*finish_row(o_keep, o_send), xg_own, vec]
    )
    a2 = gather_row(a2_own)
    act, d_pre, up_sum, a_keep, a_send, y_keep, y_send = call(
        functools.partial(mlp_kernel, n_row, n_col),
        [((tokens, ff), bf16), ((tokens, ff), bf16), ((1, ff), f32)] + token_sum + token_sum,
        scal,
        [*a2, *xg, up_bias[None], up_weight, down_weight, *near_m, *far_m],
        [((D, ff), bf16), ((D, ff), bf16)],
    )
    gp, d_resid1, sums2 = call(
        norm2_back_kernel,
        [((own, D), bf16), ((own, D), f32), ((4, D), f32)],
        None,
        [*finish_row(a_keep, a_send), xg_own, vec, resid1],
    )
    gp_all = gather_row(gp)
    mlp_mine, mlp_other = call(
        functools.partial(mlp_grad_kernel, n_row, n_col),
        [((2 * D, half_ff), bf16)] * 2,
        None,
        [*a2, *xg, act, d_pre],
    )
    d_att_cut, out_mine, out_other = call(
        functools.partial(d_att_kernel, n_row, heads),
        [((n_col, tokens // 2, 2 * HEAD), bf16)] + [((n_col * width_out // 4, 2 * width_in), bf16)] * 2,
        scal,
        [*gp_all, attended, w_out],
        [((width_out, D), bf16)],
    )
    d_qkv_head = call(
        functools.partial(backward_kernel, order),
        [((n_col, tokens // 2, 6 * HEAD), bf16)],
        scal,
        [qkv_head, turn(d_att_cut)],
        [
            ((tokens * n_col, 3 * HEAD), bf16),
            ((tokens * n_col, HEAD), bf16),
            ((tokens * n_col, 3 * HEAD), bf16),
            ((HEAD, tokens * n_col), f32),
            ((HEAD, tokens * n_col), f32),
        ],
    )[0]
    d_keep, d_send, sums1, qkv_mine, qkv_other = call(
        functools.partial(d_a1_kernel, n_row, heads),
        token_sum + [((3, D), f32)] + [((D // 2, 3 * width_out), bf16)] * 2,
        scal,
        [*xg, turn(d_qkv_head), a1, w_qkv],
        [((D, 3 * width_out), bf16)],
    )

    d_up, d_down, d_out = call(
        mlp_out_kernel,
        [((width_in, ff), f32), ((width_in, ff), f32), ((width_out, width_in), f32)],
        scal,
        sum_parts([(mlp_mine, mlp_other), (out_mine, out_other)], scal),
    )
    d_qkv = call(qkv_out_kernel, [((width_in, 3 * width_out), f32)], scal, sum_parts([(qkv_mine, qkv_other)], scal))[0]

    outs = call(
        final_kernel,
        [((n_col, 2 * own, width_in), bf16)],
        None,
        [*finish_row(d_keep, d_send), *finish_row(y_keep, y_send), xg_own, vec, resid1, d_resid1],
    )[0]
    outs = turn(outs)
    input_grad = outs[:, :own].reshape(-1, width_in)
    block_output = outs[:, own:].reshape(-1, width_in)

    sums = jnp.concatenate([sums1[:2], sums2, up_sum.reshape(-1, D), sums1[2:]])
    for axis in ("col", "dp"):
        for b in bits_of(axis):
            sums = sums + swap(sums, axis, b)
    feats = sums[:6]
    for b in bits_of("row"):
        feats = feats + swap(feats, "row", b)
    feats = lax.dynamic_slice_in_dim(feats, c * width_in, width_in, 1)
    d_qv_bias = jnp.stack([sums[-1, :width_out], sums[-1, 2 * width_out : 3 * width_out]])

    return (
        block_output,
        input_grad,
        feats[0],
        feats[1],
        d_qkv.reshape(1, 1, -1),
        d_qv_bias,
        d_out.reshape(1, 1, -1),
        feats[4],
        feats[2],
        feats[3],
        d_up,
        sums[6:-1].reshape(ff),
        d_down,
        feats[5],
    )


def solution(mesh):
    in_specs = (
        P(("dp", "row"), "col"),
        P("col"),
        P("col"),
        P("col", "row", None),
        P(None, "row"),
        P("row", "col", None),
        P("col"),
        P("col"),
        P("col"),
        P("col", "row"),
        P("row"),
        P("col", "row"),
        P("col"),
        P(("dp", "row"), "col"),
    )
    out_specs = (
        P(("dp", "row"), "col"),
        P(("dp", "row"), "col"),
        P("col"),
        P("col"),
        P("col", "row", None),
        P(None, "row"),
        P("row", "col", None),
        P("col"),
        P("col"),
        P("col"),
        P("col", "row"),
        P("row"),
        P("col", "row"),
        P("col"),
    )
    return jax.shard_map(body, mesh=mesh, in_specs=in_specs, out_specs=out_specs, check_vma=False)
```

```python
import functools
import math

import jax
import jax.numpy as jnp
from jax import lax
from jax.experimental import pallas as pl
from jax.experimental.pallas import tpu as pltpu
from jax.sharding import PartitionSpec as P

D = 768
HEAD = 64
SCALE = 1.0 / math.sqrt(HEAD)
C0 = math.sqrt(2.0 / math.pi)
C1 = 0.044715
bf16 = jnp.bfloat16
f32 = jnp.float32
VMEM = pl.BlockSpec(memory_space=pltpu.VMEM)
SMEM = pl.BlockSpec(memory_space=pltpu.SMEM)


def dot_nn(a, b):
    return lax.dot_general(a, b, (((1,), (0,)), ((), ())), preferred_element_type=f32)


def dot_nt(a, b):
    return lax.dot_general(a, b, (((1,), (1,)), ((), ())), preferred_element_type=f32)


def dot_tn(a, b):
    return lax.dot_general(a, b, (((0,), (0,)), ((), ())), preferred_element_type=f32)


def call(kernel, outs, scalars, args, scratch=(), limit=20):
    first = [] if scalars is None else [scalars]
    return pl.pallas_call(
        kernel,
        out_shape=[jax.ShapeDtypeStruct(s, t) for s, t in outs],
        in_specs=[SMEM] * len(first) + [VMEM] * len(args),
        out_specs=[VMEM] * len(outs),
        scratch_shapes=[pltpu.VMEM(s, t) for s, t in scratch],
        compiler_params=pltpu.CompilerParams(vmem_limit_bytes=limit * 1024 * 1024),
        cost_estimate=pl.CostEstimate(flops=1, bytes_accessed=1, transcendentals=0),
    )(*first, *args)


def swap(value, axis, bit):
    n = lax.axis_size(axis)
    return lax.ppermute(value, axis, [(i, i ^ bit) for i in range(n)])


def turn(value, split=0, concat=0):
    return lax.all_to_all(value, "col", split, concat, tiled=True)


def bits_of(axis, first=1):
    n = lax.axis_size(axis)
    bits = []
    b = first
    while b < n:
        bits.append(b)
        b *= 2
    return bits


def row_order():
    order = [0]
    for b in reversed(bits_of("row")):
        order = order + [o ^ b for o in order]
    return order


def gather_row(value):
    pieces = [value]
    for b in reversed(bits_of("row")):
        pieces = pieces + [swap(p, "row", b) for p in pieces]
    return pieces


def gather_col(value):
    pieces = {0: value}
    for b in reversed(bits_of("col")):
        for k in list(pieces):
            pieces[k ^ b] = swap(pieces[k], "col", b)
    return [pieces[k] for k in range(lax.axis_size("col"))]


def finish_row(keep, send):
    bits = bits_of("row")
    for b in bits[:-1]:
        keep, send = add_halves(keep, swap(send, "row", b))
    return keep, swap(send, "row", bits[-1])


def add_halves(keep, got):
    rows, width = keep.shape
    return call(halves_kernel, [((rows // 2, width), f32), ((rows // 2, width), bf16)], None, [keep, got])


def after(value, *others):
    return lax.optimization_barrier((value, others))[0]


def place(scal, order, col, kk, chunk, n_col, second):
    half = chunk // 2
    at = ((scal[0] ^ order[kk]) * n_col + col) * chunk + second * half
    return pl.ds(pl.multiple_of(at, half), half)


def load_natural(scal, order, src, dst):
    n_col, rows, width = src.shape
    half = rows // len(order)
    for col in range(n_col):
        for kk in range(len(order)):
            both = src[col, kk * half : (kk + 1) * half, :]
            for second in range(2):
                at = place(scal, order, col, kk, 2 * half, n_col, second)
                dst[at, :] = both[:, second * (width // 2) : (second + 1) * (width // 2)]


def store_natural(scal, order, src, dst):
    n_col, rows, _ = dst.shape
    half = rows // len(order)
    for col in range(n_col):
        for kk in range(len(order)):
            both = [src[place(scal, order, col, kk, 2 * half, n_col, second), :] for second in range(2)]
            dst[col, kk * half : (kk + 1) * half, :] = jnp.concatenate(both, axis=1)


def beside(value, chunk):
    half = chunk // 2
    starts = range(0, value.shape[0], chunk)
    first = jnp.concatenate([value[i : i + half] for i in starts], axis=0)
    second = jnp.concatenate([value[i + half : i + chunk] for i in starts], axis=0)
    return jnp.concatenate([first, second], axis=1)


def under(value, chunk):
    half = chunk // 2
    width = value.shape[1] // 2
    parts = []
    for i in range(0, value.shape[0], half):
        parts += [value[i : i + half, :width], value[i : i + half, width:]]
    return jnp.concatenate(parts, axis=0)


def block_probs(q, k, block, i):
    scores = dot_nt(q, k) * SCALE
    rows = lax.broadcasted_iota(jnp.int32, scores.shape, 0) + i * block
    cols = lax.broadcasted_iota(jnp.int32, scores.shape, 1)
    scores = jnp.where(cols <= rows, scores, -1e30)
    top = jnp.max(scores, axis=-1, keepdims=True)
    e = jnp.exp(scores - top)
    return e / jnp.sum(e, axis=-1, keepdims=True)


def forward_kernel(order, scal, qkv_ref, out_ref, nat, res):
    load_natural(scal, order, qkv_ref, nat)
    block = nat.shape[0] // len(order)
    k = nat[:, HEAD : 2 * HEAD]
    v = nat[:, 2 * HEAD :]
    for i in range(len(order)):
        upto = (i + 1) * block
        p = block_probs(nat[i * block : upto, :HEAD], k[:upto], block, i)
        res[i * block : upto, :] = dot_nn(p.astype(bf16), v[:upto]).astype(bf16)
    store_natural(scal, order, res, out_ref)


def backward_kernel(order, scal, qkv_ref, do_ref, out_ref, nat, dnat, res, dkt, dvt):
    load_natural(scal, order, qkv_ref, nat)
    load_natural(scal, order, do_ref, dnat)
    block = nat.shape[0] // len(order)
    k = nat[:, HEAD : 2 * HEAD]
    v = nat[:, 2 * HEAD :]
    dkt[...] = jnp.zeros_like(dkt)
    dvt[...] = jnp.zeros_like(dvt)
    for i in range(len(order)):
        upto = (i + 1) * block
        q = nat[i * block : upto, :HEAD]
        do = dnat[i * block : upto, :]
        p = block_probs(q, k[:upto], block, i)
        dvt[:, :upto] += dot_tn(do, p.astype(bf16))
        dp = dot_nt(do, v[:upto])
        ds = (p * (dp - jnp.sum(dp * p, axis=-1, keepdims=True))).astype(bf16)
        res[i * block : upto, :HEAD] = (dot_nn(ds, k[:upto]) * SCALE).astype(bf16)
        dkt[:, :upto] += dot_tn(q, ds)
    res[:, HEAD : 2 * HEAD] = (dkt[...].T * SCALE).astype(bf16)
    res[:, 2 * HEAD :] = dvt[...].T.astype(bf16)
    store_natural(scal, order, res, out_ref)


def norm_stats(v):
    mean = jnp.sum(v, axis=-1, keepdims=True) / D
    var = jnp.sum(v * v, axis=-1, keepdims=True) / D - mean * mean
    inverse = lax.rsqrt(var + 1e-05)
    return (v - mean) * inverse, inverse


def norm_back(grad, centred, inverse, gain):
    scaled = grad * gain
    first = jnp.sum(scaled, axis=-1, keepdims=True) / D
    second = jnp.sum(scaled * centred, axis=-1, keepdims=True) / D
    return inverse * (scaled - first - centred * second)


def stacked(refs, rows=slice(None)):
    return jnp.concatenate([r[rows, :] for r in refs], axis=0)


def halves_kernel(keep_ref, got_ref, keep, send):
    half = keep_ref.shape[0] // 2
    keep[...] = keep_ref[:half, :] + got_ref[:half, :].astype(f32)
    send[...] = (keep_ref[half:, :] + got_ref[half:, :].astype(f32)).astype(bf16)


def halves_out(value, keep, send, at=0):
    half, width = value.shape[0] // 2, value.shape[1]
    keep[:, at : at + width] = value[:half]
    send[:, at : at + width] = value[half:].astype(bf16)


def message_kernel(own, x, g, *refs):
    vectors, out = refs[:-1], refs[-1]
    n_col = out.shape[0]
    x_all = x[...].astype(f32).T.astype(bf16)
    g_all = g[...].astype(f32).T.astype(bf16)
    width = x_all.shape[1]
    rest = jnp.concatenate([v[...] for v in vectors] + [jnp.zeros((8 - len(vectors), width), f32)], axis=0)
    parts = []
    for _ in range(3):
        part = rest.astype(bf16).astype(f32)
        parts.append(part)
        rest = rest - part
    parts.append(jnp.zeros((8, width), f32))
    parts = jnp.concatenate(parts, axis=0).astype(bf16)
    parts = beside(parts, parts.shape[0])
    half = own // 2
    for j in range(n_col):
        out[j, :half, :] = beside(x_all[j * own : (j + 1) * own], own)
        out[j, half:own, :] = beside(g_all[j * own : (j + 1) * own], own)
        out[j, own:, :] = parts


def prep_kernel(scal, qkv, out, half_a):
    half, width3 = half_a.shape[0], qkv.shape[1]
    rows = pl.ds(pl.multiple_of(scal[2] * half, 32), half)
    half_a[:, :width3] = qkv[rows, :]
    half_a[:, width3:] = out[rows, :]


def prep_mlp_kernel(scal, up, down, half_m):
    tall, half_ff = up.shape[0], half_m.shape[1]
    lanes = pl.ds(pl.multiple_of(scal[2] * half_ff, 128), half_ff)
    half_m[:tall, :] = up[:, lanes]
    half_m[tall:, :] = down[:, lanes]


def token_kernel(got, xg, vec):
    n_col, rows, width = got.shape
    width = width // 2
    own = xg.shape[0] // 2
    for j in range(n_col):
        at = slice(j * width, (j + 1) * width)
        xg[:, at] = under(got[j, :own, :], own)
        v = under(got[j, own:, :].astype(f32), 2 * (rows - own))
        vec[:, at] = v[:8] + v[8:16] + v[16:24]


def qkv_kernel(heads, tokens, n_row, n_col, scal, *refs):
    xgs, (vec, qv_bias, own_qkv, own_out), refs = refs[:n_row], refs[n_row : n_row + 4], refs[n_row + 4 :]
    near, far, (cut, a1_out, w_all, w_out) = refs[: n_col - 1], refs[n_col - 1 : 2 * n_col - 2], refs[2 * n_col - 2 :]
    c, d = scal[1], scal[2]
    rows, width3 = own_qkv.shape
    half = rows // 2
    w_all[pl.ds(pl.multiple_of(c * rows, 64), rows), :] = own_qkv[...]
    w_out[c] = own_out[...]
    for k in range(1, n_col):
        for part, ref in ((d, near[k - 1]), (1 - d, far[k - 1])):
            w_all[pl.ds(pl.multiple_of(((c ^ k) * 2 + part) * half, 32), half), :] = ref[:, :width3]
            w_out[c ^ k, pl.ds(pl.multiple_of(part * half, 32), half), :] = ref[:, width3:]
    x = stacked(xgs, slice(0, tokens // n_row))
    centred, _ = norm_stats(x.astype(f32))
    a1 = (centred * vec[0:1, :] + vec[1:2, :]).astype(bf16)
    a1_out[...] = a1
    width = heads * HEAD
    shifts = jnp.concatenate([qv_bias[0:1, :], jnp.zeros((1, width), f32), qv_bias[1:2, :]], axis=1)
    qkv = (dot_nn(a1, w_all[...]) + shifts).astype(bf16)
    for h in range(n_col):
        if h < heads:
            lo = h * HEAD
            piece = jnp.concatenate([qkv[:, j * width + lo : j * width + lo + HEAD] for j in range(3)], axis=1)
            cut[h] = beside(piece, tokens // n_row)
        else:
            cut[h] = jnp.zeros((tokens // 2, 6 * HEAD), bf16)


def out_kernel(heads, chunk, o, w, att_out, keep, send):
    att = jnp.concatenate([under(o[h], chunk) for h in range(heads)], axis=1)
    att_out[...] = att
    w_all = jnp.concatenate([w[j] for j in range(w.shape[0])], axis=1)
    halves_out(dot_nn(att, w_all), keep, send)


def norm2_kernel(keep, got, xg, vec, resid_out, a2_out):
    own = keep.shape[0]
    resid = xg[:own, :].astype(f32) + (keep[...] + got[...].astype(f32)) + vec[4:5, :]
    resid_out[...] = resid
    centred, _ = norm_stats(resid)
    a2_out[...] = (centred * vec[2:3, :] + vec[3:4, :]).astype(bf16)


def mlp_kernel(n_row, n_col, scal, *refs):
    a2s, gs, refs = refs[:n_row], refs[n_row : 2 * n_row], refs[2 * n_row :]
    up_bias, up_own, down_own = refs[:3]
    near, far = refs[3 : 2 + n_col], refs[2 + n_col : 1 + 2 * n_col]
    act_out, d_pre_out, bias_sum, keep, send, wu, wd = refs[1 + 2 * n_col :]
    c, d = scal[1], scal[2]
    rows, width = up_own.shape
    half = width // 2
    mine = pl.ds(pl.multiple_of(d * half, 128), half)
    other = pl.ds(pl.multiple_of((1 - d) * half, 128), half)
    here = pl.ds(pl.multiple_of(c * rows, 64), rows)
    for w, own in ((wu, up_own), (wd, down_own)):
        w[here, :half] = own[:, mine]
        w[here, half:] = own[:, other]
    for k in range(1, n_col):
        there = pl.ds(pl.multiple_of((c ^ k) * rows, 64), rows)
        wu[there, :half] = near[k - 1][:rows, :]
        wd[there, :half] = near[k - 1][rows:, :]
        wu[there, half:] = far[k - 1][:rows, :]
        wd[there, half:] = far[k - 1][rows:, :]
    own = a2s[0].shape[0]
    shift = jnp.concatenate([up_bias[:, mine], up_bias[:, other]], axis=1)
    pre = dot_nn(stacked(a2s), wu[...]) + shift
    square = pre * pre
    t = jnp.tanh(C0 * (pre + C1 * (square * pre)))
    act = (0.5 * pre * (1.0 + t)).astype(bf16)
    slope = 0.5 * (1.0 + t) + (0.5 * C0) * pre * (1.0 - t * t) * (1.0 + (3.0 * C1) * square)
    d_act = dot_nn(stacked(gs, slice(own, 2 * own)), wd[...])
    d_pre = (d_act * slope).astype(bf16)
    act_out[...] = act
    d_pre_out[...] = d_pre
    total = jnp.sum(d_pre.astype(f32), axis=0, keepdims=True)
    bias_sum[:, mine] = total[:, :half]
    bias_sum[:, other] = total[:, half:]
    halves_out(dot_nt(d_pre, wu[...]), keep, send)
    halves_out(dot_nt(act, wd[...]), keep, send, D)


def mlp_grad_kernel(n_row, *refs):
    a2s, gs, refs = refs[:n_row], refs[n_row : 2 * n_row], refs[2 * n_row :]
    act, d_pre, up_mine, up_other, down_mine, down_other = refs
    half = act.shape[1] // 2
    own = a2s[0].shape[0]
    a2, g = stacked(a2s), stacked(gs, slice(own, 2 * own))
    up_mine[...] = dot_tn(a2, d_pre[:, :half]).astype(bf16)
    up_other[...] = dot_tn(a2, d_pre[:, half:]).astype(bf16)
    down_mine[...] = dot_tn(g, act[:, :half]).astype(bf16)
    down_other[...] = dot_tn(g, act[:, half:]).astype(bf16)


def norm2_back_kernel(keep, got, xg, vec, resid_ref, gp_out, d_resid_out, sums):
    own = keep.shape[0]
    d_a2 = keep[:, :D] + got[:, :D].astype(f32)
    centred, inverse = norm_stats(resid_ref[...])
    g = xg[own:, :].astype(f32)
    d_resid = g + norm_back(d_a2, centred, inverse, vec[2:3, :])
    gp = d_resid.astype(bf16)
    d_resid_out[...] = d_resid
    gp_out[...] = gp
    for i, v in enumerate((d_a2 * centred, d_a2, gp.astype(f32), g)):
        sums[i : i + 1, :] = jnp.sum(v, axis=0, keepdims=True)


def d_att_kernel(n_row, heads, scal, *refs):
    gps, (att, w, cut, mine, other, full) = refs[:n_row], refs[n_row:]
    d = scal[2]
    gp = stacked(gps)
    n_col, rows, width = w.shape
    w_all = jnp.concatenate([w[j] for j in range(n_col)], axis=1)
    d_att = dot_nt(gp, w_all).astype(bf16)
    for h in range(n_col):
        if h < heads:
            cut[h] = beside(d_att[:, h * HEAD : (h + 1) * HEAD], gps[0].shape[0])
        else:
            cut[h] = jnp.zeros((gp.shape[0] // 2, 2 * HEAD), bf16)
    full[...] = dot_tn(att[...], gp).astype(bf16)
    half = rows // 2
    for to, part in ((mine, d), (other, 1 - d)):
        piece = full[pl.ds(pl.multiple_of(part * half, 32), half), :]
        for j in range(n_col):
            to[j * (half // 2) : (j + 1) * (half // 2), :] = beside(piece[:, j * width : (j + 1) * width], half)


def d_a1_kernel(n_row, heads, scal, *refs):
    xgs, (ds, a1, w), refs = refs[:n_row], refs[n_row : n_row + 3], refs[n_row + 3 :]
    sums2, up_sum, refs = refs[0], refs[1], refs[2:]
    keep, send, sums, mine, other, full = refs
    d = scal[2]
    tokens = a1.shape[0]
    pieces = [under(ds[h], tokens // n_row) for h in range(heads)]
    d_qkv = jnp.concatenate([p[:, j * HEAD : (j + 1) * HEAD] for j in range(3) for p in pieces], axis=1)
    part = dot_nt(d_qkv, w[...])
    halves_out(part, keep, send)
    full[...] = dot_tn(a1[...], d_qkv).astype(bf16)
    n_col = ds.shape[0]
    half = full.shape[0] // (2 * n_col)
    for j in range(n_col):
        at = slice(j * half, (j + 1) * half)
        mine[at, :] = full[pl.ds(pl.multiple_of((2 * j + d) * half, 32), half), :]
        other[at, :] = full[pl.ds(pl.multiple_of((2 * j + 1 - d) * half, 32), half), :]
    centred, _ = norm_stats(stacked(xgs, slice(0, tokens // n_row)).astype(f32))
    pad = jnp.zeros((1, D - d_qkv.shape[1]), f32)
    total = jnp.concatenate(
        [
            jnp.sum(part * centred, axis=0, keepdims=True),
            jnp.sum(part, axis=0, keepdims=True),
            sums2[...],
            up_sum[...],
            jnp.concatenate([jnp.sum(d_qkv.astype(f32), axis=0, keepdims=True), pad], axis=1),
        ],
        axis=0,
    )
    sums[...] = total
    other[n_col * half :, :] = pack_sums(total)


def final_kernel(d_keep, d_got, a_keep, a_got, xg, vec, resid, d_resid, out):
    n_col, width, rows = out.shape
    own = rows // 2
    d_a1 = d_keep[...] + d_got[...].astype(f32)
    centred, inverse = norm_stats(xg[:own, :].astype(f32))
    d_x = (d_resid[...] + norm_back(d_a1, centred, inverse, vec[0:1, :])).astype(bf16)
    y = (resid[...] + (a_keep[:, D:] + a_got[:, D:].astype(f32)) + vec[5:6, :]).astype(bf16)
    both = jnp.concatenate([d_x.astype(f32), y.astype(f32)], axis=0)
    for j in range(n_col):
        out[j] = both[:, j * width : (j + 1) * width].T.astype(bf16)


def part_kernel(n_in, order, scal, *refs):
    mine, got, (keep, send) = refs[:n_in], refs[n_in : 2 * n_in], refs[2 * n_in :]
    n_col = len(order)
    height = 2 * keep.shape[0] // n_col
    for i, k in enumerate(order):
        to, at = (keep, i) if i < n_col // 2 else (send, i - n_col // 2)
        at = at * height
        for m, g in zip(mine, got):
            rows = m.shape[0] // n_col
            there = pl.ds(pl.multiple_of((scal[1] ^ k) * rows, 16), rows)
            total = m[there, :].astype(f32) + g[there, :].astype(f32)
            to[at : at + rows, :] = total.astype(to.dtype)
            at += rows


def add_kernel(*refs):
    total = refs[0][...].astype(f32)
    for r in refs[1:-1]:
        total = total + r[...].astype(f32)
    refs[-1][...] = total.astype(refs[-1].dtype)


def pack_sums(v):
    parts = []
    for _ in range(3):
        part = v.astype(bf16).astype(f32)
        parts.append(part)
        v = v - part
    cut = 3 * v.shape[1] // 4
    rows = [p[:, :cut] for p in parts] + [jnp.concatenate([p[:, cut:] for p in parts], axis=1)]
    return jnp.concatenate(rows, axis=0).astype(bf16)


def unpack_sums(v):
    v = v.astype(f32)
    n = v.shape[0] // 4
    third = v.shape[1] // 3
    parts = [
        jnp.concatenate([v[i * n : (i + 1) * n], v[3 * n :, i * third : (i + 1) * third]], axis=1) for i in range(3)
    ]
    return parts[0] + parts[1] + parts[2]


def qkv_part_kernel(order, scal, mine, got, own_sums, keep, send, sums):
    n_col = len(order)
    rows = mine.shape[0] // n_col
    for i, k in enumerate(order):
        to, at = (keep, i) if i < n_col // 2 else (send, i - n_col // 2)
        there = pl.ds(pl.multiple_of((scal[1] ^ k) * rows, 16), rows)
        total = mine[there, :].astype(f32) + got[there, :].astype(f32)
        to[at * rows : (at + 1) * rows, :] = total.astype(to.dtype)
    total = own_sums[...] + unpack_sums(got[mine.shape[0] :, :])
    sums[...] = total
    send[keep.shape[0] :, :] = pack_sums(total)


def qkv_half_kernel(keep_ref, got_ref, sums_ref, keep, send, sums):
    rows = keep_ref.shape[0]
    half = rows // 2
    keep[...] = keep_ref[:half, :] + got_ref[:half, :].astype(f32)
    send[:half, :] = (keep_ref[half:, :] + got_ref[half:rows, :].astype(f32)).astype(bf16)
    total = sums_ref[...] + unpack_sums(got_ref[rows:, :])
    sums[...] = total
    send[half:, :] = pack_sums(total)


def qkv_add_kernel(keep_ref, got_ref, sums_ref, out, sums):
    rows = keep_ref.shape[0]
    out[...] = (keep_ref[...] + got_ref[:rows, :].astype(f32)).astype(bf16)
    sums[...] = sums_ref[...] + unpack_sums(got_ref[rows:, :])


def flat_store(value, cut, out):
    rows, width = value.shape
    lines = 2 * width // 128
    for i in range(cut.shape[0]):
        high = min(width, (i + 1) * 128)
        cut[i, :, : high - i * 128] = value[:, i * 128 : high]
    both = []
    for odd in range(2):
        pieces = [cut[i, pl.ds(odd, rows // 2, stride=2), :] for i in range(cut.shape[0])]
        both.append(jnp.concatenate(pieces, axis=1)[:, :width])
    both = jnp.concatenate(both, axis=1)
    for g in range(lines):
        out[pl.ds(g, rows // 2, stride=lines), :] = both[:, g * 128 : (g + 1) * 128]


def up_out_kernel(scal, part, away, up):
    half = part.shape[1]
    up[:, pl.ds(pl.multiple_of(scal[2] * half, 128), half)] = part[...].astype(f32)
    up[:, pl.ds(pl.multiple_of((1 - scal[2]) * half, 128), half)] = away[...].astype(f32)


def down_out_kernel(scal, part, away, down, out, full, cut):
    d = scal[2]
    rows, width = down.shape
    half = width // 2
    for ref, index in ((part, d), (away, 1 - d)):
        down[:, pl.ds(pl.multiple_of(index * half, 128), half)] = ref[:rows, :].astype(f32)
        piece = under(ref[rows:, :].astype(f32), rows // 2)
        full[pl.ds(pl.multiple_of(index * (rows // 2), 32), rows // 2), :] = piece
    flat_store(full, cut, out)


def qkv_out_kernel(scal, part, away, out, full, cut):
    half = part.shape[0]
    full[pl.ds(pl.multiple_of(scal[2] * half, 32), half), :] = part[...].astype(f32)
    full[pl.ds(pl.multiple_of((1 - scal[2]) * half, 32), half), :] = away[...].astype(f32)
    flat_store(full, cut, out)


def vector_kernel(scal, sums, feats, *outs):
    width = outs[0].shape[1]
    mine = feats[:, :width]
    for j in range(1, feats.shape[1] // width):
        mine = jnp.where(scal[1] == j, feats[:, j * width : (j + 1) * width], mine)
    for i in range(6):
        outs[i][...] = mine[i : i + 1, :]
    outs[6][...] = sums[6:7, :]
    width = outs[7].shape[1]
    outs[7][0:1, :] = sums[7:8, :width]
    outs[7][1:2, :] = sums[7:8, 2 * width : 3 * width]


def last_kernel(got, first, second):
    n_col, _, two = got.shape
    own = two // 2
    first[...] = jnp.concatenate([got[j, :, :own] for j in range(n_col)], axis=1)
    second[...] = jnp.concatenate([got[j, :, own:] for j in range(n_col)], axis=1)


def col_order():
    order = [0]
    for b in reversed(bits_of("col")):
        order = order + [o ^ b for o in order]
    return order


def join_dp(mine, got, scal):
    rows = sum(m.shape[0] for m in mine) // 2
    width = mine[0].shape[1]
    return call(
        functools.partial(part_kernel, len(mine), col_order()),
        [((rows, width), f32), ((rows, width), bf16)],
        scal,
        [*mine, *got],
    )


def finish_col(keep, send, first=1):
    bits = bits_of("col", first)
    for b in bits[:-1]:
        keep, send = add_halves(keep, swap(send, "col", b))
    return keep, swap(send, "col", bits[-1])


def share_dp(own, got):
    shape = own.shape
    total = call(add_kernel, [(shape, bf16)], None, [own, got])[0]
    for b in bits_of("dp", 2):
        total = call(add_kernel, [(shape, bf16)], None, [total, swap(total, "dp", b)])[0]
    return total, swap(total, "dp", 1)


def body(
    block_input,
    ln1_gain,
    ln1_bias,
    qkv_weight,
    qv_bias,
    out_weight,
    out_bias,
    ln2_gain,
    ln2_bias,
    up_weight,
    up_bias,
    down_weight,
    down_bias,
    out_grad,
):
    n_col = lax.axis_size("col")
    n_row = lax.axis_size("row")
    width_in = D // n_col
    width_out = D // n_row
    heads = width_out // HEAD
    order = row_order()
    own = block_input.shape[0] // n_col
    tokens = own * n_row
    half_ff = up_weight.shape[1] // 2
    ff = 2 * half_ff
    cols = range(1, n_col)
    c = lax.axis_index("col").astype(jnp.int32)
    d = lax.axis_index("dp").astype(jnp.int32) & 1
    scal = jnp.stack([lax.axis_index("row").astype(jnp.int32), c, d])
    token_sum = [((tokens // 2, D), f32), ((tokens // 2, D), bf16)]

    message = call(
        functools.partial(message_kernel, own),
        [((n_col, own + 16, 2 * width_in), bf16)],
        None,
        [
            block_input.T,
            out_grad.T,
            *[v[None] for v in (ln1_gain, ln1_bias, ln2_gain, ln2_bias, out_bias, down_bias)],
        ],
    )[0]

    qkv_flat, out_flat = qkv_weight, out_weight
    own_qkv = qkv_flat.reshape(width_in, 3 * width_out)
    own_out = out_flat.reshape(width_out, width_in)
    half_a = call(
        prep_kernel, [((width_in // 2, 3 * width_out + width_in), bf16)], scal, [own_qkv, own_out]
    )[0]
    half_m = call(prep_mlp_kernel, [((2 * width_in, half_ff), bf16)], scal, [up_weight, down_weight])[0]
    near_a = gather_col(half_a)[1:]
    far_a = [swap(v, "dp", 1) for v in near_a]
    half_m = after(half_m, near_a[2])
    near_m = gather_col(half_m)[1:]
    far_m = [swap(v, "dp", 1) for v in near_m]

    got = after(turn(message), near_a[0])
    xg_own, vec = call(token_kernel, [((2 * own, D), bf16), ((8, D), f32)], None, [got])
    xg = gather_row(xg_own)
    qkv_cut, a1, w_qkv, w_out = call(
        functools.partial(qkv_kernel, heads, tokens, n_row, n_col),
        [
            ((n_col, tokens // 2, 6 * HEAD), bf16),
            ((tokens, D), bf16),
            ((D, 3 * width_out), bf16),
            ((n_col, width_out, width_in), bf16),
        ],
        scal,
        [*xg, vec, qv_bias, own_qkv, own_out, *near_a, *far_a],
    )
    qkv_head = turn(after(qkv_cut, near_m[:2]))
    att_head = call(
        functools.partial(forward_kernel, order),
        [((n_col, tokens // 2, 2 * HEAD), bf16)],
        scal,
        [qkv_head],
        [((tokens * n_col, 3 * HEAD), bf16), ((tokens * n_col, HEAD), bf16)],
    )[0]
    attended, o_keep, o_send = call(
        functools.partial(out_kernel, heads, own),
        [((tokens, width_out), bf16)] + token_sum,
        None,
        [after(turn(after(att_head, near_m[2])), far_m[:2]), w_out],
    )
    resid1, a2_own = call(
        norm2_kernel, [((own, D), f32), ((own, D), bf16)], None, [*after(finish_row(o_keep, o_send), far_m[2]), xg_own, vec]
    )
    a2 = gather_row(a2_own)
    act, d_pre, up_sum, a_keep, a_send = call(
        functools.partial(mlp_kernel, n_row, n_col),
        [
            ((tokens, ff), bf16),
            ((tokens, ff), bf16),
            ((1, ff), f32),
            ((tokens // 2, 2 * D), f32),
            ((tokens // 2, 2 * D), bf16),
        ],
        scal,
        [*a2, *xg, up_bias[None], up_weight, down_weight, *near_m, *far_m],
        [((D, ff), bf16), ((D, ff), bf16)],
    )
    up_mine, up_other, down_mine, down_other = call(
        functools.partial(mlp_grad_kernel, n_row),
        [((D, half_ff), bf16)] * 4,
        None,
        [*a2, *xg, act, d_pre],
    )
    a_keep, a_got = finish_row(a_keep, a_send)
    a_got = after(a_got, up_other, down_other)
    up_got = swap(up_other, "dp", 1)
    down_got = swap(after(down_other, up_got), "dp", 1)
    gp, d_resid1, sums2 = call(
        norm2_back_kernel,
        [((own, D), bf16), ((own, D), f32), ((4, D), f32)],
        None,
        [a_keep, a_got, xg_own, vec, resid1],
    )
    gp_all = gather_row(gp)
    d_att_cut, out_mine, out_other = call(
        functools.partial(d_att_kernel, n_row, heads),
        [((n_col, tokens // 2, 2 * HEAD), bf16)] + [((n_col * width_out // 4, 2 * width_in), bf16)] * 2,
        scal,
        [*gp_all, attended, w_out],
        [((width_out, D), bf16)],
    )
    out_got = swap(out_other, "dp", 1)
    up_parts = join_dp([up_mine], [after(up_got, gp_all)], scal)
    d_att_head = after(turn(d_att_cut), up_parts, down_got)
    up_total, up_away = share_dp(*finish_col(*up_parts))
    d_qkv_head = call(
        functools.partial(backward_kernel, order),
        [((n_col, tokens // 2, 6 * HEAD), bf16)],
        scal,
        [qkv_head, d_att_head],
        [
            ((tokens * n_col, 3 * HEAD), bf16),
            ((tokens * n_col, HEAD), bf16),
            ((tokens * n_col, 3 * HEAD), bf16),
            ((HEAD, tokens * n_col), f32),
            ((HEAD, tokens * n_col), f32),
        ],
    )[0]
    down_parts = join_dp([down_mine, out_mine], [down_got, out_got], scal)
    d_qkv_cut = after(turn(after(d_qkv_head, up_total)), down_parts)
    d_keep, d_send, sums1, qkv_mine, qkv_other = call(
        functools.partial(d_a1_kernel, n_row, heads),
        token_sum + [((8, D), f32), ((D // 2, 3 * width_out), bf16), ((D // 2 + 32, 3 * width_out), bf16)],
        scal,
        [*xg, d_qkv_cut, a1, w_qkv, sums2, up_sum],
        [((D, 3 * width_out), bf16)],
    )
    qkv_got = swap(qkv_other, "dp", 1)

    outs = call(
        final_kernel,
        [((n_col, width_in, 2 * own), bf16)],
        None,
        [*finish_row(d_keep, d_send), a_keep, a_got, xg_own, vec, resid1, d_resid1],
    )[0]
    input_grad, block_output = call(last_kernel, [((width_in, tokens), bf16)] * 2, None, [turn(outs)])

    d_up = call(up_out_kernel, [((width_in, ff), f32)], scal, [up_total, up_away])[0]
    d_down, d_out = call(
        down_out_kernel,
        [((width_in, ff), f32), ((width_out * width_in // 128, 128), f32)],
        scal,
        share_dp(*finish_col(*down_parts)),
        [((width_out, width_in), f32), ((pl.cdiv(width_in, 128), width_out, 128), f32)],
    )
    rows, width = D // 2, 3 * width_out
    keep, send, sums = call(
        functools.partial(qkv_part_kernel, col_order()),
        [((rows // 2, width), f32), ((rows // 2 + 32, width), bf16), ((8, D), f32)],
        scal,
        [qkv_mine, after(qkv_got, outs), sums1],
    )
    bits = bits_of("col")
    for b in bits[:-1]:
        rows //= 2
        keep, send, sums = call(
            qkv_half_kernel,
            [((rows // 2, width), f32), ((rows // 2 + 32, width), bf16), ((8, D), f32)],
            None,
            [keep, swap(send, "col", b), sums],
        )
    total, sums = call(
        qkv_add_kernel,
        [((rows // 2, width), bf16), ((8, D), f32)],
        None,
        [keep, swap(send, "col", bits[-1]), sums],
    )

    def add(value, axis, bit, kind=f32):
        return call(add_kernel, [(value.shape, kind)], None, [value, swap(value, axis, bit)])[0]

    for b in bits_of("dp", 2):
        total, sums = add(total, "dp", b, bf16), add(sums, "dp", b)
    away = swap(total, "dp", 1)
    feats = sums
    for b in bits_of("row"):
        feats = add(feats, "row", b)
    d_qkv = call(
        qkv_out_kernel,
        [((width * width_in // 128, 128), f32)],
        scal,
        [total, after(away, d_up, d_down, input_grad)],
        [((width_in, width), f32), ((pl.cdiv(width, 128), width_in, 128), f32)],
    )[0]
    vecs = call(
        vector_kernel,
        [((1, width_in), f32)] * 6 + [((1, ff), f32), ((2, width_out), f32)],
        scal,
        [sums, feats],
    )

    return (
        block_output.T,
        input_grad.T,
        vecs[0].reshape(-1),
        vecs[1].reshape(-1),
        d_qkv.reshape(1, 1, -1),
        vecs[7],
        d_out.reshape(1, 1, -1),
        vecs[4].reshape(-1),
        vecs[2].reshape(-1),
        vecs[3].reshape(-1),
        d_up,
        vecs[6].reshape(-1),
        d_down,
        vecs[5].reshape(-1),
    )


def solution(mesh):
    in_specs = (
        P(("dp", "row"), "col"),
        P("col"),
        P("col"),
        P("col", "row", None),
        P(None, "row"),
        P("row", "col", None),
        P("col"),
        P("col"),
        P("col"),
        P("col", "row"),
        P("row"),
        P("col", "row"),
        P("col"),
        P(("dp", "row"), "col"),
    )
    out_specs = (
        P(("dp", "row"), "col"),
        P(("dp", "row"), "col"),
        P("col"),
        P("col"),
        P("col", "row", None),
        P(None, "row"),
        P("row", "col", None),
        P("col"),
        P("col"),
        P("col"),
        P("col", "row"),
        P("row"),
        P("col", "row"),
        P("col"),
    )
    return jax.shard_map(body, mesh=mesh, in_specs=in_specs, out_specs=out_specs, check_vma=False)
```

```python
import functools
import math

import jax
import jax.numpy as jnp
from jax import lax
from jax.experimental import pallas as pl
from jax.experimental.pallas import tpu as pltpu
from jax.sharding import PartitionSpec as P

D = 768
HEAD = 64
SCALE = 1.0 / math.sqrt(HEAD)
C0 = math.sqrt(2.0 / math.pi)
C1 = 0.044715
bf16 = jnp.bfloat16
f32 = jnp.float32
VMEM = pl.BlockSpec(memory_space=pltpu.VMEM)
SMEM = pl.BlockSpec(memory_space=pltpu.SMEM)


def dot_nn(a, b):
    return lax.dot_general(a, b, (((1,), (0,)), ((), ())), preferred_element_type=f32)


def dot_nt(a, b):
    return lax.dot_general(a, b, (((1,), (1,)), ((), ())), preferred_element_type=f32)


def dot_tn(a, b):
    return lax.dot_general(a, b, (((0,), (0,)), ((), ())), preferred_element_type=f32)


def call(kernel, outs, scalars, args, scratch=(), limit=20, cost=0):
    first = [] if scalars is None else [scalars]
    return pl.pallas_call(
        kernel,
        out_shape=[jax.ShapeDtypeStruct(s, t) for s, t in outs],
        in_specs=[SMEM] * len(first) + [VMEM] * len(args),
        out_specs=[VMEM] * len(outs),
        scratch_shapes=[pltpu.VMEM(s, t) for s, t in scratch],
        compiler_params=pltpu.CompilerParams(vmem_limit_bytes=limit * 1024 * 1024),
        cost_estimate=pl.CostEstimate(flops=1, bytes_accessed=1 + 3_000_000 * cost, transcendentals=0),
    )(*first, *args)


def swap(value, axis, bit):
    n = lax.axis_size(axis)
    return lax.ppermute(value, axis, [(i, i ^ bit) for i in range(n)])


def turn(value, split=0, concat=0):
    return lax.all_to_all(value, "col", split, concat, tiled=True)


def bits_of(axis, first=1):
    n = lax.axis_size(axis)
    bits = []
    b = first
    while b < n:
        bits.append(b)
        b *= 2
    return bits


def row_order():
    order = [0]
    for b in reversed(bits_of("row")):
        order = order + [o ^ b for o in order]
    return order


def gather_row(value):
    pieces = [value]
    for b in reversed(bits_of("row")):
        pieces = pieces + [swap(p, "row", b) for p in pieces]
    return pieces


def gather_col(value):
    pieces = {0: value}
    for b in reversed(bits_of("col")):
        for k in list(pieces):
            pieces[k ^ b] = swap(pieces[k], "col", b)
    return [pieces[k] for k in range(lax.axis_size("col"))]


def finish_row(keep, send):
    bits = bits_of("row")
    for b in bits[:-1]:
        keep, send = add_halves(keep, swap(send, "row", b))
    return keep, swap(send, "row", bits[-1])


def add_halves(keep, got):
    rows, width = keep.shape
    return call(halves_kernel, [((rows // 2, width), f32), ((rows // 2, width), bf16)], None, [keep, got])


def after(value, *others):
    return lax.optimization_barrier((value, others))[0]


def beside(value, chunk):
    half = chunk // 2
    starts = range(0, value.shape[0], chunk)
    first = jnp.concatenate([value[i : i + half] for i in starts], axis=0)
    second = jnp.concatenate([value[i + half : i + chunk] for i in starts], axis=0)
    return jnp.concatenate([first, second], axis=1)


def under(value, chunk):
    half = chunk // 2
    width = value.shape[1] // 2
    parts = []
    for i in range(0, value.shape[0], half):
        parts += [value[i : i + half, :width], value[i : i + half, width:]]
    return jnp.concatenate(parts, axis=0)


def place(scal, order, k, kk, chunk, n_col):
    at = ((scal[0] ^ order[kk]) * n_col + (scal[1] ^ k)) * chunk
    return pl.ds(pl.multiple_of(at, chunk), chunk)


def load_natural(scal, order, pieces, dst):
    chunk = pieces[0].shape[0] // len(order)
    for k, piece in enumerate(pieces):
        for kk in range(len(order)):
            dst[place(scal, order, k, kk, chunk, len(pieces)), :] = piece[kk * chunk : (kk + 1) * chunk, :]


def chunk_of(scal, order, quarter, chunk):
    want = quarter ^ scal[0]
    index = jnp.int32(0)
    for i, o in enumerate(order):
        index = jnp.where(want == o, i, index)
    return pl.ds(pl.multiple_of(index * chunk, chunk), chunk)


def row_exps(q, k, low, first):
    scores = dot_nt(q, k)
    tail = scores[:, low:]
    rows = lax.broadcasted_iota(jnp.int32, tail.shape, 0) + first
    cols = lax.broadcasted_iota(jnp.int32, tail.shape, 1)
    tail = jnp.where(cols <= rows, tail, -1e30)
    scores = tail if low == 0 else jnp.concatenate([scores[:, :low], tail], axis=1)
    top = jnp.max(scores, axis=-1, keepdims=True)
    e = jnp.exp2((scores - top) * (SCALE * math.log2(math.e)))
    return e, jnp.sum(e, axis=-1, keepdims=True)


def attention_kernel(order, n_col, heads, scal, q_ref, *refs):
    pieces, (w, att_out, keep, send, nat) = refs[:n_col], refs[n_col:]
    load_natural(scal, order, pieces, nat)
    n_row = len(order)
    chunk = q_ref.shape[0] // n_row
    block = chunk * n_col
    width = heads * HEAD
    first = scal[1] * chunk
    parts = [[] for _ in range(n_row)]
    for h in range(heads):
        k = nat[:, h * HEAD : (h + 1) * HEAD]
        v = nat[:, width + h * HEAD : width + (h + 1) * HEAD]
        for i in range(n_row):
            upto = (i + 1) * block
            q = q_ref[chunk_of(scal, order, i, chunk), :][:, h * HEAD : (h + 1) * HEAD]
            e, total = row_exps(q, k[:upto], i * block, first)
            parts[i].append((dot_nn(e.astype(bf16), v[:upto]) / total).astype(bf16))
    for i in range(n_row):
        att_out[chunk_of(scal, order, i, chunk), :] = jnp.concatenate(parts[i], axis=1)
    w_all = jnp.concatenate([w[j] for j in range(n_col)], axis=1)
    halves_out(dot_nn(att_out[...], w_all), keep, send)


def attention_back_kernel(order, col_order, heads, scal, q_ref, *refs):
    n_col = len(col_order)
    pieces, (do_ref, dq, keep, send, nat, grads_t, grads) = refs[:n_col], refs[n_col:]
    load_natural(scal, order, pieces, nat)
    n_row = len(order)
    chunk = q_ref.shape[0] // n_row
    block = chunk * n_col
    width = heads * HEAD
    first = scal[1] * chunk
    grads_t[...] = jnp.zeros_like(grads_t)
    parts = [[] for _ in range(n_row)]
    for h in range(heads):
        here = slice(h * HEAD, (h + 1) * HEAD)
        there = slice(width + h * HEAD, width + (h + 1) * HEAD)
        k = nat[:, here]
        v = nat[:, there]
        for i in range(n_row):
            upto = (i + 1) * block
            at = chunk_of(scal, order, i, chunk)
            q = q_ref[at, :][:, here]
            do = do_ref[at, :][:, here]
            e, total = row_exps(q, k[:upto], i * block, first)
            p = e * (1.0 / total)
            grads_t[there, :upto] += dot_tn(do, p.astype(bf16))
            dp = dot_nt(do, v[:upto])
            ds = (p * (dp - jnp.sum(dp * p, axis=-1, keepdims=True))).astype(bf16)
            parts[i].append((dot_nn(ds, k[:upto]) * SCALE).astype(bf16))
            grads_t[here, :upto] += dot_tn(q, ds)
    for i in range(n_row):
        dq[chunk_of(scal, order, i, chunk), :] = jnp.concatenate(parts[i], axis=1)
    grads[:, :width] = grads_t[:width, :].T * SCALE
    grads[:, width:] = grads_t[width:, :].T
    rows = n_row * chunk
    for i, k in enumerate(col_order):
        to, base = (keep, i) if i < n_col // 2 else (send, i - n_col // 2)
        for kk in range(n_row):
            at = base * rows + kk * chunk
            to[at : at + chunk, :] = grads[place(scal, order, k, kk, chunk, n_col), :].astype(to.dtype)


def norm_stats(v):
    mean = jnp.sum(v, axis=-1, keepdims=True) / D
    var = jnp.sum(v * v, axis=-1, keepdims=True) / D - mean * mean
    inverse = lax.rsqrt(var + 1e-05)
    return (v - mean) * inverse, inverse


def norm_back(grad, centred, inverse, gain):
    scaled = grad * gain
    first = jnp.sum(scaled, axis=-1, keepdims=True) / D
    second = jnp.sum(scaled * centred, axis=-1, keepdims=True) / D
    return inverse * (scaled - first - centred * second)


def stacked(refs, rows=slice(None)):
    return jnp.concatenate([r[rows, :] for r in refs], axis=0)


def halves_kernel(keep_ref, got_ref, keep, send):
    half = keep_ref.shape[0] // 2
    keep[...] = keep_ref[:half, :] + got_ref[:half, :].astype(f32)
    send[...] = (keep_ref[half:, :] + got_ref[half:, :].astype(f32)).astype(bf16)


def halves_out(value, keep, send, at=0):
    half, width = value.shape[0] // 2, value.shape[1]
    keep[:, at : at + width] = value[:half]
    send[:, at : at + width] = value[half:].astype(bf16)


def message_kernel(own, n_col, scal, x, g, *refs):
    vectors, outs, cut = refs[: -n_col - 1], refs[-n_col - 1 : -1], refs[-1]
    x_all = x[...].astype(f32).T.astype(bf16)
    g_all = g[...].astype(f32).T.astype(bf16)
    width = x_all.shape[1]
    rest = jnp.concatenate([v[...] for v in vectors] + [jnp.zeros((8 - len(vectors), width), f32)], axis=0)
    parts = []
    for _ in range(3):
        part = rest.astype(bf16).astype(f32)
        parts.append(part)
        rest = rest - part
    parts.append(jnp.zeros((8, width), f32))
    parts = jnp.concatenate(parts, axis=0).astype(bf16)
    parts = beside(parts, parts.shape[0])
    half = own // 2
    for j in range(n_col):
        cut[j, :half, :] = beside(x_all[j * own : (j + 1) * own], own)
        cut[j, half:own, :] = beside(g_all[j * own : (j + 1) * own], own)
    for k in range(n_col):
        outs[k][:own, :] = cut[scal[1] ^ k]
        outs[k][own:, :] = parts


def prep_kernel(scal, qkv, out, half_a):
    half, width3 = half_a.shape[0], qkv.shape[1]
    rows = pl.ds(pl.multiple_of(scal[2] * half, 32), half)
    half_a[:, :width3] = qkv[rows, :]
    half_a[:, width3:] = out[rows, :]


def prep_mlp_kernel(scal, up, down, half_m):
    tall, half_ff = up.shape[0], half_m.shape[1]
    lanes = pl.ds(pl.multiple_of(scal[2] * half_ff, 128), half_ff)
    half_m[:tall, :] = up[:, lanes]
    half_m[tall:, :] = down[:, lanes]


def token_kernel(scal, *refs):
    pieces, (xg, vec, got) = refs[:-3], refs[-3:]
    n_col, rows, width = got.shape
    width = width // 2
    for k in range(n_col):
        got[scal[1] ^ k] = pieces[k][...]
    own = xg.shape[0] // 2
    for j in range(n_col):
        at = slice(j * width, (j + 1) * width)
        xg[:, at] = under(got[j, :own, :], own)
        v = under(got[j, own:, :].astype(f32), 2 * (rows - own))
        vec[:, at] = v[:8] + v[8:16] + v[16:24]


def qkv_kernel(heads, tokens, n_row, n_col, scal, *refs):
    xgs, (vec, qv_bias, own_qkv, own_out), refs = refs[:n_row], refs[n_row : n_row + 4], refs[n_row + 4 :]
    near, far, (q_out, kv_out, a1_out, w_all, w_out) = refs[: n_col - 1], refs[n_col - 1 : 2 * n_col - 2], refs[2 * n_col - 2 :]
    c, d = scal[1], scal[2]
    rows, width3 = own_qkv.shape
    half = rows // 2
    w_all[pl.ds(pl.multiple_of(c * rows, 64), rows), :] = own_qkv[...]
    w_out[c] = own_out[...]
    for k in range(1, n_col):
        for part, ref in ((d, near[k - 1]), (1 - d, far[k - 1])):
            w_all[pl.ds(pl.multiple_of(((c ^ k) * 2 + part) * half, 32), half), :] = ref[:, :width3]
            w_out[c ^ k, pl.ds(pl.multiple_of(part * half, 32), half), :] = ref[:, width3:]
    x = stacked(xgs, slice(0, tokens // n_row))
    centred, _ = norm_stats(x.astype(f32))
    a1 = (centred * vec[0:1, :] + vec[1:2, :]).astype(bf16)
    a1_out[...] = a1
    width = heads * HEAD
    shifts = jnp.concatenate([qv_bias[0:1, :], jnp.zeros((1, width), f32), qv_bias[1:2, :]], axis=1)
    qkv = (dot_nn(a1, w_all[...]) + shifts).astype(bf16)
    q_out[...] = qkv[:, :width]
    kv_out[...] = qkv[:, width:]


def norm2_kernel(keep, got, xg, vec, resid_out, a2_out):
    own = keep.shape[0]
    resid = xg[:own, :].astype(f32) + (keep[...] + got[...].astype(f32)) + vec[4:5, :]
    resid_out[...] = resid
    centred, _ = norm_stats(resid)
    a2_out[...] = (centred * vec[2:3, :] + vec[3:4, :]).astype(bf16)


def mlp_kernel(n_row, n_col, scal, *refs):
    a2s, gs, refs = refs[:n_row], refs[n_row : 2 * n_row], refs[2 * n_row :]
    up_bias, up_own, down_own = refs[:3]
    near, far = refs[3 : 2 + n_col], refs[2 + n_col : 1 + 2 * n_col]
    act_out, d_pre_out, bias_sum, keep, send, wu, wd = refs[1 + 2 * n_col :]
    c, d = scal[1], scal[2]
    rows, width = up_own.shape
    half = width // 2
    mine = pl.ds(pl.multiple_of(d * half, 128), half)
    other = pl.ds(pl.multiple_of((1 - d) * half, 128), half)
    here = pl.ds(pl.multiple_of(c * rows, 64), rows)
    for w, own in ((wu, up_own), (wd, down_own)):
        w[here, :half] = own[:, mine]
        w[here, half:] = own[:, other]
    for k in range(1, n_col):
        there = pl.ds(pl.multiple_of((c ^ k) * rows, 64), rows)
        wu[there, :half] = near[k - 1][:rows, :]
        wd[there, :half] = near[k - 1][rows:, :]
        wu[there, half:] = far[k - 1][:rows, :]
        wd[there, half:] = far[k - 1][rows:, :]
    own = a2s[0].shape[0]
    shift = jnp.concatenate([up_bias[:, mine], up_bias[:, other]], axis=1)
    pre = dot_nn(stacked(a2s), wu[...]) + shift
    square = pre * pre
    t = jnp.tanh(C0 * (pre + C1 * (square * pre)))
    act = (0.5 * pre * (1.0 + t)).astype(bf16)
    slope = 0.5 * (1.0 + t) + (0.5 * C0) * pre * (1.0 - t * t) * (1.0 + (3.0 * C1) * square)
    d_act = dot_nn(stacked(gs, slice(own, 2 * own)), wd[...])
    d_pre = (d_act * slope).astype(bf16)
    act_out[...] = act
    d_pre_out[...] = d_pre
    total = jnp.sum(d_pre.astype(f32), axis=0, keepdims=True)
    bias_sum[:, mine] = total[:, :half]
    bias_sum[:, other] = total[:, half:]
    halves_out(dot_nt(d_pre, wu[...]), keep, send)
    halves_out(dot_nt(act, wd[...]), keep, send, D)


def mlp_grad_kernel(n_row, *refs):
    a2s, gs, refs = refs[:n_row], refs[n_row : 2 * n_row], refs[2 * n_row :]
    act, d_pre, up_mine, up_other, down_mine, down_other = refs
    half = act.shape[1] // 2
    own = a2s[0].shape[0]
    a2, g = stacked(a2s), stacked(gs, slice(own, 2 * own))
    up_mine[...] = dot_tn(a2, d_pre[:, :half]).astype(bf16)
    up_other[...] = dot_tn(a2, d_pre[:, half:]).astype(bf16)
    down_mine[...] = dot_tn(g, act[:, :half]).astype(bf16)
    down_other[...] = dot_tn(g, act[:, half:]).astype(bf16)


def norm2_back_kernel(keep, got, xg, vec, resid_ref, gp_out, d_resid_out, sums):
    own = keep.shape[0]
    d_a2 = keep[:, :D] + got[:, :D].astype(f32)
    centred, inverse = norm_stats(resid_ref[...])
    g = xg[own:, :].astype(f32)
    d_resid = g + norm_back(d_a2, centred, inverse, vec[2:3, :])
    gp = d_resid.astype(bf16)
    d_resid_out[...] = d_resid
    gp_out[...] = gp
    for i, v in enumerate((d_a2 * centred, d_a2, gp.astype(f32), g)):
        sums[i : i + 1, :] = jnp.sum(v, axis=0, keepdims=True)


def d_att_kernel(n_row, heads, scal, *refs):
    gps, (att, w, d_att_out, mine, other, full) = refs[:n_row], refs[n_row:]
    d = scal[2]
    gp = stacked(gps)
    n_col, rows, width = w.shape
    w_all = jnp.concatenate([w[j] for j in range(n_col)], axis=1)
    d_att = dot_nt(gp, w_all).astype(bf16)
    d_att_out[...] = d_att
    full[...] = dot_tn(att[...], gp).astype(bf16)
    half = rows // 2
    for to, part in ((mine, d), (other, 1 - d)):
        piece = full[pl.ds(pl.multiple_of(part * half, 32), half), :]
        for j in range(n_col):
            to[j * (half // 2) : (j + 1) * (half // 2), :] = beside(piece[:, j * width : (j + 1) * width], half)


def d_a1_kernel(n_row, n_col, scal, *refs):
    xgs, (dq, dkv_keep, dkv_got, a1, w), refs = refs[:n_row], refs[n_row : n_row + 5], refs[n_row + 5 :]
    sums2, up_sum, refs = refs[0], refs[1], refs[2:]
    keep, send, sums, mine, other, full = refs
    d = scal[2]
    tokens = a1.shape[0]
    d_kv = (dkv_keep[...] + dkv_got[...].astype(f32)).astype(bf16)
    d_qkv = jnp.concatenate([dq[...], d_kv], axis=1)
    part = dot_nt(d_qkv, w[...])
    half = tokens // 2
    keep[...] = part[:half]
    send[:half, :] = part[half:].astype(bf16)
    full[...] = dot_tn(a1[...], d_qkv).astype(bf16)
    half = full.shape[0] // (2 * n_col)
    for j in range(n_col):
        at = slice(j * half, (j + 1) * half)
        mine[at, :] = full[pl.ds(pl.multiple_of((2 * j + d) * half, 32), half), :]
        other[at, :] = full[pl.ds(pl.multiple_of((2 * j + 1 - d) * half, 32), half), :]
    centred, _ = norm_stats(stacked(xgs, slice(0, tokens // n_row)).astype(f32))
    pad = jnp.zeros((1, D - d_qkv.shape[1]), f32)
    total = jnp.concatenate(
        [
            jnp.sum(part * centred, axis=0, keepdims=True),
            jnp.sum(part, axis=0, keepdims=True),
            sums2[...],
            up_sum[...],
            jnp.concatenate([jnp.sum(d_qkv.astype(f32), axis=0, keepdims=True), pad], axis=1),
        ],
        axis=0,
    )
    sums[...] = total
    send[tokens // 2 :, :] = pack_wide(total)


def final_kernel(d_keep, d_got, sums_ref, a_keep, a_got, xg, vec, resid, d_resid, out, sums):
    n_col, width, rows = out.shape
    own = rows // 2
    d_a1 = d_keep[...] + d_got[:own, :].astype(f32)
    sums[...] = add_row_sums(sums_ref[...], unpack_wide(d_got[own:, :]))
    centred, inverse = norm_stats(xg[:own, :].astype(f32))
    d_x = (d_resid[...] + norm_back(d_a1, centred, inverse, vec[0:1, :])).astype(bf16)
    y = (resid[...] + (a_keep[:, D:] + a_got[:, D:].astype(f32)) + vec[5:6, :]).astype(bf16)
    both = jnp.concatenate([d_x.astype(f32), y.astype(f32)], axis=0)
    for j in range(n_col):
        out[j] = both[:, j * width : (j + 1) * width].T.astype(bf16)


def part_kernel(n_in, order, scal, *refs):
    mine, got, (keep, send) = refs[:n_in], refs[n_in : 2 * n_in], refs[2 * n_in :]
    n_col = len(order)
    height = 2 * keep.shape[0] // n_col
    for i, k in enumerate(order):
        to, at = (keep, i) if i < n_col // 2 else (send, i - n_col // 2)
        at = at * height
        for m, g in zip(mine, got):
            rows = m.shape[0] // n_col
            there = pl.ds(pl.multiple_of((scal[1] ^ k) * rows, 16), rows)
            total = m[there, :].astype(f32) + g[there, :].astype(f32)
            to[at : at + rows, :] = total.astype(to.dtype)
            at += rows


def add_kernel(*refs):
    total = refs[0][...].astype(f32)
    for r in refs[1:-1]:
        total = total + r[...].astype(f32)
    refs[-1][...] = total.astype(refs[-1].dtype)


def three_parts(v):
    parts = []
    for _ in range(3):
        part = v.astype(bf16).astype(f32)
        parts.append(part)
        v = v - part
    return parts


def pack_wide(v):
    return jnp.concatenate(three_parts(v) + [jnp.zeros_like(v)], axis=0).astype(bf16)


def unpack_wide(v):
    v = v.astype(f32)
    n = v.shape[0] // 4
    return v[:n] + v[n : 2 * n] + v[2 * n : 3 * n]


def pack_sums(v):
    parts = three_parts(v)
    cut = 3 * v.shape[1] // 4
    rows = [p[:, :cut] for p in parts] + [jnp.concatenate([p[:, cut:] for p in parts], axis=1)]
    return jnp.concatenate(rows, axis=0).astype(bf16)


def unpack_sums(v):
    v = v.astype(f32)
    n = v.shape[0] // 4
    third = v.shape[1] // 3
    parts = [
        jnp.concatenate([v[i * n : (i + 1) * n], v[3 * n :, i * third : (i + 1) * third]], axis=1) for i in range(3)
    ]
    return parts[0] + parts[1] + parts[2]


def add_row_sums(own, got):
    return jnp.concatenate([own[:6] + got[:6], own[6:]], axis=0)


def d_half_kernel(keep_ref, got_ref, sums_ref, keep, send, sums):
    rows = keep_ref.shape[0]
    half = rows // 2
    keep[...] = keep_ref[:half, :] + got_ref[:half, :].astype(f32)
    send[:half, :] = (keep_ref[half:, :] + got_ref[half:rows, :].astype(f32)).astype(bf16)
    total = add_row_sums(sums_ref[...], unpack_wide(got_ref[rows:, :]))
    sums[...] = total
    send[half:, :] = pack_wide(total)


def qkv_part_kernel(order, scal, mine, got, own_sums, keep, send):
    n_col = len(order)
    rows = mine.shape[0] // n_col
    for i, k in enumerate(order):
        to, at = (keep, i) if i < n_col // 2 else (send, i - n_col // 2)
        there = pl.ds(pl.multiple_of((scal[1] ^ k) * rows, 16), rows)
        total = mine[there, :].astype(f32) + got[there, :].astype(f32)
        to[at * rows : (at + 1) * rows, :] = total.astype(to.dtype)
    send[keep.shape[0] :, :] = pack_sums(own_sums[...])


def qkv_half_kernel(keep_ref, got_ref, sums_ref, keep, send, sums):
    rows = keep_ref.shape[0]
    half = rows // 2
    keep[...] = keep_ref[:half, :] + got_ref[:half, :].astype(f32)
    send[:half, :] = (keep_ref[half:, :] + got_ref[half:rows, :].astype(f32)).astype(bf16)
    total = sums_ref[...] + unpack_sums(got_ref[rows:, :])
    sums[...] = total
    send[half:, :] = pack_sums(total)


def qkv_add_kernel(keep_ref, got_ref, sums_ref, out, sums):
    rows = out.shape[0] - 32
    out[:rows, :] = (keep_ref[:rows, :].astype(f32) + got_ref[:rows, :].astype(f32)).astype(bf16)
    total = sums_ref[...] + unpack_sums(got_ref[rows:, :])
    sums[...] = total
    out[rows:, :] = pack_sums(total)


def flat_store(value, cut, out):
    rows, width = value.shape
    lines = 2 * width // 128
    for i in range(cut.shape[0]):
        high = min(width, (i + 1) * 128)
        cut[i, :, : high - i * 128] = value[:, i * 128 : high]
    both = []
    for odd in range(2):
        pieces = [cut[i, pl.ds(odd, rows // 2, stride=2), :] for i in range(cut.shape[0])]
        both.append(jnp.concatenate(pieces, axis=1)[:, :width])
    both = jnp.concatenate(both, axis=1)
    for g in range(lines):
        out[pl.ds(g, rows // 2, stride=lines), :] = both[:, g * 128 : (g + 1) * 128]


def up_out_kernel(scal, part, away, up):
    half = part.shape[1]
    up[:, pl.ds(pl.multiple_of(scal[2] * half, 128), half)] = part[...].astype(f32)
    up[:, pl.ds(pl.multiple_of((1 - scal[2]) * half, 128), half)] = away[...].astype(f32)


def down_out_kernel(scal, part, away, down, out, full, cut):
    d = scal[2]
    rows, width = down.shape
    half = width // 2
    for ref, index in ((part, d), (away, 1 - d)):
        down[:, pl.ds(pl.multiple_of(index * half, 128), half)] = ref[:rows, :].astype(f32)
        piece = under(ref[rows:, :].astype(f32), rows // 2)
        full[pl.ds(pl.multiple_of(index * (rows // 2), 32), rows // 2), :] = piece
    flat_store(full, cut, out)


def qkv_out_kernel(scal, part, away, sums_ref, out, *refs):
    outs, (full, cut) = refs[:-2], refs[-2:]
    half = part.shape[0] - 32
    full[pl.ds(pl.multiple_of(scal[2] * half, 32), half), :] = part[:half, :].astype(f32)
    full[pl.ds(pl.multiple_of((1 - scal[2]) * half, 32), half), :] = away[:half, :].astype(f32)
    flat_store(full, cut, out)
    sums = sums_ref[...] + unpack_sums(away[half:, :])
    width = outs[0].shape[1]
    mine = sums[:, :width]
    for j in range(1, sums.shape[1] // width):
        mine = jnp.where(scal[1] == j, sums[:, j * width : (j + 1) * width], mine)
    for i in range(6):
        outs[i][...] = mine[i : i + 1, :]
    outs[6][...] = sums[6:7, :]
    width = outs[7].shape[1]
    outs[7][0:1, :] = sums[7:8, :width]
    outs[7][1:2, :] = sums[7:8, 2 * width : 3 * width]


def last_kernel(got, first, second):
    n_col, _, two = got.shape
    own = two // 2
    first[...] = jnp.concatenate([got[j, :, :own] for j in range(n_col)], axis=1)
    second[...] = jnp.concatenate([got[j, :, own:] for j in range(n_col)], axis=1)


def col_order():
    order = [0]
    for b in reversed(bits_of("col")):
        order = order + [o ^ b for o in order]
    return order


def join_dp(mine, got, scal):
    rows = sum(m.shape[0] for m in mine) // 2
    width = mine[0].shape[1]
    return call(
        functools.partial(part_kernel, len(mine), col_order()),
        [((rows, width), f32), ((rows, width), bf16)],
        scal,
        [*mine, *got],
    )


def finish_col(keep, send, first=1):
    bits = bits_of("col", first)
    for b in bits[:-1]:
        keep, send = add_halves(keep, swap(send, "col", b))
    return keep, swap(send, "col", bits[-1])


def share_dp(own, got):
    shape = own.shape
    total = call(add_kernel, [(shape, bf16)], None, [own, got])[0]
    for b in bits_of("dp", 2):
        total = call(add_kernel, [(shape, bf16)], None, [total, swap(total, "dp", b)])[0]
    return total, swap(total, "dp", 1)


def body(
    block_input,
    ln1_gain,
    ln1_bias,
    qkv_weight,
    qv_bias,
    out_weight,
    out_bias,
    ln2_gain,
    ln2_bias,
    up_weight,
    up_bias,
    down_weight,
    down_bias,
    out_grad,
):
    n_col = lax.axis_size("col")
    n_row = lax.axis_size("row")
    width_in = D // n_col
    width_out = D // n_row
    heads = width_out // HEAD
    order = row_order()
    own = block_input.shape[0] // n_col
    tokens = own * n_row
    half_ff = up_weight.shape[1] // 2
    ff = 2 * half_ff
    cols = range(1, n_col)
    c = lax.axis_index("col").astype(jnp.int32)
    d = lax.axis_index("dp").astype(jnp.int32) & 1
    scal = jnp.stack([lax.axis_index("row").astype(jnp.int32), c, d])
    token_sum = [((tokens // 2, D), f32), ((tokens // 2, D), bf16)]

    shape = (own + 16, 2 * width_in)
    message = call(
        functools.partial(message_kernel, own, n_col),
        [(shape, bf16)] * n_col,
        scal,
        [
            block_input.T,
            out_grad.T,
            *[v[None] for v in (ln1_gain, ln1_bias, ln2_gain, ln2_bias, out_bias, down_bias)],
        ],
        [((n_col, own, 2 * width_in), bf16)],
    )
    got = [message[0]] + [swap(message[k], "col", k) for k in range(1, n_col)]

    qkv_flat, out_flat = qkv_weight, out_weight
    own_qkv = qkv_flat.reshape(width_in, 3 * width_out)
    own_out = out_flat.reshape(width_out, width_in)
    half_a = call(
        prep_kernel, [((width_in // 2, 3 * width_out + width_in), bf16)], scal, [own_qkv, own_out]
    )[0]
    half_m = call(prep_mlp_kernel, [((2 * width_in, half_ff), bf16)], scal, [up_weight, down_weight])[0]
    near_a = gather_col(half_a)[1:]
    far_a = [swap(v, "dp", 1) for v in near_a]
    half_m = after(half_m, near_a[2], far_a[:2])
    near_m = gather_col(half_m)[1:]
    far_m = [swap(v, "dp", 1) for v in near_m[:2]]

    xg_own, vec = call(
        token_kernel, [((2 * own, D), bf16), ((8, D), f32)], scal, got, [((n_col, *shape), bf16)]
    )
    xg = gather_row(xg_own)
    q, kv, a1, w_qkv, w_out = call(
        functools.partial(qkv_kernel, heads, tokens, n_row, n_col),
        [
            ((tokens, width_out), bf16),
            ((tokens, 2 * width_out), bf16),
            ((tokens, D), bf16),
            ((D, 3 * width_out), bf16),
            ((n_col, width_out, width_in), bf16),
        ],
        scal,
        [*xg, vec, qv_bias, own_qkv, own_out, *near_a, *far_a],
    )
    kv_all = gather_col(after(kv, near_m[:2]))
    attended, o_keep, o_send = call(
        functools.partial(attention_kernel, order, n_col, heads),
        [((tokens, width_out), bf16)] + token_sum,
        scal,
        [q, *after(kv_all, near_m[2], far_m), w_out],
        [((tokens * n_col, 2 * width_out), bf16)],
        cost=5,
    )
    far_m.append(swap(near_m[2], "dp", 1))
    resid1, a2_own = call(
        norm2_kernel, [((own, D), f32), ((own, D), bf16)], None, [*after(finish_row(o_keep, o_send), far_m), xg_own, vec]
    )
    a2 = gather_row(a2_own)
    act, d_pre, up_sum, a_keep, a_send = call(
        functools.partial(mlp_kernel, n_row, n_col),
        [
            ((tokens, ff), bf16),
            ((tokens, ff), bf16),
            ((1, ff), f32),
            ((tokens // 2, 2 * D), f32),
            ((tokens // 2, 2 * D), bf16),
        ],
        scal,
        [*a2, *xg, up_bias[None], up_weight, down_weight, *near_m, *far_m],
        [((D, ff), bf16), ((D, ff), bf16)],
    )
    bits = bits_of("row")
    for b in bits[:-1]:
        a_keep, a_send = add_halves(a_keep, swap(a_send, "row", b))
    a_got = swap(a_send, "row", bits[-1])
    act, d_pre = after((act, d_pre), a_send)
    up_mine, up_other, down_mine, down_other = call(
        functools.partial(mlp_grad_kernel, n_row),
        [((D, half_ff), bf16)] * 4,
        None,
        [*a2, *xg, act, d_pre],
    )
    a_got = after(a_got, up_other, down_other)
    up_got = swap(up_other, "dp", 1)
    gp, d_resid1, sums2 = call(
        norm2_back_kernel,
        [((own, D), bf16), ((own, D), f32), ((4, D), f32)],
        None,
        [a_keep, a_got, xg_own, vec, resid1],
    )
    gp_all = gather_row(gp)
    d_att, out_mine, out_other = call(
        functools.partial(d_att_kernel, n_row, heads),
        [((tokens, width_out), bf16)] + [((n_col * width_out // 4, 2 * width_in), bf16)] * 2,
        scal,
        [*gp_all, attended, w_out],
        [((width_out, D), bf16)],
    )
    out_got = swap(out_other, "dp", 1)
    up_parts = join_dp([up_mine], [after(up_got, gp_all)], scal)
    down_got = swap(after(down_other, up_parts), "dp", 1)
    up_got = swap(up_parts[1], "col", 1)
    dq, dkv_keep, dkv_send = call(
        functools.partial(attention_back_kernel, order, col_order(), heads),
        [
            ((tokens, width_out), bf16),
            ((n_col // 2 * tokens, 2 * width_out), f32),
            ((n_col // 2 * tokens, 2 * width_out), bf16),
        ],
        scal,
        [q, *kv_all, after(d_att, up_parts)],
        [
            ((tokens * n_col, 2 * width_out), bf16),
            ((2 * width_out, tokens * n_col), f32),
            ((tokens * n_col, 2 * width_out), f32),
        ],
        cost=10,
    )
    dkv_got = swap(after(dkv_send, up_got), "col", 1)
    up_pair = finish_col(*add_halves(up_parts[0], after(up_got, dkv_send)), 2)
    dkv_keep, dkv_send = add_halves(dkv_keep, after(dkv_got, down_got, up_pair))
    dkv_keep, dkv_got = finish_col(dkv_keep, dkv_send, 2)
    down_parts = join_dp([down_mine, out_mine], after((down_got, out_got), dkv_send), scal)
    down_got = swap(down_parts[1], "col", 1)
    dkv_got = after(dkv_got, down_got)
    d_keep, d_send, sums1, qkv_mine, qkv_other = call(
        functools.partial(d_a1_kernel, n_row, n_col),
        [((tokens // 2, D), f32), ((tokens // 2 + 32, D), bf16), ((8, D), f32)]
        + [((D // 2, 3 * width_out), bf16)] * 2,
        scal,
        [*xg, dq, dkv_keep, dkv_got, a1, w_qkv, sums2, up_sum],
        [((D, 3 * width_out), bf16)],
    )
    qkv_got = swap(qkv_other, "dp", 1)

    down_half = add_halves(down_parts[0], after(down_got, d_send))
    up_total, up_away = share_dp(*after(up_pair, d_send))
    bits = bits_of("row")
    for b in bits[:-1]:
        half = d_keep.shape[0] // 2
        d_keep, d_send, sums1 = call(
            d_half_kernel,
            [((half, D), f32), ((half + 32, D), bf16), ((8, D), f32)],
            None,
            [d_keep, swap(d_send, "row", b), sums1],
        )
    outs, sums = call(
        final_kernel,
        [((n_col, width_in, 2 * own), bf16), ((8, D), f32)],
        None,
        [d_keep, swap(d_send, "row", bits[-1]), sums1, a_keep, a_got, xg_own, vec, resid1, d_resid1],
    )
    down_pair = finish_col(*down_half, 2)
    input_grad, block_output = call(last_kernel, [((width_in, tokens), bf16)] * 2, None, [turn(outs)])

    rows, width = D // 2, 3 * width_out
    keep, send = call(
        functools.partial(qkv_part_kernel, col_order()),
        [((rows // 2, width), f32), ((rows // 2 + 32, width), bf16)],
        scal,
        [qkv_mine, after(qkv_got, outs, down_pair), sums],
    )
    bits = bits_of("col")
    for b in bits[:-1]:
        rows //= 2
        keep, send, sums = call(
            qkv_half_kernel,
            [((rows // 2, width), f32), ((rows // 2 + 32, width), bf16), ((8, D), f32)],
            None,
            [keep, swap(send, "col", b), sums],
        )
    d_up = call(up_out_kernel, [((width_in, ff), f32)], scal, [up_total, up_away])[0]
    last = [((rows // 2 + 32, width), bf16), ((8, D), f32)]
    got = after(swap(send, "col", bits[-1]), input_grad, d_up)
    total, sums = call(qkv_add_kernel, last, None, [keep, got, sums])
    for b in bits_of("dp", 2):
        total, sums = call(qkv_add_kernel, last, None, [total, swap(total, "dp", b), sums])
    d_down, d_out = call(
        down_out_kernel,
        [((width_in, ff), f32), ((width_out * width_in // 128, 128), f32)],
        scal,
        share_dp(*after(down_pair, send)),
        [((width_out, width_in), f32), ((pl.cdiv(width_in, 128), width_out, 128), f32)],
    )
    d_qkv, *vecs = call(
        qkv_out_kernel,
        [((width * width_in // 128, 128), f32)]
        + [((1, width_in), f32)] * 6
        + [((1, ff), f32), ((2, width_out), f32)],
        scal,
        [total, after(swap(total, "dp", 1), d_down), sums],
        [((width_in, width), f32), ((pl.cdiv(width, 128), width_in, 128), f32)],
    )

    return (
        block_output.T,
        input_grad.T,
        vecs[0].reshape(-1),
        vecs[1].reshape(-1),
        d_qkv.reshape(1, 1, -1),
        vecs[7],
        d_out.reshape(1, 1, -1),
        vecs[4].reshape(-1),
        vecs[2].reshape(-1),
        vecs[3].reshape(-1),
        d_up,
        vecs[6].reshape(-1),
        d_down,
        vecs[5].reshape(-1),
    )


def solution(mesh):
    in_specs = (
        P(("dp", "row"), "col"),
        P("col"),
        P("col"),
        P("col", "row", None),
        P(None, "row"),
        P("row", "col", None),
        P("col"),
        P("col"),
        P("col"),
        P("col", "row"),
        P("row"),
        P("col", "row"),
        P("col"),
        P(("dp", "row"), "col"),
    )
    out_specs = (
        P(("dp", "row"), "col"),
        P(("dp", "row"), "col"),
        P("col"),
        P("col"),
        P("col", "row", None),
        P(None, "row"),
        P("row", "col", None),
        P("col"),
        P("col"),
        P("col"),
        P("col", "row"),
        P("row"),
        P("col", "row"),
        P("col"),
    )
    return jax.shard_map(body, mesh=mesh, in_specs=in_specs, out_specs=out_specs, check_vma=False)
```

```python
import functools
import math

import jax
import jax.numpy as jnp
from jax import lax
from jax.experimental import pallas as pl
from jax.experimental.pallas import tpu as pltpu
from jax.sharding import PartitionSpec as P

D = 768
HEAD = 64
SCALE = 1.0 / math.sqrt(HEAD)
C0 = math.sqrt(2.0 / math.pi)
C1 = 0.044715
bf16 = jnp.bfloat16
f32 = jnp.float32
VMEM = pl.BlockSpec(memory_space=pltpu.VMEM)
SMEM = pl.BlockSpec(memory_space=pltpu.SMEM)


def dot_nn(a, b):
    return lax.dot_general(a, b, (((1,), (0,)), ((), ())), preferred_element_type=f32)


def dot_nt(a, b):
    return lax.dot_general(a, b, (((1,), (1,)), ((), ())), preferred_element_type=f32)


def dot_tn(a, b):
    return lax.dot_general(a, b, (((0,), (0,)), ((), ())), preferred_element_type=f32)


def call(kernel, outs, scalars, args, scratch=(), limit=20, cost=0):
    first = [] if scalars is None else [scalars]
    return pl.pallas_call(
        kernel,
        out_shape=[jax.ShapeDtypeStruct(s, t) for s, t in outs],
        in_specs=[SMEM] * len(first) + [VMEM] * len(args),
        out_specs=[VMEM] * len(outs),
        scratch_shapes=[pltpu.VMEM(s, t) for s, t in scratch],
        compiler_params=pltpu.CompilerParams(vmem_limit_bytes=limit * 1024 * 1024),
        cost_estimate=pl.CostEstimate(flops=1, bytes_accessed=1 + 3_000_000 * cost, transcendentals=0),
    )(*first, *args)


def swap(value, axis, bit):
    n = lax.axis_size(axis)
    return lax.ppermute(value, axis, [(i, i ^ bit) for i in range(n)])


def turn(value, split=0, concat=0):
    return lax.all_to_all(value, "col", split, concat, tiled=True)


def bits_of(axis, first=1):
    n = lax.axis_size(axis)
    bits = []
    b = first
    while b < n:
        bits.append(b)
        b *= 2
    return bits


def row_order():
    order = [0]
    for b in reversed(bits_of("row")):
        order = order + [o ^ b for o in order]
    return order


def gather_row(value):
    pieces = [value]
    for b in reversed(bits_of("row")):
        pieces = pieces + [swap(p, "row", b) for p in pieces]
    return pieces


def gather_col(value, *others):
    pieces = {0: value}
    for b in reversed(bits_of("col")):
        for k in list(pieces):
            piece = after(pieces[k], *others) if k and others else pieces[k]
            pieces[k ^ b] = swap(piece, "col", b)
    return [pieces[k] for k in range(lax.axis_size("col"))]


def finish_row(keep, send):
    bits = bits_of("row")
    for b in bits[:-1]:
        keep, send = add_halves(keep, swap(send, "row", b))
    return keep, swap(send, "row", bits[-1])


def add_halves(keep, got):
    rows, width = keep.shape
    return call(halves_kernel, [((rows // 2, width), f32), ((rows // 2, width), bf16)], None, [keep, got])


def after(value, *others):
    return lax.optimization_barrier((value, others))[0]


def beside(value, chunk):
    half = chunk // 2
    starts = range(0, value.shape[0], chunk)
    first = jnp.concatenate([value[i : i + half] for i in starts], axis=0)
    second = jnp.concatenate([value[i + half : i + chunk] for i in starts], axis=0)
    return jnp.concatenate([first, second], axis=1)


def under(value, chunk):
    half = chunk // 2
    width = value.shape[1] // 2
    parts = []
    for i in range(0, value.shape[0], half):
        parts += [value[i : i + half, :width], value[i : i + half, width:]]
    return jnp.concatenate(parts, axis=0)


def place(scal, order, k, kk, chunk, n_col):
    at = ((scal[0] ^ order[kk]) * n_col + (scal[1] ^ k)) * chunk
    return pl.ds(pl.multiple_of(at, chunk), chunk)


def load_natural(scal, order, pieces, dst):
    chunk = pieces[0].shape[0] // len(order)
    for k, piece in enumerate(pieces):
        for kk in range(len(order)):
            dst[place(scal, order, k, kk, chunk, len(pieces)), :] = piece[kk * chunk : (kk + 1) * chunk, :]


def chunk_of(scal, order, quarter, chunk):
    want = quarter ^ scal[0]
    index = jnp.int32(0)
    for i, o in enumerate(order):
        index = jnp.where(want == o, i, index)
    return pl.ds(pl.multiple_of(index * chunk, chunk), chunk)


def row_exps(q, k, low, first):
    scores = dot_nt(q, k)
    tail = scores[:, low:]
    rows = lax.broadcasted_iota(jnp.int32, tail.shape, 0) + first
    cols = lax.broadcasted_iota(jnp.int32, tail.shape, 1)
    tail = jnp.where(cols <= rows, tail, -1e30)
    scores = tail if low == 0 else jnp.concatenate([scores[:, :low], tail], axis=1)
    top = jnp.max(scores, axis=-1, keepdims=True)
    e = jnp.exp2((scores - top) * (SCALE * math.log2(math.e)))
    return e, jnp.sum(e, axis=-1, keepdims=True)


def attention_kernel(order, n_col, heads, scal, q_ref, *refs):
    pieces, (w, att_out, keep, send, nat) = refs[:n_col], refs[n_col:]
    load_natural(scal, order, pieces, nat)
    n_row = len(order)
    chunk = q_ref.shape[0] // n_row
    block = chunk * n_col
    width = heads * HEAD
    first = scal[1] * chunk
    ks = [nat[:, h * HEAD : (h + 1) * HEAD] for h in range(heads)]
    vs = [nat[:, width + h * HEAD : width + (h + 1) * HEAD] for h in range(heads)]
    parts = []
    for i in range(n_row):
        upto = (i + 1) * block
        q = q_ref[chunk_of(scal, order, i, chunk), :]
        es = [row_exps(q[:, h * HEAD : (h + 1) * HEAD], ks[h][:upto], i * block, first) for h in range(heads)]
        parts.append([(dot_nn(e.astype(bf16), v[:upto]) / total).astype(bf16) for (e, total), v in zip(es, vs)])
    for i in range(n_row):
        att_out[chunk_of(scal, order, i, chunk), :] = jnp.concatenate(parts[i], axis=1)
    w_all = jnp.concatenate([w[j] for j in range(n_col)], axis=1)
    halves_out(dot_nn(att_out[...], w_all), keep, send)


def attention_back_kernel(order, col_order, heads, scal, q_ref, *refs):
    n_col = len(col_order)
    pieces, (do_ref, dq, keep, send, nat, grads_t, grads) = refs[:n_col], refs[n_col:]
    load_natural(scal, order, pieces, nat)
    n_row = len(order)
    chunk = q_ref.shape[0] // n_row
    block = chunk * n_col
    width = heads * HEAD
    first = scal[1] * chunk
    grads_t[...] = jnp.zeros_like(grads_t)
    here = [slice(h * HEAD, (h + 1) * HEAD) for h in range(heads)]
    there = [slice(width + h * HEAD, width + (h + 1) * HEAD) for h in range(heads)]
    ks = [nat[:, at] for at in here]
    vs = [nat[:, at] for at in there]
    parts = []
    for i in range(n_row):
        upto = (i + 1) * block
        at = chunk_of(scal, order, i, chunk)
        q_all, do_all = q_ref[at, :], do_ref[at, :]
        qs, dos = [q_all[:, x] for x in here], [do_all[:, x] for x in here]
        es = [row_exps(q, k[:upto], i * block, first) for q, k in zip(qs, ks)]
        dps = [dot_nt(do, v[:upto]) for do, v in zip(dos, vs)]
        ps = [e * (1.0 / total) for e, total in es]
        dss = [
            (p * (dp - jnp.sum(dp * p, axis=-1, keepdims=True))).astype(bf16) for p, dp in zip(ps, dps)
        ]
        parts.append([(dot_nn(ds, k[:upto]) * SCALE).astype(bf16) for ds, k in zip(dss, ks)])
        d_vs = [dot_tn(do, p.astype(bf16)) for do, p in zip(dos, ps)]
        d_ks = [dot_tn(q, ds) for q, ds in zip(qs, dss)]
        for h in range(heads):
            grads_t[there[h], :upto] += d_vs[h]
            grads_t[here[h], :upto] += d_ks[h]
    for i in range(n_row):
        dq[chunk_of(scal, order, i, chunk), :] = jnp.concatenate(parts[i], axis=1)
    grads[:, :width] = grads_t[:width, :].T * SCALE
    grads[:, width:] = grads_t[width:, :].T
    rows = n_row * chunk
    for i, k in enumerate(col_order):
        to, base = (keep, i) if i < n_col // 2 else (send, i - n_col // 2)
        for kk in range(n_row):
            at = base * rows + kk * chunk
            to[at : at + chunk, :] = grads[place(scal, order, k, kk, chunk, n_col), :].astype(to.dtype)


def norm_stats(v):
    mean = jnp.sum(v, axis=-1, keepdims=True) / D
    var = jnp.sum(v * v, axis=-1, keepdims=True) / D - mean * mean
    inverse = lax.rsqrt(var + 1e-05)
    return (v - mean) * inverse, inverse


def norm_back(grad, centred, inverse, gain):
    scaled = grad * gain
    first = jnp.sum(scaled, axis=-1, keepdims=True) / D
    second = jnp.sum(scaled * centred, axis=-1, keepdims=True) / D
    return inverse * (scaled - first - centred * second)


def stacked(refs, rows=slice(None)):
    return jnp.concatenate([r[rows, :] for r in refs], axis=0)


def halves_kernel(keep_ref, got_ref, keep, send):
    half = keep_ref.shape[0] // 2
    keep[...] = keep_ref[:half, :] + got_ref[:half, :].astype(f32)
    send[...] = (keep_ref[half:, :] + got_ref[half:, :].astype(f32)).astype(bf16)


def halves_out(value, keep, send, at=0):
    half, width = value.shape[0] // 2, value.shape[1]
    keep[:, at : at + width] = value[:half]
    send[:, at : at + width] = value[half:].astype(bf16)


def message_kernel(own, n_col, scal, x, g, *refs):
    vectors, outs, cut = refs[: -n_col - 1], refs[-n_col - 1 : -1], refs[-1]
    x_all = x[...].astype(f32).T.astype(bf16)
    g_all = g[...].astype(f32).T.astype(bf16)
    width = x_all.shape[1]
    rest = jnp.concatenate([v[...] for v in vectors] + [jnp.zeros((8 - len(vectors), width), f32)], axis=0)
    parts = []
    for _ in range(3):
        part = rest.astype(bf16).astype(f32)
        parts.append(part)
        rest = rest - part
    parts.append(jnp.zeros((8, width), f32))
    parts = jnp.concatenate(parts, axis=0).astype(bf16)
    parts = beside(parts, parts.shape[0])
    half = own // 2
    for j in range(n_col):
        cut[j, :half, :] = beside(x_all[j * own : (j + 1) * own], own)
        cut[j, half:own, :] = beside(g_all[j * own : (j + 1) * own], own)
    for k in range(n_col):
        outs[k][:own, :] = cut[scal[1] ^ k]
        outs[k][own:, :] = parts


def prep_kernel(scal, qkv, out, half_a):
    half, width3 = half_a.shape[0], qkv.shape[1]
    rows = pl.ds(pl.multiple_of(scal[2] * half, 32), half)
    half_a[:, :width3] = qkv[rows, :]
    half_a[:, width3:] = out[rows, :]


def prep_mlp_kernel(scal, up, down, half_m):
    tall, half_ff = up.shape[0], half_m.shape[1]
    lanes = pl.ds(pl.multiple_of(scal[2] * half_ff, 128), half_ff)
    half_m[:tall, :] = up[:, lanes]
    half_m[tall:, :] = down[:, lanes]


def token_kernel(scal, *refs):
    pieces, (xg, vec, got) = refs[:-3], refs[-3:]
    n_col, rows, width = got.shape
    width = width // 2
    for k in range(n_col):
        got[scal[1] ^ k] = pieces[k][...]
    own = xg.shape[0] // 2
    for j in range(n_col):
        at = slice(j * width, (j + 1) * width)
        xg[:, at] = under(got[j, :own, :], own)
        v = under(got[j, own:, :].astype(f32), 2 * (rows - own))
        vec[:, at] = v[:8] + v[8:16] + v[16:24]


def qkv_kernel(heads, tokens, n_row, n_col, scal, *refs):
    xgs, (vec, qv_bias, own_qkv, own_out), refs = refs[:n_row], refs[n_row : n_row + 4], refs[n_row + 4 :]
    near, far, (q_out, kv_out, a1_out, w_all, w_out) = refs[: n_col - 1], refs[n_col - 1 : 2 * n_col - 2], refs[2 * n_col - 2 :]
    c, d = scal[1], scal[2]
    rows, width3 = own_qkv.shape
    half = rows // 2
    w_all[pl.ds(pl.multiple_of(c * rows, 64), rows), :] = own_qkv[...]
    w_out[c] = own_out[...]
    for k in range(1, n_col):
        for part, ref in ((d, near[k - 1]), (1 - d, far[k - 1])):
            w_all[pl.ds(pl.multiple_of(((c ^ k) * 2 + part) * half, 32), half), :] = ref[:, :width3]
            w_out[c ^ k, pl.ds(pl.multiple_of(part * half, 32), half), :] = ref[:, width3:]
    x = stacked(xgs, slice(0, tokens // n_row))
    centred, _ = norm_stats(x.astype(f32))
    a1 = (centred * vec[0:1, :] + vec[1:2, :]).astype(bf16)
    a1_out[...] = a1
    width = heads * HEAD
    shifts = jnp.concatenate([qv_bias[0:1, :], jnp.zeros((1, width), f32), qv_bias[1:2, :]], axis=1)
    qkv = (dot_nn(a1, w_all[...]) + shifts).astype(bf16)
    q_out[...] = qkv[:, :width]
    kv_out[...] = qkv[:, width:]


def norm2_kernel(keep, got, xg, vec, resid_out, a2_out):
    own = keep.shape[0]
    resid = xg[:own, :].astype(f32) + (keep[...] + got[...].astype(f32)) + vec[4:5, :]
    resid_out[...] = resid
    centred, _ = norm_stats(resid)
    a2_out[...] = (centred * vec[2:3, :] + vec[3:4, :]).astype(bf16)


def mlp_kernel(n_row, n_col, scal, *refs):
    a2s, gs, refs = refs[:n_row], refs[n_row : 2 * n_row], refs[2 * n_row :]
    up_bias, up_own, down_own = refs[:3]
    near, far = refs[3 : 2 + n_col], refs[2 + n_col : 1 + 2 * n_col]
    act_out, d_pre_out, bias_sum, keep, send, wu, wd = refs[1 + 2 * n_col :]
    c, d = scal[1], scal[2]
    rows, width = up_own.shape
    half = width // 2
    mine = pl.ds(pl.multiple_of(d * half, 128), half)
    other = pl.ds(pl.multiple_of((1 - d) * half, 128), half)
    here = pl.ds(pl.multiple_of(c * rows, 64), rows)
    for w, own in ((wu, up_own), (wd, down_own)):
        w[here, :half] = own[:, mine]
        w[here, half:] = own[:, other]
    for k in range(1, n_col):
        there = pl.ds(pl.multiple_of((c ^ k) * rows, 64), rows)
        wu[there, :half] = near[k - 1][:rows, :]
        wd[there, :half] = near[k - 1][rows:, :]
        wu[there, half:] = far[k - 1][:rows, :]
        wd[there, half:] = far[k - 1][rows:, :]
    own = a2s[0].shape[0]
    shift = jnp.concatenate([up_bias[:, mine], up_bias[:, other]], axis=1)
    pre = dot_nn(stacked(a2s), wu[...]) + shift
    square = pre * pre
    t = jnp.tanh(C0 * (pre + C1 * (square * pre)))
    act = (0.5 * pre * (1.0 + t)).astype(bf16)
    slope = 0.5 * (1.0 + t) + (0.5 * C0) * pre * (1.0 - t * t) * (1.0 + (3.0 * C1) * square)
    d_act = dot_nn(stacked(gs, slice(own, 2 * own)), wd[...])
    d_pre = (d_act * slope).astype(bf16)
    act_out[...] = act
    d_pre_out[...] = d_pre
    total = jnp.sum(d_pre.astype(f32), axis=0, keepdims=True)
    bias_sum[:, mine] = total[:, :half]
    bias_sum[:, other] = total[:, half:]
    halves_out(dot_nt(d_pre, wu[...]), keep, send)
    halves_out(dot_nt(act, wd[...]), keep, send, D)


def mlp_grad_kernel(n_row, *refs):
    a2s, gs, refs = refs[:n_row], refs[n_row : 2 * n_row], refs[2 * n_row :]
    act, d_pre, up_mine, up_other, down_mine, down_other = refs
    half = act.shape[1] // 2
    own = a2s[0].shape[0]
    a2, g = stacked(a2s), stacked(gs, slice(own, 2 * own))
    up_mine[...] = dot_tn(a2, d_pre[:, :half]).astype(bf16)
    up_other[...] = dot_tn(a2, d_pre[:, half:]).astype(bf16)
    down_mine[...] = dot_tn(g, act[:, :half]).astype(bf16)
    down_other[...] = dot_tn(g, act[:, half:]).astype(bf16)


def norm2_back_kernel(keep, got, xg, vec, resid_ref, gp_out, d_resid_out, sums):
    own = keep.shape[0]
    d_a2 = keep[:, :D] + got[:, :D].astype(f32)
    centred, inverse = norm_stats(resid_ref[...])
    g = xg[own:, :].astype(f32)
    d_resid = g + norm_back(d_a2, centred, inverse, vec[2:3, :])
    gp = d_resid.astype(bf16)
    d_resid_out[...] = d_resid
    gp_out[...] = gp
    for i, v in enumerate((d_a2 * centred, d_a2, gp.astype(f32), g)):
        sums[i : i + 1, :] = jnp.sum(v, axis=0, keepdims=True)


def d_att_kernel(n_row, heads, scal, *refs):
    gps, (att, w, d_att_out, mine, other, full) = refs[:n_row], refs[n_row:]
    d = scal[2]
    gp = stacked(gps)
    n_col, rows, width = w.shape
    w_all = jnp.concatenate([w[j] for j in range(n_col)], axis=1)
    d_att = dot_nt(gp, w_all).astype(bf16)
    d_att_out[...] = d_att
    full[...] = dot_tn(att[...], gp).astype(bf16)
    half = rows // 2
    for to, part in ((mine, d), (other, 1 - d)):
        piece = full[pl.ds(pl.multiple_of(part * half, 32), half), :]
        for j in range(n_col):
            to[j * (half // 2) : (j + 1) * (half // 2), :] = beside(piece[:, j * width : (j + 1) * width], half)


def narrow(value):
    wide = 2 * value.shape[1] // 3
    return jnp.concatenate([value[:, :wide], beside(value[:, wide:], value.shape[0])], axis=0)


def widen(value):
    rows = 2 * value.shape[0] // 3
    return jnp.concatenate([value[:rows], under(value[rows:], rows)], axis=1)


def d_a1_kernel(n_row, n_col, scal, *refs):
    xgs, (dq, dkv_keep, dkv_got, a1, w), refs = refs[:n_row], refs[n_row : n_row + 5], refs[n_row + 5 :]
    sums2, up_sum, refs = refs[0], refs[1], refs[2:]
    keep, send, sums, mine, other, full = refs
    d = scal[2]
    tokens = a1.shape[0]
    d_kv = (dkv_keep[...] + dkv_got[...].astype(f32)).astype(bf16)
    d_qkv = jnp.concatenate([dq[...], d_kv], axis=1)
    part = dot_nt(d_qkv, w[...])
    half = tokens // 2
    keep[...] = part[:half]
    send[:half, :] = part[half:].astype(bf16)
    full[...] = dot_tn(a1[...], d_qkv).astype(bf16)
    half = full.shape[0] // (2 * n_col)
    for j in range(n_col):
        at = slice(j * 3 * half // 2, (j + 1) * 3 * half // 2)
        mine[at, :] = narrow(full[pl.ds(pl.multiple_of((2 * j + d) * half, 32), half), :])
        other[at, :] = narrow(full[pl.ds(pl.multiple_of((2 * j + 1 - d) * half, 32), half), :])
    centred, _ = norm_stats(stacked(xgs, slice(0, tokens // n_row)).astype(f32))
    pad = jnp.zeros((1, D - d_qkv.shape[1]), f32)
    total = jnp.concatenate(
        [
            jnp.sum(part * centred, axis=0, keepdims=True),
            jnp.sum(part, axis=0, keepdims=True),
            sums2[...],
            up_sum[...],
            jnp.concatenate([jnp.sum(d_qkv.astype(f32), axis=0, keepdims=True), pad], axis=1),
        ],
        axis=0,
    )
    sums[...] = total
    send[tokens // 2 :, :] = pack_wide(total)


def final_kernel(d_keep, d_got, sums_ref, a_keep, a_got, xg, vec, resid, d_resid, out, sums):
    n_col, width, rows = out.shape
    own = rows // 2
    d_a1 = d_keep[...] + d_got[:own, :].astype(f32)
    sums[...] = add_row_sums(sums_ref[...], unpack_wide(d_got[own:, :]))
    centred, inverse = norm_stats(xg[:own, :].astype(f32))
    d_x = (d_resid[...] + norm_back(d_a1, centred, inverse, vec[0:1, :])).astype(bf16)
    y = (resid[...] + (a_keep[:, D:] + a_got[:, D:].astype(f32)) + vec[5:6, :]).astype(bf16)
    both = jnp.concatenate([d_x.astype(f32), y.astype(f32)], axis=0)
    for j in range(n_col):
        out[j] = both[:, j * width : (j + 1) * width].T.astype(bf16)


def part_kernel(n_in, order, scal, *refs):
    mine, got, (keep, send) = refs[:n_in], refs[n_in : 2 * n_in], refs[2 * n_in :]
    n_col = len(order)
    height = 2 * keep.shape[0] // n_col
    for i, k in enumerate(order):
        to, at = (keep, i) if i < n_col // 2 else (send, i - n_col // 2)
        at = at * height
        for m, g in zip(mine, got):
            rows = m.shape[0] // n_col
            there = pl.ds(pl.multiple_of((scal[1] ^ k) * rows, 16), rows)
            total = m[there, :].astype(f32) + g[there, :].astype(f32)
            to[at : at + rows, :] = total.astype(to.dtype)
            at += rows


def add_kernel(*refs):
    total = refs[0][...].astype(f32)
    for r in refs[1:-1]:
        total = total + r[...].astype(f32)
    refs[-1][...] = total.astype(refs[-1].dtype)


def three_parts(v):
    parts = []
    for _ in range(3):
        part = v.astype(bf16).astype(f32)
        parts.append(part)
        v = v - part
    return parts


def pack_wide(v):
    return jnp.concatenate(three_parts(v) + [jnp.zeros_like(v)], axis=0).astype(bf16)


def unpack_wide(v):
    v = v.astype(f32)
    n = v.shape[0] // 4
    return v[:n] + v[n : 2 * n] + v[2 * n : 3 * n]


def pack_sums(v):
    half = v.shape[1] // 2
    rows = [p[:, at : at + half] for p in three_parts(v) for at in (0, half)]
    return jnp.concatenate(rows, axis=0).astype(bf16)


def unpack_sums(v):
    v = v.astype(f32)
    n = v.shape[0] // 6
    parts = [jnp.concatenate([v[i * n : (i + 1) * n], v[(i + 1) * n : (i + 2) * n]], axis=1) for i in (0, 2, 4)]
    return parts[0] + parts[1] + parts[2]


def add_row_sums(own, got):
    return jnp.concatenate([own[:6] + got[:6], own[6:]], axis=0)


def d_half_kernel(keep_ref, got_ref, sums_ref, keep, send, sums):
    rows = keep_ref.shape[0]
    half = rows // 2
    keep[...] = keep_ref[:half, :] + got_ref[:half, :].astype(f32)
    send[:half, :] = (keep_ref[half:, :] + got_ref[half:rows, :].astype(f32)).astype(bf16)
    total = add_row_sums(sums_ref[...], unpack_wide(got_ref[rows:, :]))
    sums[...] = total
    send[half:, :] = pack_wide(total)


def qkv_part_kernel(order, scal, mine, got, own_sums, keep, send):
    n_col = len(order)
    rows = mine.shape[0] // n_col
    for i, k in enumerate(order):
        to, at = (keep, i) if i < n_col // 2 else (send, i - n_col // 2)
        there = pl.ds(pl.multiple_of((scal[1] ^ k) * rows, 16), rows)
        total = mine[there, :].astype(f32) + got[there, :].astype(f32)
        to[at * rows : (at + 1) * rows, :] = total.astype(to.dtype)
    send[keep.shape[0] :, :] = pack_sums(own_sums[...])


def qkv_half_kernel(keep_ref, got_ref, sums_ref, keep, send, sums):
    rows = keep_ref.shape[0]
    half = rows // 2
    keep[...] = keep_ref[:half, :] + got_ref[:half, :].astype(f32)
    send[:half, :] = (keep_ref[half:, :] + got_ref[half:rows, :].astype(f32)).astype(bf16)
    total = sums_ref[...] + unpack_sums(got_ref[rows:, :])
    sums[...] = total
    send[half:, :] = pack_sums(total)


def qkv_add_kernel(keep_ref, got_ref, sums_ref, out, sums):
    rows = out.shape[0] - 48
    out[:rows, :] = (keep_ref[:rows, :].astype(f32) + got_ref[:rows, :].astype(f32)).astype(bf16)
    total = sums_ref[...] + unpack_sums(got_ref[rows:, :])
    sums[...] = total
    out[rows:, :] = pack_sums(total)


def flat_store(value, cut, out):
    rows, width = value.shape
    lines = 2 * width // 128
    for i in range(cut.shape[0]):
        high = min(width, (i + 1) * 128)
        cut[i, :, : high - i * 128] = value[:, i * 128 : high]
    both = []
    for odd in range(2):
        pieces = [cut[i, pl.ds(odd, rows // 2, stride=2), :] for i in range(cut.shape[0])]
        both.append(jnp.concatenate(pieces, axis=1)[:, :width])
    both = jnp.concatenate(both, axis=1)
    for g in range(lines):
        out[pl.ds(g, rows // 2, stride=lines), :] = both[:, g * 128 : (g + 1) * 128]


def up_out_kernel(scal, part, away, up):
    half = part.shape[1]
    up[:, pl.ds(pl.multiple_of(scal[2] * half, 128), half)] = part[...].astype(f32)
    up[:, pl.ds(pl.multiple_of((1 - scal[2]) * half, 128), half)] = away[...].astype(f32)


def down_out_kernel(scal, part, away, down, out, full, cut):
    d = scal[2]
    rows, width = down.shape
    half = width // 2
    for ref, index in ((part, d), (away, 1 - d)):
        down[:, pl.ds(pl.multiple_of(index * half, 128), half)] = ref[:rows, :].astype(f32)
        piece = under(ref[rows:, :].astype(f32), rows // 2)
        full[pl.ds(pl.multiple_of(index * (rows // 2), 32), rows // 2), :] = piece
    flat_store(full, cut, out)


def qkv_out_kernel(scal, part, away, sums_ref, out, *refs):
    outs, (full, cut) = refs[:-2], refs[-2:]
    rows = part.shape[0] - 48
    half = 2 * rows // 3
    full[pl.ds(pl.multiple_of(scal[2] * half, 32), half), :] = widen(part[:rows, :].astype(f32))
    full[pl.ds(pl.multiple_of((1 - scal[2]) * half, 32), half), :] = widen(away[:rows, :].astype(f32))
    flat_store(full, cut, out)
    sums = sums_ref[...] + unpack_sums(away[rows:, :])
    width = outs[0].shape[1]
    mine = sums[:, :width]
    for j in range(1, sums.shape[1] // width):
        mine = jnp.where(scal[1] == j, sums[:, j * width : (j + 1) * width], mine)
    for i in range(6):
        outs[i][...] = mine[i : i + 1, :]
    outs[6][...] = sums[6:7, :]
    width = outs[7].shape[1]
    outs[7][0:1, :] = sums[7:8, :width]
    outs[7][1:2, :] = sums[7:8, 2 * width : 3 * width]


def last_kernel(got, first, second):
    n_col, _, two = got.shape
    own = two // 2
    first[...] = jnp.concatenate([got[j, :, :own] for j in range(n_col)], axis=1)
    second[...] = jnp.concatenate([got[j, :, own:] for j in range(n_col)], axis=1)


def col_order():
    order = [0]
    for b in reversed(bits_of("col")):
        order = order + [o ^ b for o in order]
    return order


def join_dp(mine, got, scal):
    rows = sum(m.shape[0] for m in mine) // 2
    width = mine[0].shape[1]
    return call(
        functools.partial(part_kernel, len(mine), col_order()),
        [((rows, width), f32), ((rows, width), bf16)],
        scal,
        [*mine, *got],
    )


def finish_col(keep, send, first=1):
    bits = bits_of("col", first)
    for b in bits[:-1]:
        keep, send = add_halves(keep, swap(send, "col", b))
    return keep, swap(send, "col", bits[-1])


def share_dp(own, got):
    shape = own.shape
    total = call(add_kernel, [(shape, bf16)], None, [own, got])[0]
    for b in bits_of("dp", 2):
        total = call(add_kernel, [(shape, bf16)], None, [total, swap(total, "dp", b)])[0]
    return total, swap(total, "dp", 1)


def body(
    block_input,
    ln1_gain,
    ln1_bias,
    qkv_weight,
    qv_bias,
    out_weight,
    out_bias,
    ln2_gain,
    ln2_bias,
    up_weight,
    up_bias,
    down_weight,
    down_bias,
    out_grad,
):
    n_col = lax.axis_size("col")
    n_row = lax.axis_size("row")
    width_in = D // n_col
    width_out = D // n_row
    heads = width_out // HEAD
    order = row_order()
    own = block_input.shape[0] // n_col
    tokens = own * n_row
    half_ff = up_weight.shape[1] // 2
    ff = 2 * half_ff
    cols = range(1, n_col)
    c = lax.axis_index("col").astype(jnp.int32)
    d = lax.axis_index("dp").astype(jnp.int32) & 1
    scal = jnp.stack([lax.axis_index("row").astype(jnp.int32), c, d])
    token_sum = [((tokens // 2, D), f32), ((tokens // 2, D), bf16)]

    shape = (own + 16, 2 * width_in)
    message = call(
        functools.partial(message_kernel, own, n_col),
        [(shape, bf16)] * n_col,
        scal,
        [
            block_input.T,
            out_grad.T,
            *[v[None] for v in (ln1_gain, ln1_bias, ln2_gain, ln2_bias, out_bias, down_bias)],
        ],
        [((n_col, own, 2 * width_in), bf16)],
    )
    got = [message[0]] + [swap(message[k], "col", k) for k in range(1, n_col)]

    qkv_flat, out_flat = qkv_weight, out_weight
    own_qkv = qkv_flat.reshape(width_in, 3 * width_out)
    own_out = out_flat.reshape(width_out, width_in)
    half_a = call(
        prep_kernel, [((width_in // 2, 3 * width_out + width_in), bf16)], scal, [own_qkv, own_out]
    )[0]
    half_m = call(prep_mlp_kernel, [((2 * width_in, half_ff), bf16)], scal, [up_weight, down_weight])[0]
    near_a = gather_col(half_a, got)[1:]
    far_a = [swap(v, "dp", 1) for v in near_a]
    half_m = after(half_m, near_a[2], far_a[:2])
    near_m = [swap(half_m, "col", b) for b in bits_of("col")]
    far_m = [swap(v, "dp", 1) for v in near_m]

    xg_own, vec = call(
        token_kernel, [((2 * own, D), bf16), ((8, D), f32)], scal, got, [((n_col, *shape), bf16)]
    )
    xg = gather_row(xg_own)
    q, kv, a1, w_qkv, w_out = call(
        functools.partial(qkv_kernel, heads, tokens, n_row, n_col),
        [
            ((tokens, width_out), bf16),
            ((tokens, 2 * width_out), bf16),
            ((tokens, D), bf16),
            ((D, 3 * width_out), bf16),
            ((n_col, width_out, width_in), bf16),
        ],
        scal,
        [*xg, vec, qv_bias, own_qkv, own_out, *near_a, *far_a],
    )
    kv_all = gather_col(after(kv, near_m), far_m[0])
    near_m.append(swap(after(near_m[1], kv_all), "col", 1))
    attended, o_keep, o_send = call(
        functools.partial(attention_kernel, order, n_col, heads),
        [((tokens, width_out), bf16)] + token_sum,
        scal,
        [q, *after(kv_all, far_m[1]), w_out],
        [((tokens * n_col, 2 * width_out), bf16)],
        cost=5,
    )
    far_m.append(swap(near_m[2], "dp", 1))
    resid1, a2_own = call(
        norm2_kernel, [((own, D), f32), ((own, D), bf16)], None, [*after(finish_row(o_keep, o_send), far_m), xg_own, vec]
    )
    a2 = gather_row(a2_own)
    act, d_pre, up_sum, a_keep, a_send = call(
        functools.partial(mlp_kernel, n_row, n_col),
        [
            ((tokens, ff), bf16),
            ((tokens, ff), bf16),
            ((1, ff), f32),
            ((tokens // 2, 2 * D), f32),
            ((tokens // 2, 2 * D), bf16),
        ],
        scal,
        [*a2, *xg, up_bias[None], up_weight, down_weight, *near_m, *far_m],
        [((D, ff), bf16), ((D, ff), bf16)],
    )
    bits = bits_of("row")
    for b in bits[:-1]:
        a_keep, a_send = add_halves(a_keep, swap(a_send, "row", b))
    a_got = swap(a_send, "row", bits[-1])
    act, d_pre = after((act, d_pre), a_send)
    up_mine, up_other, down_mine, down_other = call(
        functools.partial(mlp_grad_kernel, n_row),
        [((D, half_ff), bf16)] * 4,
        None,
        [*a2, *xg, act, d_pre],
    )
    a_got = after(a_got, up_other, down_other)
    up_got = swap(up_other, "dp", 1)
    gp, d_resid1, sums2 = call(
        norm2_back_kernel,
        [((own, D), bf16), ((own, D), f32), ((4, D), f32)],
        None,
        [a_keep, a_got, xg_own, vec, resid1],
    )
    gp_all = gather_row(gp)
    d_att, out_mine, out_other = call(
        functools.partial(d_att_kernel, n_row, heads),
        [((tokens, width_out), bf16)] + [((n_col * width_out // 4, 2 * width_in), bf16)] * 2,
        scal,
        [*gp_all, attended, w_out],
        [((width_out, D), bf16)],
    )
    out_got = swap(out_other, "dp", 1)
    up_parts = join_dp([up_mine], [after(up_got, gp_all)], scal)
    down_got = swap(after(down_other, up_parts), "dp", 1)
    up_got = swap(up_parts[1], "col", 1)
    dq, dkv_keep, dkv_send = call(
        functools.partial(attention_back_kernel, order, col_order(), heads),
        [
            ((tokens, width_out), bf16),
            ((n_col // 2 * tokens, 2 * width_out), f32),
            ((n_col // 2 * tokens, 2 * width_out), bf16),
        ],
        scal,
        [q, *kv_all, after(d_att, up_parts)],
        [
            ((tokens * n_col, 2 * width_out), bf16),
            ((2 * width_out, tokens * n_col), f32),
            ((tokens * n_col, 2 * width_out), f32),
        ],
        cost=10,
    )
    dkv_got = swap(after(dkv_send, up_got), "col", 1)
    up_pair = finish_col(*add_halves(up_parts[0], after(up_got, dkv_send)), 2)
    dkv_keep, dkv_send = add_halves(dkv_keep, after(dkv_got, down_got, up_pair))
    dkv_keep, dkv_got = finish_col(dkv_keep, dkv_send, 2)
    down_parts = join_dp([down_mine, out_mine], after((down_got, out_got), dkv_send), scal)
    down_got = swap(down_parts[1], "col", 1)
    d_keep, d_send, sums1, qkv_mine, qkv_other = call(
        functools.partial(d_a1_kernel, n_row, n_col),
        [((tokens // 2, D), f32), ((tokens // 2 + 32, D), bf16), ((8, D), f32)]
        + [((3 * D // 4, 2 * width_out), bf16)] * 2,
        scal,
        [*xg, dq, dkv_keep, dkv_got, a1, w_qkv, sums2, up_sum],
        [((D, 3 * width_out), bf16)],
    )
    qkv_got = swap(qkv_other, "dp", 1)

    down_half = add_halves(down_parts[0], after(down_got, d_send))
    up_total, up_away = share_dp(*after(up_pair, d_send))
    bits = bits_of("row")
    for b in bits[:-1]:
        half = d_keep.shape[0] // 2
        d_keep, d_send, sums1 = call(
            d_half_kernel,
            [((half, D), f32), ((half + 32, D), bf16), ((8, D), f32)],
            None,
            [d_keep, swap(d_send, "row", b), sums1],
        )
    outs, sums = call(
        final_kernel,
        [((n_col, width_in, 2 * own), bf16), ((8, D), f32)],
        None,
        [d_keep, swap(d_send, "row", bits[-1]), sums1, a_keep, a_got, xg_own, vec, resid1, d_resid1],
    )
    down_pair = finish_col(*down_half, 2)
    input_grad, block_output = call(last_kernel, [((width_in, tokens), bf16)] * 2, None, [turn(outs)])

    rows, width = 3 * D // 4, 2 * width_out
    keep, send = call(
        functools.partial(qkv_part_kernel, col_order()),
        [((rows // 2, width), f32), ((rows // 2 + 48, width), bf16)],
        scal,
        [qkv_mine, after(qkv_got, outs, down_pair), sums],
    )
    bits = bits_of("col")
    for b in bits[:-1]:
        rows //= 2
        keep, send, sums = call(
            qkv_half_kernel,
            [((rows // 2, width), f32), ((rows // 2 + 48, width), bf16), ((8, D), f32)],
            None,
            [keep, swap(send, "col", b), sums],
        )
    d_up = call(up_out_kernel, [((width_in, ff), f32)], scal, [up_total, up_away])[0]
    last = [((rows // 2 + 48, width), bf16), ((8, D), f32)]
    got = after(swap(send, "col", bits[-1]), input_grad, d_up)
    total, sums = call(qkv_add_kernel, last, None, [keep, got, sums])
    for b in bits_of("dp", 2):
        total, sums = call(qkv_add_kernel, last, None, [total, swap(total, "dp", b), sums])
    d_down, d_out = call(
        down_out_kernel,
        [((width_in, ff), f32), ((width_out * width_in // 128, 128), f32)],
        scal,
        share_dp(*after(down_pair, send)),
        [((width_out, width_in), f32), ((pl.cdiv(width_in, 128), width_out, 128), f32)],
    )
    d_qkv, *vecs = call(
        qkv_out_kernel,
        [((3 * width_out * width_in // 128, 128), f32)]
        + [((1, width_in), f32)] * 6
        + [((1, ff), f32), ((2, width_out), f32)],
        scal,
        [total, after(swap(total, "dp", 1), d_down), sums],
        [((width_in, 3 * width_out), f32), ((pl.cdiv(3 * width_out, 128), width_in, 128), f32)],
    )

    return (
        block_output.T,
        input_grad.T,
        vecs[0].reshape(-1),
        vecs[1].reshape(-1),
        d_qkv.reshape(1, 1, -1),
        vecs[7],
        d_out.reshape(1, 1, -1),
        vecs[4].reshape(-1),
        vecs[2].reshape(-1),
        vecs[3].reshape(-1),
        d_up,
        vecs[6].reshape(-1),
        d_down,
        vecs[5].reshape(-1),
    )


def solution(mesh):
    in_specs = (
        P(("dp", "row"), "col"),
        P("col"),
        P("col"),
        P("col", "row", None),
        P(None, "row"),
        P("row", "col", None),
        P("col"),
        P("col"),
        P("col"),
        P("col", "row"),
        P("row"),
        P("col", "row"),
        P("col"),
        P(("dp", "row"), "col"),
    )
    out_specs = (
        P(("dp", "row"), "col"),
        P(("dp", "row"), "col"),
        P("col"),
        P("col"),
        P("col", "row", None),
        P(None, "row"),
        P("row", "col", None),
        P("col"),
        P("col"),
        P("col"),
        P("col", "row"),
        P("row"),
        P("col", "row"),
        P("col"),
    )
    return jax.shard_map(body, mesh=mesh, in_specs=in_specs, out_specs=out_specs, check_vma=False)
```

```python
import functools
import math

import jax
import jax.numpy as jnp
from jax import lax
from jax.experimental import pallas as pl
from jax.experimental.pallas import tpu as pltpu
from jax.sharding import PartitionSpec as P

D = 768
HEAD = 64
SCALE = 1.0 / math.sqrt(HEAD)
C0 = math.sqrt(2.0 / math.pi)
C1 = 0.044715
bf16 = jnp.bfloat16
f32 = jnp.float32
VMEM = pl.BlockSpec(memory_space=pltpu.VMEM)
SMEM = pl.BlockSpec(memory_space=pltpu.SMEM)


def dot_nn(a, b):
    return lax.dot_general(a, b, (((1,), (0,)), ((), ())), preferred_element_type=f32)


def dot_nt(a, b):
    return lax.dot_general(a, b, (((1,), (1,)), ((), ())), preferred_element_type=f32)


def dot_tn(a, b):
    return lax.dot_general(a, b, (((0,), (0,)), ((), ())), preferred_element_type=f32)


def call(kernel, outs, scalars, args, scratch=(), limit=20, cost=0):
    first = [] if scalars is None else [scalars]
    return pl.pallas_call(
        kernel,
        out_shape=[jax.ShapeDtypeStruct(s, t) for s, t in outs],
        in_specs=[SMEM] * len(first) + [VMEM] * len(args),
        out_specs=[VMEM] * len(outs),
        scratch_shapes=[pltpu.VMEM(s, t) for s, t in scratch],
        compiler_params=pltpu.CompilerParams(vmem_limit_bytes=limit * 1024 * 1024),
        cost_estimate=pl.CostEstimate(flops=1, bytes_accessed=1 + 3_000_000 * cost, transcendentals=0),
    )(*first, *args)


def swap(value, axis, bit):
    n = lax.axis_size(axis)
    return lax.ppermute(value, axis, [(i, i ^ bit) for i in range(n)])


def turn(value, split=0, concat=0):
    return lax.all_to_all(value, "col", split, concat, tiled=True)


def bits_of(axis, first=1):
    n = lax.axis_size(axis)
    bits = []
    b = first
    while b < n:
        bits.append(b)
        b *= 2
    return bits


def row_order():
    order = [0]
    for b in reversed(bits_of("row")):
        order = order + [o ^ b for o in order]
    return order


def gather_row(value):
    pieces = [value]
    for b in reversed(bits_of("row")):
        pieces = pieces + [swap(p, "row", b) for p in pieces]
    return pieces


def gather_col(value, *others):
    pieces = {0: value}
    for b in reversed(bits_of("col")):
        for k in list(pieces):
            piece = after(pieces[k], *others) if k and others else pieces[k]
            pieces[k ^ b] = swap(piece, "col", b)
    return [pieces[k] for k in range(lax.axis_size("col"))]


def finish_row(keep, send):
    bits = bits_of("row")
    for b in bits[:-1]:
        keep, send = add_halves(keep, swap(send, "row", b))
    return keep, swap(send, "row", bits[-1])


def add_halves(keep, got):
    rows, width = keep.shape
    return call(halves_kernel, [((rows // 2, width), f32), ((rows // 2, width), bf16)], None, [keep, got])


def after(value, *others):
    return lax.optimization_barrier((value, others))[0]


def beside(value, chunk):
    half = chunk // 2
    starts = range(0, value.shape[0], chunk)
    first = jnp.concatenate([value[i : i + half] for i in starts], axis=0)
    second = jnp.concatenate([value[i + half : i + chunk] for i in starts], axis=0)
    return jnp.concatenate([first, second], axis=1)


def under(value, chunk):
    half = chunk // 2
    width = value.shape[1] // 2
    parts = []
    for i in range(0, value.shape[0], half):
        parts += [value[i : i + half, :width], value[i : i + half, width:]]
    return jnp.concatenate(parts, axis=0)


def place(scal, order, k, kk, chunk, n_col):
    at = ((scal[0] ^ order[kk]) * n_col + (scal[1] ^ k)) * chunk
    return pl.ds(pl.multiple_of(at, chunk), chunk)


def load_natural(scal, order, pieces, dst):
    chunk = pieces[0].shape[0] // len(order)
    for k, piece in enumerate(pieces):
        for kk in range(len(order)):
            dst[place(scal, order, k, kk, chunk, len(pieces)), :] = piece[kk * chunk : (kk + 1) * chunk, :]


def chunk_of(scal, order, quarter, chunk):
    want = quarter ^ scal[0]
    index = jnp.int32(0)
    for i, o in enumerate(order):
        index = jnp.where(want == o, i, index)
    return pl.ds(pl.multiple_of(index * chunk, chunk), chunk)


def row_exps(q, k, low, first):
    scores = dot_nt(q, k)
    tail = scores[:, low:]
    rows = lax.broadcasted_iota(jnp.int32, tail.shape, 0) + first
    cols = lax.broadcasted_iota(jnp.int32, tail.shape, 1)
    tail = jnp.where(cols <= rows, tail, -1e30)
    scores = tail if low == 0 else jnp.concatenate([scores[:, :low], tail], axis=1)
    top = jnp.max(scores, axis=-1, keepdims=True)
    e = jnp.exp2((scores - top) * (SCALE * math.log2(math.e)))
    return e, jnp.sum(e, axis=-1, keepdims=True)


def attention_kernel(order, n_col, heads, scal, q_ref, *refs):
    pieces, (w, att_out, keep, send, nat) = refs[:n_col], refs[n_col:]
    load_natural(scal, order, pieces, nat)
    n_row = len(order)
    chunk = q_ref.shape[0] // n_row
    block = chunk * n_col
    width = heads * HEAD
    first = scal[1] * chunk
    ks = [nat[:, h * HEAD : (h + 1) * HEAD] for h in range(heads)]
    vs = [nat[:, width + h * HEAD : width + (h + 1) * HEAD] for h in range(heads)]
    parts = []
    for i in range(n_row):
        upto = (i + 1) * block
        q = q_ref[chunk_of(scal, order, i, chunk), :]
        es = [row_exps(q[:, h * HEAD : (h + 1) * HEAD], ks[h][:upto], i * block, first) for h in range(heads)]
        parts.append([(dot_nn(e.astype(bf16), v[:upto]) / total).astype(bf16) for (e, total), v in zip(es, vs)])
    for i in range(n_row):
        att_out[chunk_of(scal, order, i, chunk), :] = jnp.concatenate(parts[i], axis=1)
    w_all = jnp.concatenate([w[j] for j in range(n_col)], axis=1)
    halves_out(dot_nn(att_out[...], w_all), keep, send)


def attention_back_kernel(order, col_order, heads, scal, q_ref, *refs):
    n_col = len(col_order)
    pieces, (do_ref, dq, keep, send, nat, grads_t, grads) = refs[:n_col], refs[n_col:]
    load_natural(scal, order, pieces, nat)
    n_row = len(order)
    chunk = q_ref.shape[0] // n_row
    block = chunk * n_col
    width = heads * HEAD
    first = scal[1] * chunk
    grads_t[...] = jnp.zeros_like(grads_t)
    here = [slice(h * HEAD, (h + 1) * HEAD) for h in range(heads)]
    there = [slice(width + h * HEAD, width + (h + 1) * HEAD) for h in range(heads)]
    ks = [nat[:, at] for at in here]
    vs = [nat[:, at] for at in there]
    parts = []
    for i in range(n_row):
        upto = (i + 1) * block
        at = chunk_of(scal, order, i, chunk)
        q_all, do_all = q_ref[at, :], do_ref[at, :]
        qs, dos = [q_all[:, x] for x in here], [do_all[:, x] for x in here]
        es = [row_exps(q, k[:upto], i * block, first) for q, k in zip(qs, ks)]
        dps = [dot_nt(do, v[:upto]) for do, v in zip(dos, vs)]
        ps = [e * (1.0 / total) for e, total in es]
        dss = [
            (p * (dp - jnp.sum(dp * p, axis=-1, keepdims=True))).astype(bf16) for p, dp in zip(ps, dps)
        ]
        parts.append([(dot_nn(ds, k[:upto]) * SCALE).astype(bf16) for ds, k in zip(dss, ks)])
        d_vs = [dot_tn(do, p.astype(bf16)) for do, p in zip(dos, ps)]
        d_ks = [dot_tn(q, ds) for q, ds in zip(qs, dss)]
        for h in range(heads):
            grads_t[there[h], :upto] += d_vs[h]
            grads_t[here[h], :upto] += d_ks[h]
    for i in range(n_row):
        dq[chunk_of(scal, order, i, chunk), :] = jnp.concatenate(parts[i], axis=1)
    grads[:, :width] = grads_t[:width, :].T * SCALE
    grads[:, width:] = grads_t[width:, :].T
    rows = n_row * chunk
    for i, k in enumerate(col_order):
        to, base = (keep, i) if i < n_col // 2 else (send, i - n_col // 2)
        for kk in range(n_row):
            at = base * rows + kk * chunk
            to[at : at + chunk, :] = grads[place(scal, order, k, kk, chunk, n_col), :].astype(to.dtype)


def norm_stats(v):
    mean = jnp.sum(v, axis=-1, keepdims=True) / D
    var = jnp.sum(v * v, axis=-1, keepdims=True) / D - mean * mean
    inverse = lax.rsqrt(var + 1e-05)
    return (v - mean) * inverse, inverse


def norm_back(grad, centred, inverse, gain):
    scaled = grad * gain
    first = jnp.sum(scaled, axis=-1, keepdims=True) / D
    second = jnp.sum(scaled * centred, axis=-1, keepdims=True) / D
    return inverse * (scaled - first - centred * second)


def stacked(refs, rows=slice(None)):
    return jnp.concatenate([r[rows, :] for r in refs], axis=0)


def halves_kernel(keep_ref, got_ref, keep, send):
    half = keep_ref.shape[0] // 2
    keep[...] = keep_ref[:half, :] + got_ref[:half, :].astype(f32)
    send[...] = (keep_ref[half:, :] + got_ref[half:, :].astype(f32)).astype(bf16)


def halves_out(value, keep, send, at=0):
    half, width = value.shape[0] // 2, value.shape[1]
    keep[:, at : at + width] = value[:half]
    send[:, at : at + width] = value[half:].astype(bf16)


def message_kernel(own, n_col, scal, x, g, *refs):
    vectors, outs, cut = refs[: -n_col - 1], refs[-n_col - 1 : -1], refs[-1]
    x_all = x[...].astype(f32).T.astype(bf16)
    g_all = g[...].astype(f32).T.astype(bf16)
    width = x_all.shape[1]
    rest = jnp.concatenate([v[...] for v in vectors] + [jnp.zeros((8 - len(vectors), width), f32)], axis=0)
    parts = []
    for _ in range(3):
        part = rest.astype(bf16).astype(f32)
        parts.append(part)
        rest = rest - part
    parts.append(jnp.zeros((8, width), f32))
    parts = jnp.concatenate(parts, axis=0).astype(bf16)
    parts = beside(parts, parts.shape[0])
    half = own // 2
    for j in range(n_col):
        cut[j, :half, :] = beside(x_all[j * own : (j + 1) * own], own)
        cut[j, half:own, :] = beside(g_all[j * own : (j + 1) * own], own)
    for k in range(n_col):
        outs[k][:own, :] = cut[scal[1] ^ k]
        outs[k][own:, :] = parts


def prep_kernel(scal, qkv, out, half_a):
    half, width3 = half_a.shape[0], qkv.shape[1]
    rows = pl.ds(pl.multiple_of(scal[2] * half, 32), half)
    half_a[:, :width3] = qkv[rows, :]
    half_a[:, width3:] = out[rows, :]


def prep_mlp_kernel(scal, up, down, half_m):
    tall, half_ff = up.shape[0], half_m.shape[1]
    lanes = pl.ds(pl.multiple_of(scal[2] * half_ff, 128), half_ff)
    half_m[:tall, :] = up[:, lanes]
    half_m[tall:, :] = down[:, lanes]


def token_kernel(scal, *refs):
    pieces, (xg, vec, got) = refs[:-3], refs[-3:]
    n_col, rows, width = got.shape
    width = width // 2
    for k in range(n_col):
        got[scal[1] ^ k] = pieces[k][...]
    own = xg.shape[0] // 2
    for j in range(n_col):
        at = slice(j * width, (j + 1) * width)
        xg[:, at] = under(got[j, :own, :], own)
        v = under(got[j, own:, :].astype(f32), 2 * (rows - own))
        vec[:, at] = v[:8] + v[8:16] + v[16:24]


def qkv_kernel(heads, tokens, n_row, n_col, scal, *refs):
    xgs, (vec, qv_bias, own_qkv, own_out), refs = refs[:n_row], refs[n_row : n_row + 4], refs[n_row + 4 :]
    near, far, (q_out, kv_out, a1_out, w_all, w_out) = refs[: n_col - 1], refs[n_col - 1 : 2 * n_col - 2], refs[2 * n_col - 2 :]
    c, d = scal[1], scal[2]
    rows, width3 = own_qkv.shape
    half = rows // 2
    w_all[pl.ds(pl.multiple_of(c * rows, 64), rows), :] = own_qkv[...]
    w_out[c] = own_out[...]
    for k in range(1, n_col):
        for part, ref in ((d, near[k - 1]), (1 - d, far[k - 1])):
            w_all[pl.ds(pl.multiple_of(((c ^ k) * 2 + part) * half, 32), half), :] = ref[:, :width3]
            w_out[c ^ k, pl.ds(pl.multiple_of(part * half, 32), half), :] = ref[:, width3:]
    x = stacked(xgs, slice(0, tokens // n_row))
    centred, _ = norm_stats(x.astype(f32))
    a1 = (centred * vec[0:1, :] + vec[1:2, :]).astype(bf16)
    a1_out[...] = a1
    width = heads * HEAD
    shifts = jnp.concatenate([qv_bias[0:1, :], jnp.zeros((1, width), f32), qv_bias[1:2, :]], axis=1)
    qkv = (dot_nn(a1, w_all[...]) + shifts).astype(bf16)
    q_out[...] = qkv[:, :width]
    kv_out[...] = qkv[:, width:]


def norm2_kernel(keep, got, xg, vec, resid_out, a2_out):
    own = keep.shape[0]
    resid = xg[:own, :].astype(f32) + (keep[...] + got[...].astype(f32)) + vec[4:5, :]
    resid_out[...] = resid
    centred, _ = norm_stats(resid)
    a2_out[...] = (centred * vec[2:3, :] + vec[3:4, :]).astype(bf16)


def mlp_kernel(n_row, n_col, scal, *refs):
    a2s, gs, refs = refs[:n_row], refs[n_row : 2 * n_row], refs[2 * n_row :]
    up_bias, up_own, down_own = refs[:3]
    near, far = refs[3 : 2 + n_col], refs[2 + n_col : 1 + 2 * n_col]
    act_out, d_pre_out, bias_sum, keep, send, wu, wd = refs[1 + 2 * n_col :]
    c, d = scal[1], scal[2]
    rows, width = up_own.shape
    half = width // 2
    mine = pl.ds(pl.multiple_of(d * half, 128), half)
    other = pl.ds(pl.multiple_of((1 - d) * half, 128), half)
    here = pl.ds(pl.multiple_of(c * rows, 64), rows)
    for w, own in ((wu, up_own), (wd, down_own)):
        w[here, :half] = own[:, mine]
        w[here, half:] = own[:, other]
    for k in range(1, n_col):
        there = pl.ds(pl.multiple_of((c ^ k) * rows, 64), rows)
        wu[there, :half] = near[k - 1][:rows, :]
        wd[there, :half] = near[k - 1][rows:, :]
        wu[there, half:] = far[k - 1][:rows, :]
        wd[there, half:] = far[k - 1][rows:, :]
    own = a2s[0].shape[0]
    shift = jnp.concatenate([up_bias[:, mine], up_bias[:, other]], axis=1)
    pre = dot_nn(stacked(a2s), wu[...]) + shift
    square = pre * pre
    t = jnp.tanh(C0 * (pre + C1 * (square * pre)))
    act = (0.5 * pre * (1.0 + t)).astype(bf16)
    slope = 0.5 * (1.0 + t) + (0.5 * C0) * pre * (1.0 - t * t) * (1.0 + (3.0 * C1) * square)
    d_act = dot_nn(stacked(gs, slice(own, 2 * own)), wd[...])
    d_pre = (d_act * slope).astype(bf16)
    act_out[...] = act
    d_pre_out[...] = d_pre
    total = jnp.sum(d_pre.astype(f32), axis=0, keepdims=True)
    bias_sum[:, mine] = total[:, :half]
    bias_sum[:, other] = total[:, half:]
    halves_out(dot_nt(d_pre, wu[...]), keep, send)
    halves_out(dot_nt(act, wd[...]), keep, send, D)


def mlp_grad_kernel(n_row, *refs):
    a2s, gs, refs = refs[:n_row], refs[n_row : 2 * n_row], refs[2 * n_row :]
    act, d_pre, up_mine, up_other, down_mine, down_other = refs
    half = act.shape[1] // 2
    own = a2s[0].shape[0]
    a2, g = stacked(a2s), stacked(gs, slice(own, 2 * own))
    up_mine[...] = dot_tn(a2, d_pre[:, :half]).astype(bf16)
    up_other[...] = dot_tn(a2, d_pre[:, half:]).astype(bf16)
    down_mine[...] = dot_tn(g, act[:, :half]).astype(bf16)
    down_other[...] = dot_tn(g, act[:, half:]).astype(bf16)


def norm2_back_kernel(keep, got, xg, vec, resid_ref, gp_out, d_resid_out, sums):
    own = keep.shape[0]
    d_a2 = keep[:, :D] + got[:, :D].astype(f32)
    centred, inverse = norm_stats(resid_ref[...])
    g = xg[own:, :].astype(f32)
    d_resid = g + norm_back(d_a2, centred, inverse, vec[2:3, :])
    gp = d_resid.astype(bf16)
    d_resid_out[...] = d_resid
    gp_out[...] = gp
    for i, v in enumerate((d_a2 * centred, d_a2, gp.astype(f32), g)):
        sums[i : i + 1, :] = jnp.sum(v, axis=0, keepdims=True)


def d_att_kernel(n_row, heads, scal, *refs):
    gps, (att, w, d_att_out, mine, other, full) = refs[:n_row], refs[n_row:]
    d = scal[2]
    gp = stacked(gps)
    n_col, rows, width = w.shape
    w_all = jnp.concatenate([w[j] for j in range(n_col)], axis=1)
    d_att = dot_nt(gp, w_all).astype(bf16)
    d_att_out[...] = d_att
    full[...] = dot_tn(att[...], gp).astype(bf16)
    half = rows // 2
    for to, part in ((mine, d), (other, 1 - d)):
        piece = full[pl.ds(pl.multiple_of(part * half, 32), half), :]
        for j in range(n_col):
            to[j * (half // 2) : (j + 1) * (half // 2), :] = beside(piece[:, j * width : (j + 1) * width], half)


def narrow(value):
    wide = 2 * value.shape[1] // 3
    return jnp.concatenate([value[:, :wide], beside(value[:, wide:], value.shape[0])], axis=0)


def widen(value):
    rows = 2 * value.shape[0] // 3
    return jnp.concatenate([value[:rows], under(value[rows:], rows)], axis=1)


def d_a1_kernel(n_row, n_col, scal, *refs):
    xgs, (dq, dkv_keep, dkv_got, a1, w), refs = refs[:n_row], refs[n_row : n_row + 5], refs[n_row + 5 :]
    sums2, up_sum, refs = refs[0], refs[1], refs[2:]
    keep, send, sums, mine, other, full = refs
    d = scal[2]
    tokens = a1.shape[0]
    d_kv = (dkv_keep[...] + dkv_got[...].astype(f32)).astype(bf16)
    d_qkv = jnp.concatenate([dq[...], d_kv], axis=1)
    part = dot_nt(d_qkv, w[...])
    half = tokens // 2
    keep[...] = part[:half]
    send[:half, :] = part[half:].astype(bf16)
    full[...] = dot_tn(a1[...], d_qkv).astype(bf16)
    half = full.shape[0] // (2 * n_col)
    for j in range(n_col):
        at = slice(j * 3 * half // 2, (j + 1) * 3 * half // 2)
        mine[at, :] = narrow(full[pl.ds(pl.multiple_of((2 * j + d) * half, 32), half), :])
        other[at, :] = narrow(full[pl.ds(pl.multiple_of((2 * j + 1 - d) * half, 32), half), :])
    centred, _ = norm_stats(stacked(xgs, slice(0, tokens // n_row)).astype(f32))
    pad = jnp.zeros((1, D - d_qkv.shape[1]), f32)
    total = jnp.concatenate(
        [
            jnp.sum(part * centred, axis=0, keepdims=True),
            jnp.sum(part, axis=0, keepdims=True),
            sums2[...],
            up_sum[...],
            jnp.concatenate([jnp.sum(d_qkv.astype(f32), axis=0, keepdims=True), pad], axis=1),
        ],
        axis=0,
    )
    sums[...] = total
    send[tokens // 2 :, :] = pack_wide(total)


def final_kernel(d_keep, d_got, sums_ref, a_keep, a_got, xg, vec, resid, d_resid, out, sums):
    n_col, width, rows = out.shape
    own = rows // 2
    d_a1 = d_keep[...] + d_got[:own, :].astype(f32)
    sums[...] = add_row_sums(sums_ref[...], unpack_wide(d_got[own:, :]))
    centred, inverse = norm_stats(xg[:own, :].astype(f32))
    d_x = (d_resid[...] + norm_back(d_a1, centred, inverse, vec[0:1, :])).astype(bf16)
    y = (resid[...] + (a_keep[:, D:] + a_got[:, D:].astype(f32)) + vec[5:6, :]).astype(bf16)
    both = jnp.concatenate([d_x.astype(f32), y.astype(f32)], axis=0)
    for j in range(n_col):
        out[j] = both[:, j * width : (j + 1) * width].T.astype(bf16)


def part_kernel(n_in, order, scal, *refs):
    mine, got, (keep, send) = refs[:n_in], refs[n_in : 2 * n_in], refs[2 * n_in :]
    n_col = len(order)
    height = 2 * keep.shape[0] // n_col
    for i, k in enumerate(order):
        to, at = (keep, i) if i < n_col // 2 else (send, i - n_col // 2)
        at = at * height
        for m, g in zip(mine, got):
            rows = m.shape[0] // n_col
            there = pl.ds(pl.multiple_of((scal[1] ^ k) * rows, 16), rows)
            total = m[there, :].astype(f32) + g[there, :].astype(f32)
            to[at : at + rows, :] = total.astype(to.dtype)
            at += rows


def add_kernel(*refs):
    total = refs[0][...].astype(f32)
    for r in refs[1:-1]:
        total = total + r[...].astype(f32)
    refs[-1][...] = total.astype(refs[-1].dtype)


def three_parts(v):
    parts = []
    for _ in range(3):
        part = v.astype(bf16).astype(f32)
        parts.append(part)
        v = v - part
    return parts


def pack_wide(v):
    return jnp.concatenate(three_parts(v) + [jnp.zeros_like(v)], axis=0).astype(bf16)


def unpack_wide(v):
    v = v.astype(f32)
    n = v.shape[0] // 4
    return v[:n] + v[n : 2 * n] + v[2 * n : 3 * n]


def pack_sums(v):
    half = v.shape[1] // 2
    rows = [p[:, at : at + half] for p in three_parts(v) for at in (0, half)]
    return jnp.concatenate(rows, axis=0).astype(bf16)


def unpack_sums(v):
    v = v.astype(f32)
    n = v.shape[0] // 6
    parts = [jnp.concatenate([v[i * n : (i + 1) * n], v[(i + 1) * n : (i + 2) * n]], axis=1) for i in (0, 2, 4)]
    return parts[0] + parts[1] + parts[2]


def add_row_sums(own, got):
    return jnp.concatenate([own[:6] + got[:6], own[6:]], axis=0)


def d_half_kernel(keep_ref, got_ref, sums_ref, keep, send, sums):
    rows = keep_ref.shape[0]
    half = rows // 2
    keep[...] = keep_ref[:half, :] + got_ref[:half, :].astype(f32)
    send[:half, :] = (keep_ref[half:, :] + got_ref[half:rows, :].astype(f32)).astype(bf16)
    total = add_row_sums(sums_ref[...], unpack_wide(got_ref[rows:, :]))
    sums[...] = total
    send[half:, :] = pack_wide(total)


def qkv_part_kernel(order, scal, mine, got, own_sums, keep, send):
    n_col = len(order)
    rows = mine.shape[0] // n_col
    for i, k in enumerate(order):
        to, at = (keep, i) if i < n_col // 2 else (send, i - n_col // 2)
        there = pl.ds(pl.multiple_of((scal[1] ^ k) * rows, 16), rows)
        total = mine[there, :].astype(f32) + got[there, :].astype(f32)
        to[at * rows : (at + 1) * rows, :] = total.astype(to.dtype)
    send[keep.shape[0] :, :] = pack_sums(own_sums[...])


def qkv_half_kernel(keep_ref, got_ref, sums_ref, keep, send, sums):
    rows = keep_ref.shape[0]
    half = rows // 2
    keep[...] = keep_ref[:half, :] + got_ref[:half, :].astype(f32)
    send[:half, :] = (keep_ref[half:, :] + got_ref[half:rows, :].astype(f32)).astype(bf16)
    total = sums_ref[...] + unpack_sums(got_ref[rows:, :])
    sums[...] = total
    send[half:, :] = pack_sums(total)


def qkv_add_kernel(keep_ref, got_ref, sums_ref, out, sums):
    rows = out.shape[0] - 48
    out[:rows, :] = (keep_ref[:rows, :].astype(f32) + got_ref[:rows, :].astype(f32)).astype(bf16)
    total = sums_ref[...] + unpack_sums(got_ref[rows:, :])
    sums[...] = total
    out[rows:, :] = pack_sums(total)


def flat_store(value, cut, flat, out):
    rows, width = value.shape
    lines = 2 * width // 128
    for i in range(cut.shape[0]):
        high = min(width, (i + 1) * 128)
        cut[i, :rows, : high - i * 128] = value[:, i * 128 : high]
    both = []
    for odd in range(2):
        pieces = [cut[i, pl.ds(odd, rows // 2, stride=2), :] for i in range(cut.shape[0])]
        both.append(jnp.concatenate(pieces, axis=1)[:, :width])
    both = jnp.concatenate(both, axis=1)
    for g in range(lines):
        flat[pl.ds(g, rows // 2, stride=lines), :] = both[:, g * 128 : (g + 1) * 128]
    out[...] = flat[: out.shape[0], :]


def up_out_kernel(scal, part, away, up):
    half = part.shape[1]
    up[:, pl.ds(pl.multiple_of(scal[2] * half, 128), half)] = part[...].astype(f32)
    up[:, pl.ds(pl.multiple_of((1 - scal[2]) * half, 128), half)] = away[...].astype(f32)


def down_out_kernel(scal, part, away, down, out, full, cut, flat):
    d = scal[2]
    rows, width = down.shape
    half = width // 2
    for ref, index in ((part, d), (away, 1 - d)):
        down[:, pl.ds(pl.multiple_of(index * half, 128), half)] = ref[:rows, :].astype(f32)
        piece = under(ref[rows:, :].astype(f32), rows // 2)
        full[pl.ds(pl.multiple_of(index * (rows // 2), 32), rows // 2), :] = piece
    flat_store(full, cut, flat, out)


def qkv_out_kernel(scal, part, away, sums_ref, out, *refs):
    outs, (full, cut, flat) = refs[:-3], refs[-3:]
    rows = part.shape[0] - 48
    half = 2 * rows // 3
    full[pl.ds(pl.multiple_of(scal[2] * half, 32), half), :] = widen(part[:rows, :].astype(f32))
    full[pl.ds(pl.multiple_of((1 - scal[2]) * half, 32), half), :] = widen(away[:rows, :].astype(f32))
    flat_store(full, cut, flat, out)
    sums = sums_ref[...] + unpack_sums(away[rows:, :])
    width = outs[0].shape[1]
    mine = sums[:, :width]
    for j in range(1, sums.shape[1] // width):
        mine = jnp.where(scal[1] == j, sums[:, j * width : (j + 1) * width], mine)
    for i in range(6):
        outs[i][...] = mine[i : i + 1, :]
    outs[6][...] = sums[6:7, :]
    width = outs[7].shape[1]
    outs[7][0:1, :] = sums[7:8, :width]
    outs[7][1:2, :] = sums[7:8, 2 * width : 3 * width]


def last_kernel(got, first, second):
    n_col, _, two = got.shape
    own = two // 2
    first[...] = jnp.concatenate([got[j, :, :own] for j in range(n_col)], axis=1)
    second[...] = jnp.concatenate([got[j, :, own:] for j in range(n_col)], axis=1)


def col_order():
    order = [0]
    for b in reversed(bits_of("col")):
        order = order + [o ^ b for o in order]
    return order


def join_dp(mine, got, scal):
    rows = sum(m.shape[0] for m in mine) // 2
    width = mine[0].shape[1]
    return call(
        functools.partial(part_kernel, len(mine), col_order()),
        [((rows, width), f32), ((rows, width), bf16)],
        scal,
        [*mine, *got],
    )


def finish_col(keep, send, first=1):
    bits = bits_of("col", first)
    for b in bits[:-1]:
        keep, send = add_halves(keep, swap(send, "col", b))
    return keep, swap(send, "col", bits[-1])


def share_dp(own, got):
    shape = own.shape
    total = call(add_kernel, [(shape, bf16)], None, [own, got])[0]
    for b in bits_of("dp", 2):
        total = call(add_kernel, [(shape, bf16)], None, [total, swap(total, "dp", b)])[0]
    return total, swap(total, "dp", 1)


def body(
    block_input,
    ln1_gain,
    ln1_bias,
    qkv_weight,
    qv_bias,
    out_weight,
    out_bias,
    ln2_gain,
    ln2_bias,
    up_weight,
    up_bias,
    down_weight,
    down_bias,
    out_grad,
):
    n_col = lax.axis_size("col")
    n_row = lax.axis_size("row")
    width_in = D // n_col
    width_out = D // n_row
    heads = width_out // HEAD
    order = row_order()
    own = block_input.shape[0] // n_col
    tokens = own * n_row
    half_ff = up_weight.shape[1] // 2
    ff = 2 * half_ff
    cols = range(1, n_col)
    c = lax.axis_index("col").astype(jnp.int32)
    d = lax.axis_index("dp").astype(jnp.int32) & 1
    scal = jnp.stack([lax.axis_index("row").astype(jnp.int32), c, d])
    token_sum = [((tokens // 2, D), f32), ((tokens // 2, D), bf16)]

    shape = (own + 16, 2 * width_in)
    message = call(
        functools.partial(message_kernel, own, n_col),
        [(shape, bf16)] * n_col,
        scal,
        [
            block_input.T,
            out_grad.T,
            *[v[None] for v in (ln1_gain, ln1_bias, ln2_gain, ln2_bias, out_bias, down_bias)],
        ],
        [((n_col, own, 2 * width_in), bf16)],
    )
    got = [message[0]] + [swap(message[k], "col", k) for k in range(1, n_col)]

    qkv_flat, out_flat = qkv_weight, out_weight
    own_qkv = qkv_flat.reshape(width_in, 3 * width_out)
    own_out = out_flat.reshape(width_out, width_in)
    half_a = call(
        prep_kernel, [((width_in // 2, 3 * width_out + width_in), bf16)], scal, [own_qkv, own_out]
    )[0]
    half_m = call(prep_mlp_kernel, [((2 * width_in, half_ff), bf16)], scal, [up_weight, down_weight])[0]
    near_a = gather_col(half_a, got)[1:]
    far_a = [swap(v, "dp", 1) for v in near_a]
    half_m = after(half_m, near_a[2], far_a[:2])
    near_m = [swap(half_m, "col", b) for b in bits_of("col")]
    far_m = [swap(v, "dp", 1) for v in near_m]

    xg_own, vec = call(
        token_kernel, [((2 * own, D), bf16), ((8, D), f32)], scal, got, [((n_col, *shape), bf16)]
    )
    xg = gather_row(xg_own)
    q, kv, a1, w_qkv, w_out = call(
        functools.partial(qkv_kernel, heads, tokens, n_row, n_col),
        [
            ((tokens, width_out), bf16),
            ((tokens, 2 * width_out), bf16),
            ((tokens, D), bf16),
            ((D, 3 * width_out), bf16),
            ((n_col, width_out, width_in), bf16),
        ],
        scal,
        [*xg, vec, qv_bias, own_qkv, own_out, *near_a, *far_a],
    )
    kv_all = gather_col(after(kv, near_m), far_m[0])
    near_m.append(swap(after(near_m[1], kv_all), "col", 1))
    attended, o_keep, o_send = call(
        functools.partial(attention_kernel, order, n_col, heads),
        [((tokens, width_out), bf16)] + token_sum,
        scal,
        [q, *after(kv_all, far_m[1]), w_out],
        [((tokens * n_col, 2 * width_out), bf16)],
        cost=5,
    )
    far_m.append(swap(near_m[2], "dp", 1))
    resid1, a2_own = call(
        norm2_kernel, [((own, D), f32), ((own, D), bf16)], None, [*after(finish_row(o_keep, o_send), far_m), xg_own, vec]
    )
    a2 = gather_row(a2_own)
    act, d_pre, up_sum, a_keep, a_send = call(
        functools.partial(mlp_kernel, n_row, n_col),
        [
            ((tokens, ff), bf16),
            ((tokens, ff), bf16),
            ((1, ff), f32),
            ((tokens // 2, 2 * D), f32),
            ((tokens // 2, 2 * D), bf16),
        ],
        scal,
        [*a2, *xg, up_bias[None], up_weight, down_weight, *near_m, *far_m],
        [((D, ff), bf16), ((D, ff), bf16)],
    )
    bits = bits_of("row")
    for b in bits[:-1]:
        a_keep, a_send = add_halves(a_keep, swap(a_send, "row", b))
    a_got = swap(a_send, "row", bits[-1])
    act, d_pre = after((act, d_pre), a_send)
    up_mine, up_other, down_mine, down_other = call(
        functools.partial(mlp_grad_kernel, n_row),
        [((D, half_ff), bf16)] * 4,
        None,
        [*a2, *xg, act, d_pre],
    )
    a_got = after(a_got, up_other, down_other)
    up_got = swap(up_other, "dp", 1)
    gp, d_resid1, sums2 = call(
        norm2_back_kernel,
        [((own, D), bf16), ((own, D), f32), ((4, D), f32)],
        None,
        [a_keep, a_got, xg_own, vec, resid1],
    )
    gp_all = gather_row(gp)
    d_att, out_mine, out_other = call(
        functools.partial(d_att_kernel, n_row, heads),
        [((tokens, width_out), bf16)] + [((n_col * width_out // 4, 2 * width_in), bf16)] * 2,
        scal,
        [*gp_all, attended, w_out],
        [((width_out, D), bf16)],
    )
    out_got = swap(out_other, "dp", 1)
    up_parts = join_dp([up_mine], [after(up_got, gp_all)], scal)
    down_got = swap(after(down_other, up_parts), "dp", 1)
    up_got = swap(up_parts[1], "col", 1)
    dq, dkv_keep, dkv_send = call(
        functools.partial(attention_back_kernel, order, col_order(), heads),
        [
            ((tokens, width_out), bf16),
            ((n_col // 2 * tokens, 2 * width_out), f32),
            ((n_col // 2 * tokens, 2 * width_out), bf16),
        ],
        scal,
        [q, *kv_all, after(d_att, up_parts)],
        [
            ((tokens * n_col, 2 * width_out), bf16),
            ((2 * width_out, tokens * n_col), f32),
            ((tokens * n_col, 2 * width_out), f32),
        ],
        cost=10,
    )
    dkv_got = swap(after(dkv_send, up_got), "col", 1)
    up_pair = finish_col(*add_halves(up_parts[0], after(up_got, dkv_send)), 2)
    dkv_keep, dkv_send = add_halves(dkv_keep, after(dkv_got, down_got, up_pair))
    dkv_keep, dkv_got = finish_col(dkv_keep, dkv_send, 2)
    down_parts = join_dp([down_mine, out_mine], after((down_got, out_got), dkv_send), scal)
    down_got = swap(down_parts[1], "col", 1)
    d_keep, d_send, sums1, qkv_mine, qkv_other = call(
        functools.partial(d_a1_kernel, n_row, n_col),
        [((tokens // 2, D), f32), ((tokens // 2 + 32, D), bf16), ((8, D), f32)]
        + [((3 * D // 4, 2 * width_out), bf16)] * 2,
        scal,
        [*xg, dq, dkv_keep, dkv_got, a1, w_qkv, sums2, up_sum],
        [((D, 3 * width_out), bf16)],
    )
    qkv_got = swap(qkv_other, "dp", 1)

    down_half = add_halves(down_parts[0], after(down_got, d_send))
    up_total, up_away = share_dp(*after(up_pair, d_send))
    bits = bits_of("row")
    for b in bits[:-1]:
        half = d_keep.shape[0] // 2
        d_keep, d_send, sums1 = call(
            d_half_kernel,
            [((half, D), f32), ((half + 32, D), bf16), ((8, D), f32)],
            None,
            [d_keep, swap(d_send, "row", b), sums1],
        )
    outs, sums = call(
        final_kernel,
        [((n_col, width_in, 2 * own), bf16), ((8, D), f32)],
        None,
        [d_keep, swap(d_send, "row", bits[-1]), sums1, a_keep, a_got, xg_own, vec, resid1, d_resid1],
    )
    down_pair = finish_col(*down_half, 2)
    input_grad, block_output = call(last_kernel, [((width_in, tokens), bf16)] * 2, None, [turn(outs)])

    rows, width = 3 * D // 4, 2 * width_out
    keep, send = call(
        functools.partial(qkv_part_kernel, col_order()),
        [((rows // 2, width), f32), ((rows // 2 + 48, width), bf16)],
        scal,
        [qkv_mine, after(qkv_got, outs, down_pair), sums],
    )
    bits = bits_of("col")
    for b in bits[:-1]:
        rows //= 2
        keep, send, sums = call(
            qkv_half_kernel,
            [((rows // 2, width), f32), ((rows // 2 + 48, width), bf16), ((8, D), f32)],
            None,
            [keep, swap(send, "col", b), sums],
        )
    d_up = call(up_out_kernel, [((width_in, ff), f32)], scal, [up_total, up_away])[0]
    last = [((rows // 2 + 48, width), bf16), ((8, D), f32)]
    got = after(swap(send, "col", bits[-1]), input_grad, d_up)
    total, sums = call(qkv_add_kernel, last, None, [keep, got, sums])
    for b in bits_of("dp", 2):
        total, sums = call(qkv_add_kernel, last, None, [total, swap(total, "dp", b), sums])
    d_down, d_out = call(
        down_out_kernel,
        [((width_in, ff), f32), ((width_out * width_in // 128, 128), f32)],
        scal,
        share_dp(*after(down_pair, send)),
        [((width_out, width_in), f32), ((pl.cdiv(width_in, 128), width_out + 8, 128), f32), ((width_out * width_in // 128 + 8, 128), f32)],
    )
    d_qkv, *vecs = call(
        qkv_out_kernel,
        [((3 * width_out * width_in // 128, 128), f32)]
        + [((1, width_in), f32)] * 6
        + [((1, ff), f32), ((2, width_out), f32)],
        scal,
        [total, after(swap(total, "dp", 1), d_down), sums],
        [((width_in, 3 * width_out), f32), ((pl.cdiv(3 * width_out, 128), width_in + 8, 128), f32), ((3 * width_out * width_in // 128 + 16, 128), f32)],
    )

    return (
        block_output.T,
        input_grad.T,
        vecs[0].reshape(-1),
        vecs[1].reshape(-1),
        d_qkv.reshape(1, 1, -1),
        vecs[7],
        d_out.reshape(1, 1, -1),
        vecs[4].reshape(-1),
        vecs[2].reshape(-1),
        vecs[3].reshape(-1),
        d_up,
        vecs[6].reshape(-1),
        d_down,
        vecs[5].reshape(-1),
    )


def solution(mesh):
    in_specs = (
        P(("dp", "row"), "col"),
        P("col"),
        P("col"),
        P("col", "row", None),
        P(None, "row"),
        P("row", "col", None),
        P("col"),
        P("col"),
        P("col"),
        P("col", "row"),
        P("row"),
        P("col", "row"),
        P("col"),
        P(("dp", "row"), "col"),
    )
    out_specs = (
        P(("dp", "row"), "col"),
        P(("dp", "row"), "col"),
        P("col"),
        P("col"),
        P("col", "row", None),
        P(None, "row"),
        P("row", "col", None),
        P("col"),
        P("col"),
        P("col"),
        P("col", "row"),
        P("row"),
        P("col", "row"),
        P("col"),
    )
    return jax.shard_map(body, mesh=mesh, in_specs=in_specs, out_specs=out_specs, check_vma=False)
```
